512 devices in a mesh: lat: 16 (over z, core), lon: 32 (over x, y).
Axes of the slice: x: 4, y: 8, z: 8, core: 2. Of those that a mesh axis runs over, the one named last changes fastest.
Arguments:
- rhs: float32 [2, 16, 32, 2048], P(None, 'lat', 'lon'), may hold values from -45 to 45
- cond: float32 [16, 32, 2048], P('lat', 'lon'), may hold values from 0.2 to 5
- blk_diag: float32 [16, 32, 16, 128, 128], P('lat', 'lon'), may hold values from -0.3 to 8, as said below
- blk_off: float32 [16, 32, 15, 128, 128], P('lat', 'lon'), may hold values from -0.3 to 0.3
- iface_idx: int32 [16, 32, 4, 256], P('lat', 'lon'), may hold values from 0 to 2047
- iface_cnt: int32 [16, 32, 4], P('lat', 'lon'), may hold values from 32 to 256, as said below
- iface_coup: float32 [16, 32, 4, 256], P('lat', 'lon'), may hold values from -4 to 4
- edge_nodes: int32 [16, 32, 2, 2048], P('lat', 'lon'), may hold values from 0 to 1279, as said below
Outputs:
- solution: float32 [2, 16, 32, 2048], P(None, 'lat', 'lon')
- residual: float32 [2, 16, 32, 2048], P(None, 'lat', 'lon')
- res_history: float32 [2], replicated
The draws below stay inside these ranges and needn't reach their ends.
Inputs may be any that keep to these rules, and one draw needn't show every extreme that they name: `blk_diag`: symmetric within each block, diagonal entries 4 to 8, off-diagonal entries of magnitude at most 0.3. `iface_cnt`: some partition has 256 live slots in every direction. `edge_nodes`: heads are always nodes of the partition itself; a tail differs from its edge's head and never names a partition beyond the first or last latitude sector; every node of every partition is the head of some edge.
All inputs are finite; a program needn't handle non-finite values.
Results may differ from the reference program's by a relative error of at most 0.0033.
Values sent between devices are 32-bit elements; how exact they have to be, the bound alone decides.
No kernel may reach another device: no remote copies, remote signals or barrier semaphores. Data moves between devices by JAX's collectives and lax.ppermute only.
A program may use at most 64 MiB of HBM per device.

```python
import math
import jax
import jax.numpy as jnp
from jax import lax

EB = 16
BS = 128
ITERS = 2
E = 2048
ND = 256
IFC = 256
SLAT = 16
SLON = 32
NODES = 131072


def draw_rhs(key, part):
    key = jax.random.fold_in(key, 11)
    first, second = jax.random.split(key)
    shape = (2, SLAT, SLON, E)
    base = jnp.clip(jax.random.normal(first, shape, jnp.float32), -5.0, 5.0)
    spread = jnp.exp(jnp.log(10.0) * jax.random.uniform(second, shape, jnp.float32))
    lat_frac = jnp.arange(SLAT, dtype=jnp.float32)[None, :, None, None] / max(SLAT - 1, 1)
    factor = jnp.exp(jnp.log(3.0) * lat_frac)
    return jnp.clip(0.3 * base * spread * factor, -45.0, 45.0)


def draw_blk_diag(key, part):
    key = jax.random.fold_in(key, 12)
    first, second = jax.random.split(key)
    shape = (SLAT, SLON, EB, BS, BS)
    noise = jnp.clip(0.08 * jax.random.normal(first, shape, jnp.float32), -0.3, 0.3)
    sym = 0.5 * (noise + jnp.swapaxes(noise, -1, -2))
    eye = (lax.broadcasted_iota(jnp.int32, (BS, BS), 0) == lax.broadcasted_iota(jnp.int32, (BS, BS), 1)).astype(jnp.float32)
    dominant = jax.random.uniform(second, shape[:-1], jnp.float32, 4.0, 8.0)
    return sym * (1.0 - eye) + dominant[..., :, None] * eye


def draw_iface_cnt(key, part):
    key = jax.random.fold_in(key, 13)
    first, second = jax.random.split(key)
    base = jax.random.randint(first, (SLAT, SLON, 4), IFC // 8, IFC + 1)
    chosen = jax.random.randint(second, (), 0, SLAT * SLON)
    flat = jnp.arange(SLAT * SLON, dtype=jnp.int32).reshape(SLAT, SLON)
    return jnp.where((flat == chosen)[:, :, None], IFC, base).astype(jnp.int32)


def draw_edge_nodes(key, part):
    key = jax.random.fold_in(key, 14)
    first, second, third, fourth = jax.random.split(key, 4)
    scores = jax.random.randint(first, (SLAT, SLON, E), 0, 2 ** 20) * E + jnp.arange(E, dtype=jnp.int32)
    order = jnp.argsort(scores, axis=-1, stable=True).astype(jnp.int32)
    heads = order % ND
    pick = jax.random.randint(second, (SLAT, SLON, E), 0, 8)
    span = jnp.where(pick < 4, 0, pick - 3)
    lat_pos = jnp.arange(SLAT, dtype=jnp.int32)[:, None, None]
    span = jnp.where((span == 1) & (lat_pos == 0), 0, span)
    span = jnp.where((span == 2) & (lat_pos == SLAT - 1), 0, span)
    own_tail = (heads + 1 + jax.random.randint(third, (SLAT, SLON, E), 0, ND - 1)) % ND
    other_tail = jax.random.randint(fourth, (SLAT, SLON, E), 0, ND)
    tails = jnp.where(span == 0, own_tail, span * ND + other_tail)
    return jnp.stack([tails, heads], 2).astype(jnp.int32)


def place_ends(values, rng, smallest, largest):
    longest = values.shape.index(max(values.shape))
    spots = []
    for shift in (0, 1):
        where = [jax.random.randint(jax.random.fold_in(rng, axis), (), 0, length) for axis, length in enumerate(values.shape)]
        where[longest] = (where[longest] + shift) % values.shape[longest]
        spots.append(tuple(where))
    return values.at[spots[0]].set(smallest).at[spots[1]].set(largest)


def block_scale(rng, extent, cuts, least, largest):
    level = 1.0
    for axis_at, blocks in cuts:
        heights = jax.random.uniform(jax.random.fold_in(jax.random.fold_in(rng, 6), axis_at), (blocks,), jnp.float32, least / len(cuts), largest / len(cuts))
        level = level * jnp.repeat(jnp.exp(heights), extent[axis_at] // blocks).reshape((-1,) + (1,) * (len(extent) - 1 - axis_at))
    return level


def centred(rng, shape, scale, limit, pieces=(), kind=jnp.bfloat16):
    entries = jax.random.normal(rng, shape, jnp.float32) * scale
    if len(pieces) > 0:
        entries = block_scale(rng, shape, pieces, -0.22, 0.18) * entries
    return jnp.clip(entries, min=-limit, max=limit).astype(kind)


def setup_inputs(seed: int = 0) -> dict:
    splits = jax.random.split(jax.random.key(seed), 9)
    return {
        "rhs": draw_rhs(jax.random.fold_in(splits[8], 71), 0),
        "cond": jnp.clip(jnp.exp(math.log(5.0) - 3.218876 * jax.random.uniform(splits[1], (SLAT, SLON, E), jnp.float32) ** block_scale(splits[1], (SLAT, SLON, E), ((0, 16), (1, 32)), -0.2, 0.2)), 0.2, 5.0),
        "blk_diag": draw_blk_diag(jax.random.fold_in(splits[8], 71), 0),
        "blk_off": centred(splits[3], (SLAT, SLON, EB - 1, BS, BS), 0.06, 0.3, ((0, 16), (1, 32)), jnp.float32),
        "iface_idx": place_ends(jax.random.randint(splits[4], (SLAT, SLON, 4, IFC), 0, E), jax.random.fold_in(splits[4], 1), 0, E - 1).astype(jnp.int32),
        "iface_cnt": draw_iface_cnt(jax.random.fold_in(splits[8], 71), 0),
        "iface_coup": centred(splits[6], (SLAT, SLON, 4, IFC), 1.0, 4.0, ((0, 16), (1, 32)), jnp.float32),
        "edge_nodes": draw_edge_nodes(jax.random.fold_in(splits[8], 71), 0),
    }


OMEGA = 0.8
HIGH = lax.Precision.HIGHEST


def complex_times(left, right):
    return jnp.stack([left[0] * right[0] - left[1] * right[1], left[0] * right[1] + left[1] * right[0]])


def complex_inverse(value):
    scale = value[0] * value[0] + value[1] * value[1]
    return jnp.stack([value[0] / scale, -value[1] / scale])


def local_apply(field, blk_diag, blk_off, cond):
    width = blk_diag.shape[-1]
    blocks = field.shape[1] // width
    shaped = field.reshape(2, blocks, width)
    result = jnp.einsum("bij,cbj->cbi", blk_diag, shaped, precision=HIGH)
    upper = jnp.einsum("bij,cbj->cbi", blk_off, shaped[:, 1:], precision=HIGH)
    lower = jnp.einsum("bji,cbj->cbi", blk_off, shaped[:, :-1], precision=HIGH)
    result = result + jnp.pad(upper, ((0, 0), (0, 1), (0, 0))) + jnp.pad(lower, ((0, 0), (1, 0), (0, 0)))
    result = result.reshape(2, -1)
    return jnp.stack([result[0] - cond * field[1], result[1] + cond * field[0]])


def reference(rhs, cond, blk_diag, blk_off, iface_idx, iface_cnt, iface_coup, edge_nodes):
    slots = lax.broadcasted_iota(jnp.int32, iface_coup.shape, 3)
    coefs = jnp.where(slots < iface_cnt[..., None], iface_coup, 0.0)

    def operator(field):
        local = jax.vmap(jax.vmap(local_apply))(field, blk_diag, blk_off, cond)
        sent = jax.vmap(jax.vmap(lambda f, i: f[:, i]))(field, iface_idx)
        zero = jnp.zeros_like(sent[:1, :, :, 0])
        from_n = jnp.concatenate([zero, sent[:-1, :, :, 1]], 0)
        from_s = jnp.concatenate([sent[1:, :, :, 0], zero], 0)
        from_w = jnp.roll(sent[:, :, :, 3], 1, axis=1)
        from_e = jnp.roll(sent[:, :, :, 2], -1, axis=1)
        arrived = jnp.stack([from_n, from_s, from_w, from_e], 3)
        terms = arrived * coefs[:, :, None]

        def place(f, i, t):
            return jnp.zeros_like(f).at[:, i.reshape(-1)].add(t.reshape(2, -1))

        return local + jax.vmap(jax.vmap(place))(field, iface_idx, terms)

    lat_pos = jnp.arange(SLAT, dtype=jnp.int32)[:, None, None]
    lon_pos = jnp.arange(SLON, dtype=jnp.int32)[None, :, None]

    def global_ids(ext_ids):
        span = ext_ids // ND
        local_id = ext_ids % ND
        dlat = jnp.where(span == 1, -1, jnp.where(span == 2, 1, 0)).astype(jnp.int32)
        dlon = jnp.where(span == 3, -1, jnp.where(span == 4, 1, 0)).astype(jnp.int32)
        owner = (lat_pos + dlat) * SLON + ((lon_pos + dlon) % SLON)
        return (owner * ND + local_id).reshape(-1).astype(jnp.int32)

    tails = global_ids(edge_nodes[:, :, 0])
    heads = global_ids(edge_nodes[:, :, 1])

    def flatten(values):
        return jnp.moveaxis(values, 2, 0).reshape(2, -1)

    def unflatten(values):
        return jnp.moveaxis(values.reshape(2, SLAT, SLON, E), 0, 2)

    edge_diag = jnp.diagonal(blk_diag, axis1=3, axis2=4).reshape(SLAT, SLON, E)
    edge_value = jnp.stack([edge_diag, cond], 2)
    edge_inv = jax.vmap(jax.vmap(complex_inverse))(edge_value)
    flat_value = flatten(edge_value)
    node_diag = jnp.zeros((2, NODES), jnp.float32).at[:, heads].add(flat_value).at[:, tails].add(flat_value)
    node_inv = complex_inverse(node_diag)

    def device_times(left, right):
        return jnp.stack([left[:, :, 0] * right[:, :, 0] - left[:, :, 1] * right[:, :, 1], left[:, :, 0] * right[:, :, 1] + left[:, :, 1] * right[:, :, 0]], 2)

    def precondition(res):
        first = OMEGA * device_times(edge_inv, res)
        second = first + OMEGA * device_times(edge_inv, res - operator(first))
        remain = flatten(res - operator(second))
        nodal = jnp.zeros((2, NODES), jnp.float32).at[:, heads].add(remain).at[:, tails].add(-remain)
        correction = complex_times(node_inv, nodal)
        return second + unflatten(correction[:, heads] - correction[:, tails])

    right = jnp.moveaxis(rhs, 0, 2)
    solution = jnp.zeros_like(right)
    residual = right
    start = jnp.sum(right * right)
    history = []
    for step in range(ITERS):
        direction = precondition(residual)
        image = operator(direction)
        c_re = jnp.sum(image[:, :, 0] * residual[:, :, 0] + image[:, :, 1] * residual[:, :, 1])
        c_im = jnp.sum(image[:, :, 0] * residual[:, :, 1] - image[:, :, 1] * residual[:, :, 0])
        ww = jnp.sum(image * image)
        alpha = jnp.stack([c_re / ww, c_im / ww])
        solution = solution + jnp.stack([alpha[0] * direction[:, :, 0] - alpha[1] * direction[:, :, 1], alpha[0] * direction[:, :, 1] + alpha[1] * direction[:, :, 0]], 2)
        residual = residual - jnp.stack([alpha[0] * image[:, :, 0] - alpha[1] * image[:, :, 1], alpha[0] * image[:, :, 1] + alpha[1] * image[:, :, 0]], 2)
        history.append(jnp.sum(residual * residual) / start)
    return jnp.moveaxis(solution, 2, 0), jnp.moveaxis(residual, 2, 0), jnp.stack(history)
```

```python
import jax
import jax.numpy as jnp
from jax import lax
from jax.experimental import pallas as pl
from jax.experimental.pallas import tpu as pltpu
from jax.sharding import PartitionSpec as P

ITERS = 2
EB = 16
BS = 128
E = EB * BS
ND = 256
IFC = 256
OMEGA = 0.8
F32 = jnp.float32
BF16 = jnp.bfloat16
LIMIT = 20 * 1024 * 1024
NT = (((1,), (1,)), ((), ()))


def complex_times(a, b):
    return a[0] * b[0] - a[1] * b[1], a[0] * b[1] + a[1] * b[0]


def complex_inverse(a):
    scale = a[0] * a[0] + a[1] * a[1]
    return a[0] / scale, -a[1] / scale


def pieces(x):
    first = x.astype(BF16).astype(F32)
    rest = x - first
    second = rest.astype(BF16).astype(F32)
    return first, second, rest - second


def lanes(x, count):
    return jnp.concatenate([x[k : k + 1] for k in range(count)], axis=1)


def to_blocks(row, ref):
    for k in range(EB):
        ref[k : k + 1] = row[:, k * BS : (k + 1) * BS]
    return ref[...]


def block_mask(blocks, rows):
    return lax.broadcasted_iota(jnp.int32, (rows, blocks.shape[1]), 0) == blocks


def lane_onehot(index):
    spot = lax.broadcasted_iota(jnp.int32, (BS, index.shape[1]), 0)
    return jnp.where(spot == index % BS, 1.0, 0.0).astype(BF16)


def take(field, onehot, mask):
    parts = [pieces(part) for part in field]
    stack = jnp.concatenate([parts[c][p] for p in range(3) for c in range(2)], axis=0)
    got = jnp.dot(stack.astype(BF16), onehot[...], preferred_element_type=F32)
    got = got[:32] + got[32:64] + got[64:]
    return [
        jnp.sum(jnp.where(mask, got[16 * c : 16 * c + 16], 0.0), axis=0, keepdims=True)
        for c in range(2)
    ]


def put(rows, onehot, mask):
    parts = [pieces(part) for part in rows]
    stack = jnp.concatenate(
        [jnp.where(mask, parts[c][p], 0.0) for p in range(3) for c in range(2)], axis=0
    )
    got = lax.dot_general(stack.astype(BF16), onehot[...], NT, preferred_element_type=F32)
    got = got[:32] + got[32:64] + got[64:]
    return got[:16], got[16:]


def put_heads(rows, onehot, block):
    spot = lax.broadcasted_iota(jnp.int32, (8, block.shape[1]), 0)
    right = [pieces(part) for part in rows]
    match = (spot % 2 == block) & (spot < 4)
    stack = jnp.concatenate(
        [
            jnp.where(match, jnp.where(spot < 2, right[0][p], right[1][p]), 0.0)
            for p in range(3)
        ],
        axis=0,
    )
    got = lax.dot_general(stack.astype(BF16), onehot[...], NT, preferred_element_type=F32)
    return got[:8] + got[8:16] + got[16:]


def take_heads(own, onehot, block):
    stack = jnp.concatenate(pieces(own), axis=0)
    got = jnp.dot(stack.astype(BF16), onehot[...], preferred_element_type=F32)
    got = got[:8] + got[8:16] + got[16:]
    low = block == 0
    return [jnp.where(low, got[2 * c : 2 * c + 1], got[2 * c + 1 : 2 * c + 2]) for c in range(2)]


def parities():
    return lax.axis_index("lat") % 2 == 0, lax.axis_index("lon") % 2 == 0


def hand_out(refs, towards, at=0):
    even_lat, even_lon = parities()
    refs[0][at : at + 4] = jnp.where(even_lat, towards[1], towards[0])
    refs[1][at : at + 4] = jnp.where(even_lat, towards[0], towards[1])
    refs[2][at : at + 4] = jnp.where(even_lon, towards[3], towards[2])
    refs[3][at : at + 4] = jnp.where(even_lon, towards[2], towards[3])


def collect(refs, at=0):
    even_lat, even_lon = parities()
    core, far, near, wide = [ref[at : at + 4] for ref in refs]
    return (
        jnp.where(even_lat, far, core),
        jnp.where(even_lat, core, far),
        jnp.where(even_lon, wide, near),
        jnp.where(even_lon, near, wide),
    )


def index_rows(idx_ref):
    idx = idx_ref[0, 0]
    return jnp.concatenate([idx[d : d + 1] for d in range(4)], axis=1)


def interface_messages(field, onehot, index):
    got = take(field, onehot, block_mask(index // BS, EB))
    return [
        jnp.concatenate(
            [
                got[c][:, d * IFC + h * BS : d * IFC + (h + 1) * BS]
                for c in range(2)
                for h in range(2)
            ],
            axis=0,
        )
        for d in range(4)
    ]


def interface_sum(arrived, coefs, onehot, index):
    rows = [
        jnp.concatenate(
            [arrived[d][2 * c + h : 2 * c + h + 1] for d in range(4) for h in range(2)], axis=1
        )
        * coefs
        for c in range(2)
    ]
    return put(rows, onehot, block_mask(index // BS, EB))


def pair(ref):
    return ref[0:EB], ref[EB : 2 * EB]


def keep(ref, value):
    ref[0:EB] = value[0]
    ref[EB : 2 * EB] = value[1]


def nodal(rows, onehot_head, onehot_tail, nodes_ref, sign, out_refs, own_ref, at):
    tails = nodes_ref[0, 0, 0:1]
    heads = nodes_ref[0, 0, 1:2]
    own = put_heads(rows, onehot_head, heads // BS)
    ext = put(rows, onehot_tail, block_mask(tails // BS, EB))
    ext = [sign * ext[0], sign * ext[1]]
    own_ref[...] = own
    for c in range(2):
        own_ref[2 * c : 2 * c + 2] += ext[c][0:2]
    towards = [
        jnp.concatenate([ext[0][2 * d : 2 * d + 2], ext[1][2 * d : 2 * d + 2]], axis=0)
        for d in range(1, 5)
    ]
    hand_out(out_refs, towards, at)


def begin_kernel(
    rhs_ref, cond_ref, diag_ref, idx_ref, cnt_ref, coup_ref, nodes_ref,
    m0, m1, m2, m3, ohi_ref, oht_ref, ohh_ref, coef_ref, value_ref, scale_ref, right_ref, first_ref, own_ref,
    blocks,
):
    messages = (m0, m1, m2, m3)
    index = index_rows(idx_ref)
    ohi_ref[...] = lane_onehot(index)
    oht_ref[...] = lane_onehot(nodes_ref[0, 0, 0:1])
    ohh_ref[...] = lane_onehot(nodes_ref[0, 0, 1:2])
    slot = lax.broadcasted_iota(jnp.int32, (1, IFC), 1)
    coef_ref[...] = jnp.concatenate(
        [jnp.where(slot < cnt_ref[0, 0, d], coup_ref[0, 0, d : d + 1], 0.0) for d in range(4)], axis=1
    )
    eye = lax.broadcasted_iota(jnp.int32, (BS, BS), 0) == lax.broadcasted_iota(jnp.int32, (BS, BS), 1)
    for b in range(EB):
        value_ref[b : b + 1] = jnp.sum(jnp.where(eye, diag_ref[0, 0, b], 0.0), axis=0, keepdims=True)
    value_ref[EB : 2 * EB] = to_blocks(cond_ref[0], blocks)
    value = pair(value_ref)
    inverse = complex_inverse(value)
    scale = (OMEGA * inverse[0], OMEGA * inverse[1])
    keep(scale_ref, scale)
    for c in range(2):
        right_ref[EB * c : EB * c + EB] = to_blocks(rhs_ref[c, 0], blocks)
    first = complex_times(scale, pair(right_ref))
    keep(first_ref, first)
    hand_out(messages, interface_messages(first, ohi_ref, index), 0)
    rows = [lanes(value[c], EB) for c in range(2)]
    nodal(rows, ohh_ref, oht_ref, nodes_ref, 1.0, messages, own_ref, 4)


def weight_kernel(diag_ref, off_ref, w_ref):
    eye = lax.broadcasted_iota(jnp.int32, (BS, BS), 0) == lax.broadcasted_iota(jnp.int32, (BS, BS), 1)

    def store(b, at, block):
        high = block.astype(BF16)
        w_ref[b, at : at + BS, 0:BS] = high
        w_ref[b, at : at + BS, BS:] = (block - high.astype(F32)).astype(BF16)

    zero = jnp.zeros((BS, 2 * BS), BF16)
    w_ref[0, 0:BS] = zero
    w_ref[EB - 1, 2 * BS :] = zero
    for b in range(EB):
        store(b, BS, jnp.where(eye, 0.0, diag_ref[0, 0, b]))
        if b < EB - 1:
            off = off_ref[0, 0, b]
            store(b + 1, 0, off)
            store(b, 2 * BS, off.T)


def stiffness(field, value, w_ref, wide, out):
    wide[0:8] = jnp.zeros((8, BS), F32)
    wide[8 * (EB + 1) :] = jnp.zeros((8, BS), F32)
    for c in range(2):
        for p, piece in enumerate(pieces(field[c])):
            wide[pl.ds(8 + 2 * p + c, EB, stride=8)] = piece
    for k in (6, 7):
        wide[pl.ds(8 + k, EB, stride=8)] = jnp.zeros((EB, BS), F32)
    for b in range(EB):
        around = jnp.concatenate([wide[8 * (b + k) : 8 * (b + k) + 8] for k in range(3)], axis=1)
        got = jnp.dot(around.astype(BF16), w_ref[b], preferred_element_type=F32)
        out[8 * b : 8 * b + 8] = got[:, :BS] + got[:, BS:]
    sums = [
        out[pl.ds(c, EB, stride=8)] + out[pl.ds(2 + c, EB, stride=8)] + out[pl.ds(4 + c, EB, stride=8)]
        for c in range(2)
    ]
    turned = complex_times(value, field)
    return sums[0] + turned[0], sums[1] + turned[1]


def local_kernel(field_ref, value_ref, w_ref, out_ref, wide, out):
    keep(out_ref, stiffness(pair(field_ref), pair(value_ref), w_ref, wide, out))


def smooth(arrived, ohi_ref, coef_ref, idx_ref, first_ref, local_ref, scale_ref, right_ref, m, second_ref):
    index = index_rows(idx_ref)
    extra = interface_sum(arrived, coef_ref[...], ohi_ref, index)
    first, local, right = pair(first_ref), pair(local_ref), pair(right_ref)
    change = complex_times(pair(scale_ref), [right[c] - local[c] - extra[c] for c in range(2)])
    second = (first[0] + change[0], first[1] + change[1])
    keep(second_ref, second)
    hand_out(m, interface_messages(second, ohi_ref, index))


def smooth_first_kernel(
    a0, a1, a2, a3, own_ref, ohi_ref, coef_ref, idx_ref, first_ref, local_ref, scale_ref, right_ref,
    m0, m1, m2, m3, second_ref, ninv_ref,
):
    arrived = collect((a0, a1, a2, a3))
    smooth(arrived, ohi_ref, coef_ref, idx_ref, first_ref, local_ref, scale_ref, right_ref, (m0, m1, m2, m3), second_ref)
    sums = own_ref[0:4]
    for part in collect((a0, a1, a2, a3), 4):
        sums = sums + part
    inverse = complex_inverse((sums[0:2], sums[2:4]))
    ninv_ref[0:2] = inverse[0]
    ninv_ref[2:4] = inverse[1]


def smooth_kernel(
    a0, a1, a2, a3, ohi_ref, coef_ref, idx_ref, first_ref, local_ref, scale_ref, right_ref,
    m0, m1, m2, m3, second_ref,
):
    arrived = collect((a0, a1, a2, a3))
    smooth(arrived, ohi_ref, coef_ref, idx_ref, first_ref, local_ref, scale_ref, right_ref, (m0, m1, m2, m3), second_ref)


def restrict_kernel(
    a0, a1, a2, a3, ohi_ref, oht_ref, ohh_ref, coef_ref, idx_ref, nodes_ref, local_ref, right_ref,
    m0, m1, m2, m3, own_ref,
):
    index = index_rows(idx_ref)
    extra = interface_sum(collect((a0, a1, a2, a3)), coef_ref[...], ohi_ref, index)
    local, right = pair(local_ref), pair(right_ref)
    rows = [lanes(right[c] - local[c] - extra[c], EB) for c in range(2)]
    nodal(rows, ohh_ref, oht_ref, nodes_ref, -1.0, (m0, m1, m2, m3), own_ref, 0)


def node_kernel(a0, a1, a2, a3, own_ref, ninv_ref, y_ref):
    sums = own_ref[0:4]
    for part in collect((a0, a1, a2, a3)):
        sums = sums + part
    result = complex_times((ninv_ref[0:2], ninv_ref[2:4]), (sums[0:2], sums[2:4]))
    y_ref[0:2] = result[0]
    y_ref[2:4] = result[1]


def prolong_kernel(
    a0, a1, a2, a3, y_ref, ohi_ref, oht_ref, ohh_ref, idx_ref, nodes_ref, second_ref,
    m0, m1, m2, m3, direction_ref,
    blocks, wide,
):
    tails = nodes_ref[0, 0, 0:1]
    heads = nodes_ref[0, 0, 1:2]
    wide[...] = jnp.zeros((2 * EB, BS), F32)
    nodes = (y_ref[...],) + collect((a0, a1, a2, a3))
    for d in range(5):
        for c in range(2):
            wide[EB * c + 2 * d : EB * c + 2 * d + 2] = nodes[d][2 * c : 2 * c + 2]
    low = take(pair(wide), oht_ref, block_mask(tails // BS, EB))
    own = jnp.concatenate([nodes[0], nodes[0]], axis=0)
    high = take_heads(own, ohh_ref, heads // BS)
    second = pair(second_ref)
    direction = [second[c] + to_blocks(high[c] - low[c], blocks) for c in range(2)]
    keep(direction_ref, direction)
    hand_out((m0, m1, m2, m3), interface_messages(direction, ohi_ref, index_rows(idx_ref)))


def image_kernel(
    a0, a1, a2, a3, ohi_ref, coef_ref, idx_ref, local_ref, scale_ref,
    m0, m1, m2, m3, image_ref, first_ref,
):
    index = index_rows(idx_ref)
    extra = interface_sum(collect((a0, a1, a2, a3)), coef_ref[...], ohi_ref, index)
    local = pair(local_ref)
    image = (local[0] + extra[0], local[1] + extra[1])
    keep(image_ref, image)
    first = complex_times(pair(scale_ref), image)
    keep(first_ref, first)
    hand_out((m0, m1, m2, m3), interface_messages(first, ohi_ref, index))


def total(x):
    return jnp.sum(jnp.sum(x, axis=0, keepdims=True), axis=1, keepdims=True)


def inner(a, b):
    return total(a[0] * b[0] + a[1] * b[1]), total(a[0] * b[1] - a[1] * b[0])


def sums_kernel(
    a0, a1, a2, a3, ohi_ref, coef_ref, idx_ref, local_ref, right_ref, image_ref,
    image2_ref, sums_ref,
):
    index = index_rows(idx_ref)
    extra = interface_sum(collect((a0, a1, a2, a3)), coef_ref[...], ohi_ref, index)
    local, right, image = pair(local_ref), pair(right_ref), pair(image_ref)
    image2 = (local[0] + extra[0], local[1] + extra[1])
    keep(image2_ref, image2)
    rest = (right[0] - image[0], right[1] - image[1])
    turn = (image[0] - image2[0], image[1] - image2[1])
    found = [inner(right, right)[0], inner(image, image)[0], inner(rest, rest)[0], inner(turn, turn)[0]]
    found += [*inner(image, rest), *inner(turn, rest), *inner(turn, image)]
    lane = lax.broadcasted_iota(jnp.int32, (1, BS), 1)
    row = jnp.zeros((1, BS), F32)
    for k, value in enumerate(found):
        row = jnp.where(lane == k, value, row)
    sums_ref[...] = jnp.broadcast_to(row[None], sums_ref.shape)


def finish_kernel(
    sums_ref, right_ref, image_ref, image2_ref, direction_ref, direction2_ref,
    solution_ref, residual_ref, history_ref,
):
    row = jnp.sum(sums_ref[...], axis=0)
    lane = lax.broadcasted_iota(jnp.int32, (1, BS), 1)
    found = [jnp.sum(jnp.where(lane == k, row, 0.0), axis=1, keepdims=True) for k in range(10)]
    start, ww, rr, tt = found[:4]
    wr, tr, tw = found[4:6], found[6:8], found[8:10]
    extra = (wr[0] / ww, wr[1] / ww)
    alpha = (1.0 + extra[0], extra[1])
    fresh = rr - (wr[0] * extra[0] + wr[1] * extra[1])
    moved = complex_times(extra, tw)
    c2 = complex_times((alpha[0], -alpha[1]), (tr[0] - moved[0], tr[1] - moved[1]))
    cross = complex_times(complex_times((extra[0], -extra[1]), alpha), (tw[0], -tw[1]))
    ww2 = (alpha[0] * alpha[0] + alpha[1] * alpha[1]) * tt
    ww2 = ww2 + (extra[0] * extra[0] + extra[1] * extra[1]) * ww - 2.0 * cross[0]
    alpha2 = (c2[0] / ww2, c2[1] / ww2)
    fresh2 = fresh - (c2[0] * alpha2[0] + c2[1] * alpha2[1])
    history_ref[...] = jnp.where(lane == 0, fresh / start, fresh2 / start)
    right, image, image2 = pair(right_ref), pair(image_ref), pair(image2_ref)
    direction, direction2 = pair(direction_ref), pair(direction2_ref)
    step = complex_times(alpha, direction)
    other = complex_times(alpha, direction2)
    step2 = complex_times(alpha2, (direction[0] - other[0], direction[1] - other[1]))
    away = complex_times(extra, image)
    other = complex_times(alpha, image2)
    away2 = complex_times(alpha2, (image[0] - other[0], image[1] - other[1]))
    for c in range(2):
        solution_ref[c, 0] = lanes(step[c] + step2[c], EB)
        residual_ref[c, 0] = lanes(right[c] - image[c] - away[c] - away2[c], EB)


def shape(*dims, dtype=F32):
    return jax.ShapeDtypeStruct(dims, dtype)


FIELD = shape(2 * EB, BS)
MESSAGES = [shape(4, BS)] * 4


def call(body, outs, args, name, scratch=(), smem=(), flops=0):
    specs = [pl.BlockSpec(memory_space=pltpu.SMEM if k in smem else pltpu.VMEM) for k in range(len(args))]
    moved = sum(a.size * a.dtype.itemsize for a in args)
    return pl.pallas_call(
        body,
        out_shape=outs,
        in_specs=specs,
        out_specs=[pl.BlockSpec(memory_space=pltpu.VMEM)] * len(outs),
        scratch_shapes=scratch,
        compiler_params=pltpu.CompilerParams(vmem_limit_bytes=LIMIT),
        cost_estimate=pl.CostEstimate(flops=flops, bytes_accessed=moved, transcendentals=0),
        name=name,
    )(*args)


def swap(pairs):
    return [(a, b) for a, b in pairs] + [(b, a) for a, b in pairs]


def exchange(messages):
    lat, lon = lax.axis_size("lat"), lax.axis_size("lon")
    core = swap([(k, k + 1) for k in range(0, lat, 2)])
    far = swap([(k, k + 1) for k in range(1, lat - 1, 2)])
    near = swap([(k, k + 1) for k in range(0, lon, 2)])
    wide = swap([(k, (k + 1) % lon) for k in range(1, lon, 2)])
    return [
        lax.ppermute(messages[0], "lat", core),
        lax.ppermute(messages[1], "lat", far),
        lax.ppermute(messages[2], "lon", near),
        lax.ppermute(messages[3], "lon", wide),
    ]


def everywhere(row, axis):
    return lax.all_to_all(row, axis, 0, 0)


def on_device(rhs, cond, blk_diag, blk_off, idx, cnt, coup, nodes):
    blocks = pltpu.VMEM((EB, BS), F32)
    wide = pltpu.VMEM((8 * (EB + 2), BS), F32)
    out = pltpu.VMEM((8 * EB, BS), F32)
    *sent, ohi, oht, ohh, coef, value, scale, right, first, own = call(
        begin_kernel,
        [shape(8, BS)] * 4
        + [shape(BS, 4 * IFC, dtype=BF16), shape(BS, E, dtype=BF16), shape(BS, E, dtype=BF16), shape(1, 4 * IFC)]
        + [FIELD] * 4
        + [shape(8, BS)],
        (rhs, cond, blk_diag, idx, cnt, coup, nodes),
        "begin",
        scratch=[blocks],
        smem=(4,),
    )
    arrived = exchange(sent)
    (weights,) = call(
        weight_kernel, [shape(EB, 3 * BS, 2 * BS, dtype=BF16)], (blk_diag, blk_off), "weights", flops=10**7
    )

    def local(field):
        return call(
            local_kernel, [FIELD], (field, value, weights), "local", scratch=[wide, out], flops=2 * 8 * EB * 3 * BS * 2 * BS
        )[0]

    images, directions = [], []
    for step in range(ITERS):
        stiff = local(first)
        if step == 0:
            *sent, second, ninv = call(
                smooth_first_kernel,
                MESSAGES + [FIELD, shape(4, BS)],
                (*arrived, own, ohi, coef, idx, first, stiff, scale, right),
                "smooth_first",
            )
            source = right
        else:
            *sent, second = call(
                smooth_kernel,
                MESSAGES + [FIELD],
                (*arrived, ohi, coef, idx, first, stiff, scale, source),
                "smooth",
            )
        arrived = exchange(sent)
        stiff = local(second)
        *sent, own = call(
            restrict_kernel,
            MESSAGES + [shape(8, BS)],
            (*arrived, ohi, oht, ohh, coef, idx, nodes, stiff, source),
            "restrict",
        )
        arrived = exchange(sent)
        (y,) = call(node_kernel, [shape(4, BS)], (*arrived, own, ninv), "node")
        arrived = exchange([y] * 4)
        *sent, direction = call(
            prolong_kernel,
            MESSAGES + [FIELD],
            (*arrived, y, ohi, oht, ohh, idx, nodes, second),
            "prolong",
            scratch=[blocks, pltpu.VMEM((2 * EB, BS), F32)],
        )
        directions.append(direction)
        arrived = exchange(sent)
        stiff = local(direction)
        if step == 0:
            *sent, image, first = call(
                image_kernel,
                MESSAGES + [FIELD, FIELD],
                (*arrived, ohi, coef, idx, stiff, scale),
                "image",
            )
            source = image
            arrived = exchange(sent)
    image2, sums = call(
        sums_kernel,
        [FIELD, shape(lax.axis_size("lat"), 1, BS)],
        (*arrived, ohi, coef, idx, stiff, right, image),
        "sums",
    )
    sums = jnp.sum(everywhere(sums, "lat"), axis=0, keepdims=True)
    sums = everywhere(jnp.broadcast_to(sums, (lax.axis_size("lon"), 1, BS)), "lon")
    solution, residual, history = call(
        finish_kernel,
        [shape(2, 1, 1, E), shape(2, 1, 1, E), shape(1, BS)],
        (sums, right, image, image2, directions[0], directions[1]),
        "finish",
    )
    return solution, residual, history[0, :ITERS]


def solution(mesh):
    placed = (
        P(None, "lat", "lon", None),
        P("lat", "lon", None),
        P("lat", "lon", None, None, None),
        P("lat", "lon", None, None, None),
        P("lat", "lon", None, None),
        P("lat", "lon", None),
        P("lat", "lon", None, None),
        P("lat", "lon", None, None),
    )
    return jax.shard_map(
        on_device,
        mesh=mesh,
        in_specs=placed,
        out_specs=(P(None, "lat", "lon", None), P(None, "lat", "lon", None), P()),
        check_vma=False,
    )
```

```python
import jax
import jax.numpy as jnp
from jax import lax
from jax.experimental import pallas as pl
from jax.experimental.pallas import tpu as pltpu
from jax.sharding import PartitionSpec as P

ITERS = 2
EB = 16
BS = 128
E = EB * BS
ND = 256
IFC = 256
OMEGA = 0.8
F32 = jnp.float32
BF16 = jnp.bfloat16
LIMIT = 20 * 1024 * 1024
BEGIN_LIMIT = 60 * 1024 * 1024
NT = (((1,), (1,)), ((), ()))


def complex_times(a, b):
    return a[0] * b[0] - a[1] * b[1], a[0] * b[1] + a[1] * b[0]


def complex_inverse(a):
    scale = a[0] * a[0] + a[1] * a[1]
    return a[0] / scale, -a[1] / scale


def pieces(x):
    first = x.astype(BF16).astype(F32)
    rest = x - first
    second = rest.astype(BF16).astype(F32)
    return first, second, rest - second


def lanes(x, count):
    return jnp.concatenate([x[k : k + 1] for k in range(count)], axis=1)


def to_blocks(row, ref):
    for k in range(EB):
        ref[k : k + 1] = row[:, k * BS : (k + 1) * BS]
    return ref[...]


def block_mask(blocks, rows):
    return lax.broadcasted_iota(jnp.int32, (rows, blocks.shape[1]), 0) == blocks


def lane_onehot(index):
    spot = lax.broadcasted_iota(jnp.int32, (BS, index.shape[1]), 0)
    return jnp.where(spot == index % BS, 1.0, 0.0).astype(BF16)


def take(field, onehot, mask):
    parts = [pieces(part) for part in field]
    stack = jnp.concatenate([parts[c][p] for p in range(3) for c in range(2)], axis=0)
    got = jnp.dot(stack.astype(BF16), onehot[...], preferred_element_type=F32)
    got = got[:32] + got[32:64] + got[64:]
    return [
        jnp.sum(jnp.where(mask, got[16 * c : 16 * c + 16], 0.0), axis=0, keepdims=True)
        for c in range(2)
    ]


def put(rows, onehot, mask):
    parts = [pieces(part) for part in rows]
    stack = jnp.concatenate(
        [jnp.where(mask, parts[c][p], 0.0) for p in range(3) for c in range(2)], axis=0
    )
    got = lax.dot_general(stack.astype(BF16), onehot[...], NT, preferred_element_type=F32)
    got = got[:32] + got[32:64] + got[64:]
    return got[:16], got[16:]


def put_heads(rows, onehot, block):
    spot = lax.broadcasted_iota(jnp.int32, (8, block.shape[1]), 0)
    right = [pieces(part) for part in rows]
    match = (spot % 2 == block) & (spot < 4)
    stack = jnp.concatenate(
        [
            jnp.where(match, jnp.where(spot < 2, right[0][p], right[1][p]), 0.0)
            for p in range(3)
        ],
        axis=0,
    )
    got = lax.dot_general(stack.astype(BF16), onehot[...], NT, preferred_element_type=F32)
    return got[:8] + got[8:16] + got[16:]


def take_heads(own, onehot, block):
    stack = jnp.concatenate(pieces(own), axis=0)
    got = jnp.dot(stack.astype(BF16), onehot[...], preferred_element_type=F32)
    got = got[:8] + got[8:16] + got[16:]
    low = block == 0
    return [jnp.where(low, got[2 * c : 2 * c + 1], got[2 * c + 1 : 2 * c + 2]) for c in range(2)]


def parities():
    return lax.axis_index("lat") % 2 == 0, lax.axis_index("lon") % 2 == 0


def hand_out(refs, towards, at=0):
    even_lat, even_lon = parities()
    refs[0][at : at + 4] = jnp.where(even_lon, towards[2], towards[3])
    refs[1][at : at + 4] = jnp.where(even_lon, towards[3], towards[2])
    refs[2][at : at + 4] = jnp.where(even_lat, towards[0], towards[1])
    refs[3][at : at + 4] = jnp.where(even_lat, towards[1], towards[0])


def collect(refs, at=0):
    even_lat, even_lon = parities()
    wide, near, far, core = [ref[at : at + 4] for ref in refs]
    return (
        jnp.where(even_lat, far, core),
        jnp.where(even_lat, core, far),
        jnp.where(even_lon, wide, near),
        jnp.where(even_lon, near, wide),
    )


def index_rows(idx_ref):
    idx = idx_ref[0, 0]
    return jnp.concatenate([idx[d : d + 1] for d in range(4)], axis=1)


def interface_messages(field, onehot, index):
    got = take(field, onehot, block_mask(index // BS, EB))
    return [
        jnp.concatenate(
            [
                got[c][:, d * IFC + h * BS : d * IFC + (h + 1) * BS]
                for c in range(2)
                for h in range(2)
            ],
            axis=0,
        )
        for d in range(4)
    ]


def interface_sum(arrived, coefs, onehot, index):
    rows = [
        jnp.concatenate(
            [arrived[d][2 * c + h : 2 * c + h + 1] for d in range(4) for h in range(2)], axis=1
        )
        * coefs
        for c in range(2)
    ]
    return put(rows, onehot, block_mask(index // BS, EB))


def pair(ref):
    return ref[0:EB], ref[EB : 2 * EB]


def keep(ref, value):
    ref[0:EB] = value[0]
    ref[EB : 2 * EB] = value[1]


def nodal(rows, onehot_head, onehot_tail, nodes_ref, sign, out_refs, own_ref, at):
    tails = nodes_ref[0, 0, 0:1]
    heads = nodes_ref[0, 0, 1:2]
    own = put_heads(rows, onehot_head, heads // BS)
    ext = put(rows, onehot_tail, block_mask(tails // BS, EB))
    ext = [sign * ext[0], sign * ext[1]]
    own_ref[...] = own
    for c in range(2):
        own_ref[2 * c : 2 * c + 2] += ext[c][0:2]
    towards = [
        jnp.concatenate([ext[0][2 * d : 2 * d + 2], ext[1][2 * d : 2 * d + 2]], axis=0)
        for d in range(1, 5)
    ]
    hand_out(out_refs, towards, at)


def begin_kernel(
    rhs_ref, cond_ref, diag_ref, idx_ref, cnt_ref, coup_ref, nodes_ref,
    m0, m1, m2, m3, coef_ref, value_ref, scale_ref, right_ref, first_ref, own_ref,
    ohi_ref, oht_ref, ohh_ref, blocks, rhs_got, cond_got, diag_got, idx_got, cnt_got, coup_got, nodes_got, sems,
):
    messages = (m0, m1, m2, m3)
    pairs = (
        (nodes_ref, nodes_got), (idx_ref, idx_got), (cnt_ref, cnt_got), (coup_ref, coup_got),
        (cond_ref, cond_got), (rhs_ref, rhs_got), (diag_ref, diag_got),
    )
    copies = [pltpu.make_async_copy(here, there, sems.at[k]) for k, (here, there) in enumerate(pairs)]
    for copy in copies:
        copy.start()
    for copy in copies[:2]:
        copy.wait()
    nodes_ref, idx_ref, cnt_ref, coup_ref, cond_ref, rhs_ref, diag_ref = [there for _, there in pairs]
    index = index_rows(idx_ref)
    ohi_ref[...] = lane_onehot(index)
    oht_ref[...] = lane_onehot(nodes_ref[0, 0, 0:1])
    ohh_ref[...] = lane_onehot(nodes_ref[0, 0, 1:2])
    for copy in copies[2:]:
        copy.wait()
    slot = lax.broadcasted_iota(jnp.int32, (1, IFC), 1)
    coef_ref[...] = jnp.concatenate(
        [jnp.where(slot < cnt_ref[0, 0, d], coup_ref[0, 0, d : d + 1], 0.0) for d in range(4)], axis=1
    )
    eye = lax.broadcasted_iota(jnp.int32, (BS, BS), 0) == lax.broadcasted_iota(jnp.int32, (BS, BS), 1)
    for b in range(EB):
        value_ref[b : b + 1] = jnp.sum(jnp.where(eye, diag_ref[0, 0, b], 0.0), axis=0, keepdims=True)
    value_ref[EB : 2 * EB] = to_blocks(cond_ref[0], blocks)
    value = pair(value_ref)
    inverse = complex_inverse(value)
    scale = (OMEGA * inverse[0], OMEGA * inverse[1])
    keep(scale_ref, scale)
    for c in range(2):
        right_ref[EB * c : EB * c + EB] = to_blocks(rhs_ref[c, 0], blocks)
    first = complex_times(scale, pair(right_ref))
    keep(first_ref, first)
    hand_out(messages, interface_messages(first, ohi_ref, index), 0)
    rows = [lanes(value[c], EB) for c in range(2)]
    nodal(rows, ohh_ref, oht_ref, nodes_ref, 1.0, messages, own_ref, 4)


def weight_kernel(diag_ref, off_ref, idx_ref, nodes_ref, w_ref, ohi_ref, oht_ref, ohh_ref):
    ohi_ref[...] = lane_onehot(index_rows(idx_ref))
    oht_ref[...] = lane_onehot(nodes_ref[0, 0, 0:1])
    ohh_ref[...] = lane_onehot(nodes_ref[0, 0, 1:2])
    eye = lax.broadcasted_iota(jnp.int32, (BS, BS), 0) == lax.broadcasted_iota(jnp.int32, (BS, BS), 1)

    def store(b, at, block):
        high = block.astype(BF16)
        w_ref[b, at : at + BS, 0:BS] = high
        w_ref[b, at : at + BS, BS:] = (block - high.astype(F32)).astype(BF16)

    zero = jnp.zeros((BS, 2 * BS), BF16)
    w_ref[0, 0:BS] = zero
    w_ref[EB - 1, 2 * BS :] = zero
    for b in range(EB):
        store(b, BS, jnp.where(eye, 0.0, diag_ref[0, 0, b]))
        if b < EB - 1:
            off = off_ref[0, 0, b]
            store(b + 1, 0, off)
            store(b, 2 * BS, off.T)


def stiffness(field, value, w_ref, wide, out):
    wide[0:8] = jnp.zeros((8, BS), F32)
    wide[8 * (EB + 1) :] = jnp.zeros((8, BS), F32)
    for c in range(2):
        for p, piece in enumerate(pieces(field[c])):
            wide[pl.ds(8 + 2 * p + c, EB, stride=8)] = piece
    for k in (6, 7):
        wide[pl.ds(8 + k, EB, stride=8)] = jnp.zeros((EB, BS), F32)
    for b in range(EB):
        around = jnp.concatenate([wide[8 * (b + k) : 8 * (b + k) + 8] for k in range(3)], axis=1)
        got = jnp.dot(around.astype(BF16), w_ref[b], preferred_element_type=F32)
        out[8 * b : 8 * b + 8] = got[:, :BS] + got[:, BS:]
    sums = [
        out[pl.ds(c, EB, stride=8)] + out[pl.ds(2 + c, EB, stride=8)] + out[pl.ds(4 + c, EB, stride=8)]
        for c in range(2)
    ]
    turned = complex_times(value, field)
    return sums[0] + turned[0], sums[1] + turned[1]


def local_kernel(field_ref, value_ref, w_ref, out_ref, wide, out):
    keep(out_ref, stiffness(pair(field_ref), pair(value_ref), w_ref, wide, out))


def smooth(arrived, ohi_ref, coef_ref, idx_ref, first_ref, local_ref, scale_ref, right_ref, m, second_ref):
    index = index_rows(idx_ref)
    extra = interface_sum(arrived, coef_ref[...], ohi_ref, index)
    first, local, right = pair(first_ref), pair(local_ref), pair(right_ref)
    change = complex_times(pair(scale_ref), [right[c] - local[c] - extra[c] for c in range(2)])
    second = (first[0] + change[0], first[1] + change[1])
    keep(second_ref, second)
    hand_out(m, interface_messages(second, ohi_ref, index))


def smooth_first_kernel(
    a0, a1, a2, a3, own_ref, ohi_ref, coef_ref, idx_ref, first_ref, local_ref, scale_ref, right_ref,
    m0, m1, m2, m3, second_ref, ninv_ref,
):
    arrived = collect((a0, a1, a2, a3))
    smooth(arrived, ohi_ref, coef_ref, idx_ref, first_ref, local_ref, scale_ref, right_ref, (m0, m1, m2, m3), second_ref)
    sums = own_ref[0:4]
    for part in collect((a0, a1, a2, a3), 4):
        sums = sums + part
    inverse = complex_inverse((sums[0:2], sums[2:4]))
    ninv_ref[0:2] = inverse[0]
    ninv_ref[2:4] = inverse[1]


def smooth_kernel(
    a0, a1, a2, a3, ohi_ref, coef_ref, idx_ref, first_ref, local_ref, scale_ref, right_ref,
    m0, m1, m2, m3, second_ref,
):
    arrived = collect((a0, a1, a2, a3))
    smooth(arrived, ohi_ref, coef_ref, idx_ref, first_ref, local_ref, scale_ref, right_ref, (m0, m1, m2, m3), second_ref)


def restrict_kernel(
    a0, a1, a2, a3, ohi_ref, oht_ref, ohh_ref, coef_ref, idx_ref, nodes_ref, local_ref, right_ref,
    m0, m1, m2, m3, own_ref,
):
    index = index_rows(idx_ref)
    extra = interface_sum(collect((a0, a1, a2, a3)), coef_ref[...], ohi_ref, index)
    local, right = pair(local_ref), pair(right_ref)
    rows = [lanes(right[c] - local[c] - extra[c], EB) for c in range(2)]
    nodal(rows, ohh_ref, oht_ref, nodes_ref, -1.0, (m0, m1, m2, m3), own_ref, 0)


def node_kernel(a0, a1, a2, a3, own_ref, ninv_ref, m0, m1, m2, m3, y_ref):
    sums = own_ref[0:4]
    for part in collect((a0, a1, a2, a3)):
        sums = sums + part
    result = complex_times((ninv_ref[0:2], ninv_ref[2:4]), (sums[0:2], sums[2:4]))
    for ref in (m0, m1, m2, m3, y_ref):
        ref[0:2] = result[0]
        ref[2:4] = result[1]


def prolong_kernel(
    a0, a1, a2, a3, y_ref, ohi_ref, oht_ref, ohh_ref, idx_ref, nodes_ref, second_ref,
    m0, m1, m2, m3, direction_ref,
    blocks, wide,
):
    tails = nodes_ref[0, 0, 0:1]
    heads = nodes_ref[0, 0, 1:2]
    wide[...] = jnp.zeros((2 * EB, BS), F32)
    nodes = (y_ref[...],) + collect((a0, a1, a2, a3))
    for d in range(5):
        for c in range(2):
            wide[EB * c + 2 * d : EB * c + 2 * d + 2] = nodes[d][2 * c : 2 * c + 2]
    low = take(pair(wide), oht_ref, block_mask(tails // BS, EB))
    own = jnp.concatenate([nodes[0], nodes[0]], axis=0)
    high = take_heads(own, ohh_ref, heads // BS)
    second = pair(second_ref)
    direction = [second[c] + to_blocks(high[c] - low[c], blocks) for c in range(2)]
    keep(direction_ref, direction)
    hand_out((m0, m1, m2, m3), interface_messages(direction, ohi_ref, index_rows(idx_ref)))


def image_kernel(
    a0, a1, a2, a3, ohi_ref, coef_ref, idx_ref, local_ref, scale_ref,
    m0, m1, m2, m3, image_ref, first_ref,
):
    index = index_rows(idx_ref)
    extra = interface_sum(collect((a0, a1, a2, a3)), coef_ref[...], ohi_ref, index)
    local = pair(local_ref)
    image = (local[0] + extra[0], local[1] + extra[1])
    keep(image_ref, image)
    first = complex_times(pair(scale_ref), image)
    keep(first_ref, first)
    hand_out((m0, m1, m2, m3), interface_messages(first, ohi_ref, index))


def total(x):
    return jnp.sum(jnp.sum(x, axis=0, keepdims=True), axis=1, keepdims=True)


def inner(a, b):
    return total(a[0] * b[0] + a[1] * b[1]), total(a[0] * b[1] - a[1] * b[0])


def sums_kernel(
    a0, a1, a2, a3, ohi_ref, coef_ref, idx_ref, local_ref, right_ref, image_ref,
    image2_ref, sums_ref,
):
    index = index_rows(idx_ref)
    extra = interface_sum(collect((a0, a1, a2, a3)), coef_ref[...], ohi_ref, index)
    local, right, image = pair(local_ref), pair(right_ref), pair(image_ref)
    image2 = (local[0] + extra[0], local[1] + extra[1])
    keep(image2_ref, image2)
    rest = (right[0] - image[0], right[1] - image[1])
    turn = (image[0] - image2[0], image[1] - image2[1])
    found = [inner(right, right)[0], inner(image, image)[0], inner(rest, rest)[0], inner(turn, turn)[0]]
    found += [*inner(image, rest), *inner(turn, rest), *inner(turn, image)]
    lane = lax.broadcasted_iota(jnp.int32, (1, BS), 1)
    row = jnp.zeros((1, BS), F32)
    for k, value in enumerate(found):
        row = jnp.where(lane == k, value, row)
    sums_ref[...] = jnp.broadcast_to(row[None], sums_ref.shape)


def finish_kernel(
    sums_ref, right_ref, image_ref, image2_ref, direction_ref, direction2_ref,
    solution_ref, residual_ref, history_ref,
):
    row = jnp.sum(sums_ref[...], axis=0)
    lane = lax.broadcasted_iota(jnp.int32, (1, BS), 1)
    found = [jnp.sum(jnp.where(lane == k, row, 0.0), axis=1, keepdims=True) for k in range(10)]
    start, ww, rr, tt = found[:4]
    wr, tr, tw = found[4:6], found[6:8], found[8:10]
    extra = (wr[0] / ww, wr[1] / ww)
    alpha = (1.0 + extra[0], extra[1])
    fresh = rr - (wr[0] * extra[0] + wr[1] * extra[1])
    moved = complex_times(extra, tw)
    c2 = complex_times((alpha[0], -alpha[1]), (tr[0] - moved[0], tr[1] - moved[1]))
    cross = complex_times(complex_times((extra[0], -extra[1]), alpha), (tw[0], -tw[1]))
    ww2 = (alpha[0] * alpha[0] + alpha[1] * alpha[1]) * tt
    ww2 = ww2 + (extra[0] * extra[0] + extra[1] * extra[1]) * ww - 2.0 * cross[0]
    alpha2 = (c2[0] / ww2, c2[1] / ww2)
    fresh2 = fresh - (c2[0] * alpha2[0] + c2[1] * alpha2[1])
    history_ref[...] = jnp.where(lane == 0, fresh / start, fresh2 / start)
    right, image, image2 = pair(right_ref), pair(image_ref), pair(image2_ref)
    direction, direction2 = pair(direction_ref), pair(direction2_ref)
    step = complex_times(alpha, direction)
    other = complex_times(alpha, direction2)
    step2 = complex_times(alpha2, (direction[0] - other[0], direction[1] - other[1]))
    away = complex_times(extra, image)
    other = complex_times(alpha, image2)
    away2 = complex_times(alpha2, (image[0] - other[0], image[1] - other[1]))
    for c in range(2):
        solution_ref[c, 0] = lanes(step[c] + step2[c], EB)
        residual_ref[c, 0] = lanes(right[c] - image[c] - away[c] - away2[c], EB)


def shape(*dims, dtype=F32):
    return jax.ShapeDtypeStruct(dims, dtype)


FIELD = shape(2 * EB, BS)
MESSAGES = [shape(4, BS)] * 4


def call(body, outs, args, name, scratch=(), space=pltpu.VMEM, limit=LIMIT, flops=0):
    specs = [pl.BlockSpec(memory_space=space)] * len(args)
    moved = sum(a.size * a.dtype.itemsize for a in args)
    return pl.pallas_call(
        body,
        out_shape=outs,
        in_specs=specs,
        out_specs=[pl.BlockSpec(memory_space=pltpu.VMEM)] * len(outs),
        scratch_shapes=scratch,
        compiler_params=pltpu.CompilerParams(vmem_limit_bytes=limit),
        cost_estimate=pl.CostEstimate(flops=flops, bytes_accessed=moved, transcendentals=0),
        name=name,
    )(*args)


def swap(pairs):
    return [(a, b) for a, b in pairs] + [(b, a) for a, b in pairs]


def exchange(messages):
    lat, lon = lax.axis_size("lat"), lax.axis_size("lon")
    swaps = (
        ("lon", swap([(k, (k + 1) % lon) for k in range(1, lon, 2)])),
        ("lon", swap([(k, k + 1) for k in range(0, lon, 2)])),
        ("lat", swap([(k, k + 1) for k in range(1, lat - 1, 2)])),
        ("lat", swap([(k, k + 1) for k in range(0, lat, 2)])),
    )
    return [lax.ppermute(message, *pairs) for message, pairs in zip(messages, swaps)]


def everywhere(row, axis):
    return lax.all_to_all(row, axis, 0, 0)


def on_device(rhs, cond, blk_diag, blk_off, idx, cnt, coup, nodes):
    blocks = pltpu.VMEM((EB, BS), F32)
    wide = pltpu.VMEM((8 * (EB + 2), BS), F32)
    out = pltpu.VMEM((8 * EB, BS), F32)
    onehots = [(BS, 4 * IFC), (BS, E), (BS, E)]
    *sent, coef, value, scale, right, first, own = call(
        begin_kernel,
        [shape(8, BS)] * 4 + [shape(1, 4 * IFC)] + [FIELD] * 4 + [shape(8, BS)],
        (rhs, cond, blk_diag, idx, cnt, coup, nodes),
        "begin",
        scratch=[pltpu.VMEM(dims, BF16) for dims in onehots]
        + [blocks]
        + [pltpu.VMEM(part.shape, part.dtype) for part in (rhs, cond, blk_diag, idx)]
        + [pltpu.SMEM(cnt.shape, cnt.dtype)]
        + [pltpu.VMEM(part.shape, part.dtype) for part in (coup, nodes)]
        + [pltpu.SemaphoreType.DMA((7,))],
        space=pltpu.HBM,
        limit=BEGIN_LIMIT,
    )
    arrived = exchange(sent)
    weights, ohi, oht, ohh = call(
        weight_kernel,
        [shape(EB, 3 * BS, 2 * BS, dtype=BF16)] + [shape(*dims, dtype=BF16) for dims in onehots],
        (blk_diag, blk_off, idx, nodes),
        "weights",
        flops=10**7,
    )

    def local(field):
        return call(
            local_kernel, [FIELD], (field, value, weights), "local", scratch=[wide, out], flops=2 * 8 * EB * 3 * BS * 2 * BS
        )[0]

    images, directions = [], []
    for step in range(ITERS):
        stiff = local(first)
        if step == 0:
            *sent, second, ninv = call(
                smooth_first_kernel,
                MESSAGES + [FIELD, shape(4, BS)],
                (*arrived, own, ohi, coef, idx, first, stiff, scale, right),
                "smooth_first",
            )
            source = right
        else:
            *sent, second = call(
                smooth_kernel,
                MESSAGES + [FIELD],
                (*arrived, ohi, coef, idx, first, stiff, scale, source),
                "smooth",
            )
        arrived = exchange(sent)
        stiff = local(second)
        *sent, own = call(
            restrict_kernel,
            MESSAGES + [shape(8, BS)],
            (*arrived, ohi, oht, ohh, coef, idx, nodes, stiff, source),
            "restrict",
        )
        arrived = exchange(sent)
        *sent, y = call(node_kernel, MESSAGES + [shape(4, BS)], (*arrived, own, ninv), "node")
        arrived = exchange(sent)
        *sent, direction = call(
            prolong_kernel,
            MESSAGES + [FIELD],
            (*arrived, y, ohi, oht, ohh, idx, nodes, second),
            "prolong",
            scratch=[blocks, pltpu.VMEM((2 * EB, BS), F32)],
        )
        directions.append(direction)
        arrived = exchange(sent)
        stiff = local(direction)
        if step == 0:
            *sent, image, first = call(
                image_kernel,
                MESSAGES + [FIELD, FIELD],
                (*arrived, ohi, coef, idx, stiff, scale),
                "image",
            )
            source = image
            arrived = exchange(sent)
    image2, sums = call(
        sums_kernel,
        [FIELD, shape(lax.axis_size("lat"), 1, BS)],
        (*arrived, ohi, coef, idx, stiff, right, image),
        "sums",
    )
    sums = jnp.sum(everywhere(sums, "lat"), axis=0, keepdims=True)
    sums = everywhere(jnp.broadcast_to(sums, (lax.axis_size("lon"), 1, BS)), "lon")
    solution, residual, history = call(
        finish_kernel,
        [shape(2, 1, 1, E), shape(2, 1, 1, E), shape(1, BS)],
        (sums, right, image, image2, directions[0], directions[1]),
        "finish",
    )
    return solution, residual, history[0, :ITERS]


def solution(mesh):
    placed = (
        P(None, "lat", "lon", None),
        P("lat", "lon", None),
        P("lat", "lon", None, None, None),
        P("lat", "lon", None, None, None),
        P("lat", "lon", None, None),
        P("lat", "lon", None),
        P("lat", "lon", None, None),
        P("lat", "lon", None, None),
    )
    return jax.shard_map(
        on_device,
        mesh=mesh,
        in_specs=placed,
        out_specs=(P(None, "lat", "lon", None), P(None, "lat", "lon", None), P()),
        check_vma=False,
    )
```

```python
import functools

import jax
import jax.numpy as jnp
from jax import lax
from jax.experimental import pallas as pl
from jax.experimental.pallas import tpu as pltpu
from jax.sharding import PartitionSpec as P

ITERS = 2
EB = 16
BS = 128
E = EB * BS
ND = 256
IFC = 256
OMEGA = 0.8
F32 = jnp.float32
BF16 = jnp.bfloat16
LIMIT = 20 * 1024 * 1024
BEGIN_LIMIT = 60 * 1024 * 1024
NT = (((1,), (1,)), ((), ()))


def complex_times(a, b):
    return a[0] * b[0] - a[1] * b[1], a[0] * b[1] + a[1] * b[0]


def complex_inverse(a):
    scale = a[0] * a[0] + a[1] * a[1]
    return a[0] / scale, -a[1] / scale


def pieces(x):
    first = x.astype(BF16).astype(F32)
    rest = x - first
    second = rest.astype(BF16).astype(F32)
    return first, second, rest - second


def lanes(x, count):
    return jnp.concatenate([x[k : k + 1] for k in range(count)], axis=1)


def to_blocks(row, ref):
    for k in range(EB):
        ref[k : k + 1] = row[:, k * BS : (k + 1) * BS]
    return ref[...]


def block_mask(blocks, rows):
    return lax.broadcasted_iota(jnp.int32, (rows, blocks.shape[1]), 0) == blocks


def lane_onehot(index):
    spot = lax.broadcasted_iota(jnp.int32, (BS, index.shape[1]), 0)
    return jnp.where(spot == index % BS, 1.0, 0.0).astype(BF16)


def take(field, onehot, mask):
    parts = [pieces(part) for part in field]
    stack = jnp.concatenate([parts[c][p] for p in range(3) for c in range(2)], axis=0)
    got = jnp.dot(stack.astype(BF16), onehot[...], preferred_element_type=F32)
    got = got[:32] + got[32:64] + got[64:]
    return [
        jnp.sum(jnp.where(mask, got[16 * c : 16 * c + 16], 0.0), axis=0, keepdims=True)
        for c in range(2)
    ]


def put(rows, onehot, mask):
    parts = [pieces(part) for part in rows]
    stack = jnp.concatenate(
        [jnp.where(mask, parts[c][p], 0.0) for p in range(3) for c in range(2)], axis=0
    )
    got = lax.dot_general(stack.astype(BF16), onehot[...], NT, preferred_element_type=F32)
    got = got[:32] + got[32:64] + got[64:]
    return got[:16], got[16:]


def put_heads(rows, onehot, block):
    spot = lax.broadcasted_iota(jnp.int32, (8, block.shape[1]), 0)
    right = [pieces(part) for part in rows]
    match = (spot % 2 == block) & (spot < 4)
    stack = jnp.concatenate(
        [
            jnp.where(match, jnp.where(spot < 2, right[0][p], right[1][p]), 0.0)
            for p in range(3)
        ],
        axis=0,
    )
    got = lax.dot_general(stack.astype(BF16), onehot[...], NT, preferred_element_type=F32)
    return got[:8] + got[8:16] + got[16:]


def take_heads(own, onehot, block):
    stack = jnp.concatenate(pieces(own), axis=0)
    got = jnp.dot(stack.astype(BF16), onehot[...], preferred_element_type=F32)
    got = got[:8] + got[8:16] + got[16:]
    low = block == 0
    return [jnp.where(low, got[2 * c : 2 * c + 1], got[2 * c + 1 : 2 * c + 2]) for c in range(2)]


def parities():
    return lax.axis_index("lat") % 2 == 0, lax.axis_index("lon") % 2 == 0


def hand_out(refs, towards, at=0):
    even_lat, even_lon = parities()
    refs[0][at : at + 4] = jnp.where(even_lon, towards[2], towards[3])
    refs[1][at : at + 4] = jnp.where(even_lon, towards[3], towards[2])
    refs[2][at : at + 4] = jnp.where(even_lat, towards[0], towards[1])
    refs[3][at : at + 4] = jnp.where(even_lat, towards[1], towards[0])


def collect(refs, at=0):
    even_lat, even_lon = parities()
    wide, near, far, core = [ref[at : at + 4] for ref in refs]
    return (
        jnp.where(even_lat, far, core),
        jnp.where(even_lat, core, far),
        jnp.where(even_lon, wide, near),
        jnp.where(even_lon, near, wide),
    )


def index_rows(idx_ref):
    idx = idx_ref[0, 0]
    return jnp.concatenate([idx[d : d + 1] for d in range(4)], axis=1)


def interface_messages(field, onehot, index):
    got = take(field, onehot, block_mask(index // BS, EB))
    return [
        jnp.concatenate(
            [
                got[c][:, d * IFC + h * BS : d * IFC + (h + 1) * BS]
                for c in range(2)
                for h in range(2)
            ],
            axis=0,
        )
        for d in range(4)
    ]


def interface_sum(arrived, coefs, onehot, index):
    rows = [
        jnp.concatenate(
            [arrived[d][2 * c + h : 2 * c + h + 1] for d in range(4) for h in range(2)], axis=1
        )
        * coefs
        for c in range(2)
    ]
    return put(rows, onehot, block_mask(index // BS, EB))


def pair(ref):
    return ref[0:EB], ref[EB : 2 * EB]


def keep(ref, value):
    ref[0:EB] = value[0]
    ref[EB : 2 * EB] = value[1]


def nodal(rows, onehot_head, onehot_tail, nodes_ref, sign):
    tails = nodes_ref[0, 0, 0:1]
    heads = nodes_ref[0, 0, 1:2]
    own = put_heads(rows, onehot_head, heads // BS)
    ext = put(rows, onehot_tail, block_mask(tails // BS, EB))
    parts = [
        sign * jnp.concatenate([ext[0][2 * d : 2 * d + 2], ext[1][2 * d : 2 * d + 2]], axis=0)
        for d in range(5)
    ]
    return own[0:4] + parts[0], parts[1:]


def begin_kernel(
    rhs_ref, cond_ref, diag_ref, idx_ref, cnt_ref, coup_ref, nodes_ref,
    m0, m1, m2, m3, coef_ref, value_ref, scale_ref, right_ref, first_ref, own_ref,
    ohi_ref, oht_ref, ohh_ref, blocks, rhs_got, cond_got, diag_got, idx_got, cnt_got, coup_got, nodes_got, sems,
):
    messages = (m0, m1, m2, m3)
    pairs = (
        (nodes_ref, nodes_got), (idx_ref, idx_got), (cnt_ref, cnt_got), (coup_ref, coup_got),
        (cond_ref, cond_got), (rhs_ref, rhs_got), (diag_ref, diag_got),
    )
    copies = [pltpu.make_async_copy(here, there, sems.at[k]) for k, (here, there) in enumerate(pairs)]
    for copy in copies:
        copy.start()
    for copy in copies[:2]:
        copy.wait()
    nodes_ref, idx_ref, cnt_ref, coup_ref, cond_ref, rhs_ref, diag_ref = [there for _, there in pairs]
    index = index_rows(idx_ref)
    ohi_ref[...] = lane_onehot(index)
    oht_ref[...] = lane_onehot(nodes_ref[0, 0, 0:1])
    ohh_ref[...] = lane_onehot(nodes_ref[0, 0, 1:2])
    for copy in copies[2:]:
        copy.wait()
    slot = lax.broadcasted_iota(jnp.int32, (1, IFC), 1)
    coef_ref[...] = jnp.concatenate(
        [jnp.where(slot < cnt_ref[0, 0, d], coup_ref[0, 0, d : d + 1], 0.0) for d in range(4)], axis=1
    )
    eye = lax.broadcasted_iota(jnp.int32, (BS, BS), 0) == lax.broadcasted_iota(jnp.int32, (BS, BS), 1)
    for b in range(EB):
        value_ref[b : b + 1] = jnp.sum(jnp.where(eye, diag_ref[0, 0, b], 0.0), axis=0, keepdims=True)
    value_ref[EB : 2 * EB] = to_blocks(cond_ref[0], blocks)
    value = pair(value_ref)
    inverse = complex_inverse(value)
    scale = (OMEGA * inverse[0], OMEGA * inverse[1])
    keep(scale_ref, scale)
    for c in range(2):
        right_ref[EB * c : EB * c + EB] = to_blocks(rhs_ref[c, 0], blocks)
    first = complex_times(scale, pair(right_ref))
    keep(first_ref, first)
    hand_out(messages, interface_messages(first, ohi_ref, index), 0)
    rows = [lanes(value[c], EB) for c in range(2)]
    own, towards = nodal(rows, ohh_ref, oht_ref, nodes_ref, 1.0)
    own_ref[0:4] = own
    hand_out(messages, towards, 4)
    ends = [to_blocks(nodes_ref[0, 0, k : k + 1].astype(F32), blocks) for k in (1, 0)]
    hand_out(messages, interface_messages(ends, ohi_ref, index), 8)


def weight_kernel(diag_ref, off_ref, idx_ref, nodes_ref, w_ref, ohi_ref, oht_ref, ohh_ref):
    ohi_ref[...] = lane_onehot(index_rows(idx_ref))
    oht_ref[...] = lane_onehot(nodes_ref[0, 0, 0:1])
    ohh_ref[...] = lane_onehot(nodes_ref[0, 0, 1:2])
    eye = lax.broadcasted_iota(jnp.int32, (BS, BS), 0) == lax.broadcasted_iota(jnp.int32, (BS, BS), 1)

    def store(b, at, block):
        high = block.astype(BF16)
        w_ref[b, at : at + BS, 0:BS] = high
        w_ref[b, at : at + BS, BS:] = (block - high.astype(F32)).astype(BF16)

    zero = jnp.zeros((BS, 2 * BS), BF16)
    w_ref[0, 0:BS] = zero
    w_ref[EB - 1, 2 * BS :] = zero
    for b in range(EB):
        store(b, BS, jnp.where(eye, 0.0, diag_ref[0, 0, b]))
        if b < EB - 1:
            off = off_ref[0, 0, b]
            store(b + 1, 0, off)
            store(b, 2 * BS, off.T)


def stiffness(field, value, w_ref, wide, out):
    wide[0:8] = jnp.zeros((8, BS), F32)
    wide[8 * (EB + 1) :] = jnp.zeros((8, BS), F32)
    for c in range(2):
        for p, piece in enumerate(pieces(field[c])):
            wide[pl.ds(8 + 2 * p + c, EB, stride=8)] = piece
    for k in (6, 7):
        wide[pl.ds(8 + k, EB, stride=8)] = jnp.zeros((EB, BS), F32)
    for b in range(EB):
        around = jnp.concatenate([wide[8 * (b + k) : 8 * (b + k) + 8] for k in range(3)], axis=1)
        got = jnp.dot(around.astype(BF16), w_ref[b], preferred_element_type=F32)
        out[8 * b : 8 * b + 8] = got[:, :BS] + got[:, BS:]
    sums = [
        out[pl.ds(c, EB, stride=8)] + out[pl.ds(2 + c, EB, stride=8)] + out[pl.ds(4 + c, EB, stride=8)]
        for c in range(2)
    ]
    turned = complex_times(value, field)
    return sums[0] + turned[0], sums[1] + turned[1]


def local_kernel(field_ref, value_ref, w_ref, out_ref, wide, out):
    keep(out_ref, stiffness(pair(field_ref), pair(value_ref), w_ref, wide, out))


def smooth(arrived, ohi_ref, coef_ref, idx_ref, first_ref, local_ref, scale_ref, right_ref, m, second_ref):
    index = index_rows(idx_ref)
    extra = interface_sum(arrived, coef_ref[...], ohi_ref, index)
    first, local, right = pair(first_ref), pair(local_ref), pair(right_ref)
    change = complex_times(pair(scale_ref), [right[c] - local[c] - extra[c] for c in range(2)])
    second = (first[0] + change[0], first[1] + change[1])
    keep(second_ref, second)
    hand_out(m, interface_messages(second, ohi_ref, index))


def smooth_first_kernel(
    a0, a1, a2, a3, own_ref, ohi_ref, coef_ref, idx_ref, first_ref, local_ref, scale_ref, right_ref,
    m0, m1, m2, m3, second_ref, ninv_ref, ends_ref, away_ref,
):
    arrived = collect((a0, a1, a2, a3))
    smooth(arrived, ohi_ref, coef_ref, idx_ref, first_ref, local_ref, scale_ref, right_ref, (m0, m1, m2, m3), second_ref)
    sums = own_ref[0:4]
    for part in collect((a0, a1, a2, a3), 4):
        sums = sums + part
    inverse = complex_inverse((sums[0:2], sums[2:4]))
    ninv_ref[0:2] = inverse[0]
    ninv_ref[2:4] = inverse[1]
    for d, part in enumerate(collect((a0, a1, a2, a3), 8)):
        for k in range(2):
            row = jnp.concatenate([part[2 * k : 2 * k + 1], part[2 * k + 1 : 2 * k + 2]], axis=1)
            row = row.astype(jnp.int32)
            at = (2 * d + k) * IFC
            ends_ref[:, at : at + IFC] = row
            away_ref[:, at : at + IFC] = lane_onehot(row)


def smooth_kernel(
    a0, a1, a2, a3, ohi_ref, coef_ref, idx_ref, first_ref, local_ref, scale_ref, right_ref,
    m0, m1, m2, m3, second_ref,
):
    arrived = collect((a0, a1, a2, a3))
    smooth(arrived, ohi_ref, coef_ref, idx_ref, first_ref, local_ref, scale_ref, right_ref, (m0, m1, m2, m3), second_ref)


def restrict_kernel(
    a0, a1, a2, a3, ohi_ref, oht_ref, ohh_ref, coef_ref, idx_ref, nodes_ref, local_ref, right_ref,
    far_ref, core_ref, row_ref, extra_ref,
):
    index = index_rows(idx_ref)
    extra = interface_sum(collect((a0, a1, a2, a3)), coef_ref[...], ohi_ref, index)
    keep(extra_ref, extra)
    local, right = pair(local_ref), pair(right_ref)
    rows = [lanes(right[c] - local[c] - extra[c], EB) for c in range(2)]
    own, towards = nodal(rows, ohh_ref, oht_ref, nodes_ref, -1.0)
    even_lat, _ = parities()
    far_ref[...] = jnp.where(even_lat, towards[0], towards[1])
    core_ref[...] = jnp.where(even_lat, towards[1], towards[0])
    for k, part in enumerate((own, towards[2], towards[3])):
        row_ref[4 * k : 4 * k + 4] = part


def row_kernel(far_ref, core_ref, row_ref, *refs):
    out_ref = refs[-1]
    parts = [row_ref[0:4] + far_ref[...] + core_ref[...], row_ref[4:8], row_ref[8:12]]
    parts += [ref[...] for ref in refs[:-1]]
    out_ref[...] = jnp.broadcast_to(jnp.concatenate(parts, axis=0)[None], out_ref.shape)


def column_kernel(known, lon, row_ref, *refs):
    inverse_ref, near_ref, out_ref = refs if known else (refs[2], refs[0], refs[1])
    me = lax.axis_index("lon")

    def at(step):
        return lax.rem(me + (lon + step), lon)

    for k in range(5):
        sums = row_ref[at(k - 2), 0:4] + row_ref[at(k - 1), 4:8] + row_ref[at(k - 3), 8:12]
        if not known:
            inverse_ref[4 * k : 4 * k + 4] = row_ref[at(k - 2), 12:16]
        inverse = inverse_ref[4 * k : 4 * k + 4]
        result = complex_times((inverse[0:2], inverse[2:4]), (sums[0:2], sums[2:4]))
        near_ref[4 * k : 4 * k + 4] = jnp.concatenate(result, axis=0)
    out_ref[...] = jnp.broadcast_to(near_ref[4:16][None], out_ref.shape)


def extend(nodes, ref):
    for d in range(5):
        for c in range(2):
            ref[EB * c + 2 * d : EB * c + 2 * d + 2] = nodes[d][2 * c : 2 * c + 2]
    return pair(ref)


def gradient(nodes, ref, onehot_head, onehot_tail, heads, tails):
    low = take(extend(nodes, ref), onehot_tail, block_mask(tails // BS, EB))
    high = take_heads(jnp.concatenate([nodes[0], nodes[0]], axis=0), onehot_head, heads // BS)
    return [high[c] - low[c] for c in range(2)]


def prolong(
    lat, column_ref, near_ref, ohi_ref, oht_ref, ohh_ref, coef_ref, idx_ref, nodes_ref, second_ref, extra_ref,
    ends_ref, away_ref, value_ref, w_ref, direction_ref, blocks, ext, wide, out,
):
    me = lax.axis_index("lat")

    def node(down, right):
        if down == 0:
            return near_ref[4 * right + 8 : 4 * right + 12]
        there = jnp.clip(me + down, 0, lat - 1)
        return column_ref[there, 4 * right + 4 : 4 * right + 8]

    def around(down, right):
        steps = ((0, 0), (-1, 0), (1, 0), (0, -1), (0, 1))
        return [node(down + i, right + j) for i, j in steps]

    ext[...] = jnp.zeros((2 * EB, BS), F32)
    rise = gradient(around(0, 0), ext, ohh_ref, oht_ref, nodes_ref[0, 0, 1:2], nodes_ref[0, 0, 0:1])
    second = pair(second_ref)
    direction = [second[c] + to_blocks(rise[c], blocks) for c in range(2)]
    keep(direction_ref, direction)
    rises = []
    for d, step in enumerate(((-1, 0), (1, 0), (0, -1), (0, 1))):
        spots = [pl.ds((2 * d + k) * IFC, IFC) for k in range(2)]
        rise = gradient(
            around(*step), ext, away_ref.at[:, spots[0]], away_ref.at[:, spots[1]],
            ends_ref[:, spots[0]], ends_ref[:, spots[1]],
        )
        if d < 2:
            there = me + step[0]
            real = (there >= 0) & (there < lat)
            rise = [jnp.where(real, part, 0.0) for part in rise]
        rises.append(rise)
    rows = [jnp.concatenate([rise[c] for rise in rises], axis=1) * coef_ref[...] for c in range(2)]
    more = put(rows, ohi_ref, block_mask(index_rows(idx_ref) // BS, EB))
    extra = pair(extra_ref)
    local = stiffness(direction, pair(value_ref), w_ref, wide, out)
    return [local[c] + extra[c] + more[c] for c in range(2)]


def prolong_first_kernel(
    lat, column_ref, near_ref, ohi_ref, oht_ref, ohh_ref, coef_ref, idx_ref, nodes_ref, second_ref, extra_ref,
    ends_ref, away_ref, value_ref, w_ref, scale_ref,
    m0, m1, m2, m3, direction_ref, image_ref, first_ref,
    *scratch,
):
    image = prolong(
        lat, column_ref, near_ref, ohi_ref, oht_ref, ohh_ref, coef_ref, idx_ref, nodes_ref, second_ref, extra_ref,
        ends_ref, away_ref, value_ref, w_ref, direction_ref, *scratch,
    )
    keep(image_ref, image)
    first = complex_times(pair(scale_ref), image)
    keep(first_ref, first)
    hand_out((m0, m1, m2, m3), interface_messages(first, ohi_ref, index_rows(idx_ref)))


def total(x):
    return jnp.sum(jnp.sum(x, axis=0, keepdims=True), axis=1, keepdims=True)


def inner(a, b):
    return total(a[0] * b[0] + a[1] * b[1]), total(a[0] * b[1] - a[1] * b[0])


def prolong_last_kernel(
    lat, column_ref, near_ref, ohi_ref, oht_ref, ohh_ref, coef_ref, idx_ref, nodes_ref, second_ref, extra_ref,
    ends_ref, away_ref, value_ref, w_ref, right_ref, image_ref,
    direction_ref, image2_ref, sums_ref,
    *scratch,
):
    image2 = prolong(
        lat, column_ref, near_ref, ohi_ref, oht_ref, ohh_ref, coef_ref, idx_ref, nodes_ref, second_ref, extra_ref,
        ends_ref, away_ref, value_ref, w_ref, direction_ref, *scratch,
    )
    right, image = pair(right_ref), pair(image_ref)
    keep(image2_ref, image2)
    rest = (right[0] - image[0], right[1] - image[1])
    turn = (image[0] - image2[0], image[1] - image2[1])
    found = [inner(right, right)[0], inner(image, image)[0], inner(rest, rest)[0], inner(turn, turn)[0]]
    found += [*inner(image, rest), *inner(turn, rest), *inner(turn, image)]
    lane = lax.broadcasted_iota(jnp.int32, (1, BS), 1)
    row = jnp.zeros((1, BS), F32)
    for k, value in enumerate(found):
        row = jnp.where(lane == k, value, row)
    sums_ref[...] = jnp.broadcast_to(row[None], sums_ref.shape)


def finish_kernel(
    sums_ref, right_ref, image_ref, image2_ref, direction_ref, direction2_ref,
    solution_ref, residual_ref, history_ref,
):
    row = jnp.sum(sums_ref[...], axis=0)
    lane = lax.broadcasted_iota(jnp.int32, (1, BS), 1)
    found = [jnp.sum(jnp.where(lane == k, row, 0.0), axis=1, keepdims=True) for k in range(10)]
    start, ww, rr, tt = found[:4]
    wr, tr, tw = found[4:6], found[6:8], found[8:10]
    extra = (wr[0] / ww, wr[1] / ww)
    alpha = (1.0 + extra[0], extra[1])
    fresh = rr - (wr[0] * extra[0] + wr[1] * extra[1])
    moved = complex_times(extra, tw)
    c2 = complex_times((alpha[0], -alpha[1]), (tr[0] - moved[0], tr[1] - moved[1]))
    cross = complex_times(complex_times((extra[0], -extra[1]), alpha), (tw[0], -tw[1]))
    ww2 = (alpha[0] * alpha[0] + alpha[1] * alpha[1]) * tt
    ww2 = ww2 + (extra[0] * extra[0] + extra[1] * extra[1]) * ww - 2.0 * cross[0]
    alpha2 = (c2[0] / ww2, c2[1] / ww2)
    fresh2 = fresh - (c2[0] * alpha2[0] + c2[1] * alpha2[1])
    history_ref[...] = jnp.where(lane == 0, fresh / start, fresh2 / start)
    right, image, image2 = pair(right_ref), pair(image_ref), pair(image2_ref)
    direction, direction2 = pair(direction_ref), pair(direction2_ref)
    step = complex_times(alpha, direction)
    other = complex_times(alpha, direction2)
    step2 = complex_times(alpha2, (direction[0] - other[0], direction[1] - other[1]))
    away = complex_times(extra, image)
    other = complex_times(alpha, image2)
    away2 = complex_times(alpha2, (image[0] - other[0], image[1] - other[1]))
    for c in range(2):
        solution_ref[c, 0] = lanes(step[c] + step2[c], EB)
        residual_ref[c, 0] = lanes(right[c] - image[c] - away[c] - away2[c], EB)


def shape(*dims, dtype=F32):
    return jax.ShapeDtypeStruct(dims, dtype)


FIELD = shape(2 * EB, BS)
MESSAGES = [shape(4, BS)] * 4


def call(body, outs, args, name, scratch=(), space=pltpu.VMEM, limit=LIMIT, flops=0):
    specs = [pl.BlockSpec(memory_space=space)] * len(args)
    moved = sum(a.size * a.dtype.itemsize for a in args)
    return pl.pallas_call(
        body,
        out_shape=outs,
        in_specs=specs,
        out_specs=[pl.BlockSpec(memory_space=pltpu.VMEM)] * len(outs),
        scratch_shapes=scratch,
        compiler_params=pltpu.CompilerParams(vmem_limit_bytes=limit),
        cost_estimate=pl.CostEstimate(flops=flops, bytes_accessed=moved, transcendentals=0),
        name=name,
    )(*args)


def swap(pairs):
    return [(a, b) for a, b in pairs] + [(b, a) for a, b in pairs]


def exchange(messages):
    lat, lon = lax.axis_size("lat"), lax.axis_size("lon")
    swaps = (
        ("lon", swap([(k, (k + 1) % lon) for k in range(1, lon, 2)])),
        ("lon", swap([(k, k + 1) for k in range(0, lon, 2)])),
        ("lat", swap([(k, k + 1) for k in range(1, lat - 1, 2)])),
        ("lat", swap([(k, k + 1) for k in range(0, lat, 2)])),
    )
    return [lax.ppermute(message, *pairs) for message, pairs in zip(messages, swaps[4 - len(messages) :])]


def everywhere(row, axis):
    return lax.all_to_all(row, axis, 0, 0)


def on_device(rhs, cond, blk_diag, blk_off, idx, cnt, coup, nodes):
    blocks = pltpu.VMEM((EB, BS), F32)
    wide = pltpu.VMEM((8 * (EB + 2), BS), F32)
    out = pltpu.VMEM((8 * EB, BS), F32)
    onehots = [(BS, 4 * IFC), (BS, E), (BS, E)]
    *sent, coef, value, scale, right, first, own = call(
        begin_kernel,
        [shape(12, BS)] * 4 + [shape(1, 4 * IFC)] + [FIELD] * 4 + [shape(4, BS)],
        (rhs, cond, blk_diag, idx, cnt, coup, nodes),
        "begin",
        scratch=[pltpu.VMEM(dims, BF16) for dims in onehots]
        + [blocks]
        + [pltpu.VMEM(part.shape, part.dtype) for part in (rhs, cond, blk_diag, idx)]
        + [pltpu.SMEM(cnt.shape, cnt.dtype)]
        + [pltpu.VMEM(part.shape, part.dtype) for part in (coup, nodes)]
        + [pltpu.SemaphoreType.DMA((7,))],
        space=pltpu.HBM,
        limit=BEGIN_LIMIT,
    )
    arrived = exchange(sent)
    weights, ohi, oht, ohh = call(
        weight_kernel,
        [shape(EB, 3 * BS, 2 * BS, dtype=BF16)] + [shape(*dims, dtype=BF16) for dims in onehots],
        (blk_diag, blk_off, idx, nodes),
        "weights",
        flops=10**7,
    )

    def local(field):
        return call(
            local_kernel, [FIELD], (field, value, weights), "local", scratch=[wide, out], flops=2 * 8 * EB * 3 * BS * 2 * BS
        )[0]

    lat, lon = lax.axis_size("lat"), lax.axis_size("lon")
    scratch = [blocks, pltpu.VMEM((2 * EB, BS), F32), wide, out]
    directions = []
    for step in range(ITERS):
        stiff = local(first)
        if step == 0:
            *sent, second, ninv, ends, away = call(
                smooth_first_kernel,
                MESSAGES + [FIELD, shape(4, BS), shape(1, 8 * IFC, dtype=jnp.int32), shape(BS, 8 * IFC, dtype=BF16)],
                (*arrived, own, ohi, coef, idx, first, stiff, scale, right),
                "smooth_first",
            )
            source = right
        else:
            *sent, second = call(
                smooth_kernel,
                MESSAGES + [FIELD],
                (*arrived, ohi, coef, idx, first, stiff, scale, source),
                "smooth",
            )
        arrived = exchange(sent)
        stiff = local(second)
        *sent, row, extra = call(
            restrict_kernel,
            MESSAGES[:2] + [shape(12, BS), FIELD],
            (*arrived, ohi, oht, ohh, coef, idx, nodes, stiff, source),
            "restrict",
        )
        arrived = exchange(sent)
        known = step > 0
        (row,) = call(
            row_kernel,
            [shape(lon, 12 if known else 16, BS)],
            (*arrived, row) + (() if known else (ninv,)),
            "row",
        )
        near, column, *found = call(
            functools.partial(column_kernel, known, lon),
            [shape(20, BS), shape(lat, 12, BS)] + ([] if known else [shape(20, BS)]),
            (everywhere(row, "lon"),) + ((inverses,) if known else ()),
            "column",
        )
        column = everywhere(column, "lat")
        args = (column, near, ohi, oht, ohh, coef, idx, nodes, second, extra, ends, away, value, weights)
        if step == 0:
            (inverses,) = found
            *sent, direction, image, first = call(
                functools.partial(prolong_first_kernel, lat),
                MESSAGES + [FIELD] * 3,
                args + (scale,),
                "prolong_first",
                scratch=scratch,
            )
            source = image
            arrived = exchange(sent)
        else:
            direction, image2, sums = call(
                functools.partial(prolong_last_kernel, lat),
                [FIELD, FIELD, shape(lat, 1, BS)],
                args + (right, image),
                "prolong_last",
                scratch=scratch,
            )
        directions.append(direction)
    sums = jnp.sum(everywhere(sums, "lat"), axis=0, keepdims=True)
    sums = everywhere(jnp.broadcast_to(sums, (lax.axis_size("lon"), 1, BS)), "lon")
    solution, residual, history = call(
        finish_kernel,
        [shape(2, 1, 1, E), shape(2, 1, 1, E), shape(1, BS)],
        (sums, right, image, image2, directions[0], directions[1]),
        "finish",
    )
    return solution, residual, history[0, :ITERS]


def solution(mesh):
    placed = (
        P(None, "lat", "lon", None),
        P("lat", "lon", None),
        P("lat", "lon", None, None, None),
        P("lat", "lon", None, None, None),
        P("lat", "lon", None, None),
        P("lat", "lon", None),
        P("lat", "lon", None, None),
        P("lat", "lon", None, None),
    )
    return jax.shard_map(
        on_device,
        mesh=mesh,
        in_specs=placed,
        out_specs=(P(None, "lat", "lon", None), P(None, "lat", "lon", None), P()),
        check_vma=False,
    )
```

```python
import functools

import jax
import jax.numpy as jnp
from jax import lax
from jax.experimental import pallas as pl
from jax.experimental.pallas import tpu as pltpu
from jax.sharding import PartitionSpec as P

ITERS = 2
EB = 16
BS = 128
E = EB * BS
ND = 256
IFC = 256
OMEGA = 0.8
F32 = jnp.float32
BF16 = jnp.bfloat16
LIMIT = 20 * 1024 * 1024
BEGIN_LIMIT = 60 * 1024 * 1024
NT = (((1,), (1,)), ((), ()))


def complex_times(a, b):
    return a[0] * b[0] - a[1] * b[1], a[0] * b[1] + a[1] * b[0]


def complex_inverse(a):
    scale = a[0] * a[0] + a[1] * a[1]
    return a[0] / scale, -a[1] / scale


def pieces(x):
    first = x.astype(BF16).astype(F32)
    rest = x - first
    second = rest.astype(BF16).astype(F32)
    return first, second, rest - second


def lanes(x, count):
    return jnp.concatenate([x[k : k + 1] for k in range(count)], axis=1)


def to_blocks(row, ref):
    for k in range(EB):
        ref[k : k + 1] = row[:, k * BS : (k + 1) * BS]
    return ref[...]


def block_mask(blocks, rows):
    return lax.broadcasted_iota(jnp.int32, (rows, blocks.shape[1]), 0) == blocks


def lane_onehot(index):
    spot = lax.broadcasted_iota(jnp.int32, (BS, index.shape[1]), 0)
    return jnp.where(spot == index % BS, 1.0, 0.0).astype(BF16)


def take(field, onehot, mask):
    parts = [pieces(part) for part in field]
    stack = jnp.concatenate([parts[c][p] for p in range(3) for c in range(2)], axis=0)
    got = jnp.dot(stack.astype(BF16), onehot[...], preferred_element_type=F32)
    got = got[:32] + got[32:64] + got[64:]
    return [
        jnp.sum(jnp.where(mask, got[16 * c : 16 * c + 16], 0.0), axis=0, keepdims=True)
        for c in range(2)
    ]


def put(rows, onehot, mask):
    parts = [pieces(part) for part in rows]
    stack = jnp.concatenate(
        [jnp.where(mask, parts[c][p], 0.0) for p in range(3) for c in range(2)], axis=0
    )
    got = lax.dot_general(stack.astype(BF16), onehot[...], NT, preferred_element_type=F32)
    got = got[:32] + got[32:64] + got[64:]
    return got[:16], got[16:]


def put_heads(rows, onehot, block):
    spot = lax.broadcasted_iota(jnp.int32, (8, block.shape[1]), 0)
    right = [pieces(part) for part in rows]
    match = (spot % 2 == block) & (spot < 4)
    stack = jnp.concatenate(
        [
            jnp.where(match, jnp.where(spot < 2, right[0][p], right[1][p]), 0.0)
            for p in range(3)
        ],
        axis=0,
    )
    got = lax.dot_general(stack.astype(BF16), onehot[...], NT, preferred_element_type=F32)
    return got[:8] + got[8:16] + got[16:]


def take_heads(own, onehot, block):
    stack = jnp.concatenate(pieces(own), axis=0)
    got = jnp.dot(stack.astype(BF16), onehot[...], preferred_element_type=F32)
    got = got[:8] + got[8:16] + got[16:]
    low = block == 0
    return [jnp.where(low, got[2 * c : 2 * c + 1], got[2 * c + 1 : 2 * c + 2]) for c in range(2)]


def parities():
    return lax.axis_index("lat") % 2 == 0, lax.axis_index("lon") % 2 == 0


def hand_out(refs, towards, at=0):
    even_lat, even_lon = parities()
    refs[0][at : at + 4] = jnp.where(even_lon, towards[2], towards[3])
    refs[1][at : at + 4] = jnp.where(even_lon, towards[3], towards[2])
    refs[2][at : at + 4] = jnp.where(even_lat, towards[0], towards[1])
    refs[3][at : at + 4] = jnp.where(even_lat, towards[1], towards[0])


def collect(refs, at=0):
    even_lat, even_lon = parities()
    wide, near, far, core = [ref[at : at + 4] for ref in refs]
    return (
        jnp.where(even_lat, far, core),
        jnp.where(even_lat, core, far),
        jnp.where(even_lon, wide, near),
        jnp.where(even_lon, near, wide),
    )


def index_rows(idx_ref):
    idx = idx_ref[0, 0]
    return jnp.concatenate([idx[d : d + 1] for d in range(4)], axis=1)


def interface_messages(field, onehot, index):
    got = take(field, onehot, block_mask(index // BS, EB))
    return [
        jnp.concatenate(
            [
                got[c][:, d * IFC + h * BS : d * IFC + (h + 1) * BS]
                for c in range(2)
                for h in range(2)
            ],
            axis=0,
        )
        for d in range(4)
    ]


def interface_sum(arrived, coefs, onehot, index):
    rows = [
        jnp.concatenate(
            [arrived[d][2 * c + h : 2 * c + h + 1] for d in range(4) for h in range(2)], axis=1
        )
        * coefs
        for c in range(2)
    ]
    return put(rows, onehot, block_mask(index // BS, EB))


def pair(ref):
    return ref[0:EB], ref[EB : 2 * EB]


def keep(ref, value):
    ref[0:EB] = value[0]
    ref[EB : 2 * EB] = value[1]


def nodal(rows, onehot_head, onehot_tail, nodes_ref, sign):
    tails = nodes_ref[0, 0, 0:1]
    heads = nodes_ref[0, 0, 1:2]
    own = put_heads(rows, onehot_head, heads // BS)
    ext = put(rows, onehot_tail, block_mask(tails // BS, EB))
    parts = [
        sign * jnp.concatenate([ext[0][2 * d : 2 * d + 2], ext[1][2 * d : 2 * d + 2]], axis=0)
        for d in range(5)
    ]
    return own[0:4] + parts[0], parts[1:]


def begin_kernel(
    rhs_ref, cond_ref, diag_ref, idx_ref, cnt_ref, coup_ref, nodes_ref,
    m0, m1, m2, m3, coef_ref, value_ref, scale_ref, right_ref, first_ref, own_ref,
    ohi_ref, oht_ref, ohh_ref, blocks, rhs_got, cond_got, diag_got, idx_got, cnt_got, coup_got, nodes_got, sems,
):
    messages = (m0, m1, m2, m3)
    pairs = (
        (nodes_ref, nodes_got), (idx_ref, idx_got), (cnt_ref, cnt_got), (coup_ref, coup_got),
        (cond_ref, cond_got), (rhs_ref, rhs_got), (diag_ref, diag_got),
    )
    copies = [pltpu.make_async_copy(here, there, sems.at[k]) for k, (here, there) in enumerate(pairs)]
    for copy in copies:
        copy.start()
    for copy in copies[:2]:
        copy.wait()
    nodes_ref, idx_ref, cnt_ref, coup_ref, cond_ref, rhs_ref, diag_ref = [there for _, there in pairs]
    index = index_rows(idx_ref)
    ohi_ref[...] = lane_onehot(index)
    oht_ref[...] = lane_onehot(nodes_ref[0, 0, 0:1])
    ohh_ref[...] = lane_onehot(nodes_ref[0, 0, 1:2])
    for copy in copies[2:]:
        copy.wait()
    slot = lax.broadcasted_iota(jnp.int32, (1, IFC), 1)
    coef_ref[...] = jnp.concatenate(
        [jnp.where(slot < cnt_ref[0, 0, d], coup_ref[0, 0, d : d + 1], 0.0) for d in range(4)], axis=1
    )
    eye = lax.broadcasted_iota(jnp.int32, (BS, BS), 0) == lax.broadcasted_iota(jnp.int32, (BS, BS), 1)
    for b in range(EB):
        value_ref[b : b + 1] = jnp.sum(jnp.where(eye, diag_ref[0, 0, b], 0.0), axis=0, keepdims=True)
    value_ref[EB : 2 * EB] = to_blocks(cond_ref[0], blocks)
    value = pair(value_ref)
    inverse = complex_inverse(value)
    scale = (OMEGA * inverse[0], OMEGA * inverse[1])
    keep(scale_ref, scale)
    for c in range(2):
        right_ref[EB * c : EB * c + EB] = to_blocks(rhs_ref[c, 0], blocks)
    first = complex_times(scale, pair(right_ref))
    keep(first_ref, first)
    hand_out(messages, interface_messages(first, ohi_ref, index), 0)
    rows = [lanes(value[c], EB) for c in range(2)]
    own, towards = nodal(rows, ohh_ref, oht_ref, nodes_ref, 1.0)
    own_ref[0:4] = own
    hand_out(messages, towards, 4)
    ends = [to_blocks(nodes_ref[0, 0, k : k + 1].astype(F32), blocks) for k in (1, 0)]
    hand_out(messages, interface_messages(ends, ohi_ref, index), 8)


def weight_kernel(diag_ref, off_ref, idx_ref, nodes_ref, w_ref, ohi_ref, oht_ref, ohh_ref):
    ohi_ref[...] = lane_onehot(index_rows(idx_ref))
    oht_ref[...] = lane_onehot(nodes_ref[0, 0, 0:1])
    ohh_ref[...] = lane_onehot(nodes_ref[0, 0, 1:2])
    eye = lax.broadcasted_iota(jnp.int32, (BS, BS), 0) == lax.broadcasted_iota(jnp.int32, (BS, BS), 1)

    def store(b, at, block):
        high = block.astype(BF16)
        w_ref[b, at : at + BS, 0:BS] = high
        w_ref[b, at : at + BS, BS:] = (block - high.astype(F32)).astype(BF16)

    zero = jnp.zeros((BS, 2 * BS), BF16)
    w_ref[0, 0:BS] = zero
    w_ref[EB - 1, 2 * BS :] = zero
    for b in range(EB):
        store(b, BS, jnp.where(eye, 0.0, diag_ref[0, 0, b]))
        if b < EB - 1:
            off = off_ref[0, 0, b]
            store(b + 1, 0, off)
            store(b, 2 * BS, off.T)


def stiffness(field, value, w_ref, wide, out):
    wide[0:8] = jnp.zeros((8, BS), F32)
    wide[8 * (EB + 1) :] = jnp.zeros((8, BS), F32)
    for c in range(2):
        for p, piece in enumerate(pieces(field[c])):
            wide[pl.ds(8 + 2 * p + c, EB, stride=8)] = piece
    for k in (6, 7):
        wide[pl.ds(8 + k, EB, stride=8)] = jnp.zeros((EB, BS), F32)
    for b in range(EB):
        around = jnp.concatenate([wide[8 * (b + k) : 8 * (b + k) + 8] for k in range(3)], axis=1)
        got = jnp.dot(around.astype(BF16), w_ref[b], preferred_element_type=F32)
        out[8 * b : 8 * b + 8] = got[:, :BS] + got[:, BS:]
    sums = [
        out[pl.ds(c, EB, stride=8)] + out[pl.ds(2 + c, EB, stride=8)] + out[pl.ds(4 + c, EB, stride=8)]
        for c in range(2)
    ]
    turned = complex_times(value, field)
    return sums[0] + turned[0], sums[1] + turned[1]


def local_kernel(field_ref, value_ref, w_ref, out_ref, wide, out):
    keep(out_ref, stiffness(pair(field_ref), pair(value_ref), w_ref, wide, out))


def smooth(arrived, ohi_ref, coef_ref, idx_ref, first_ref, local_ref, scale_ref, right_ref, m, second_ref):
    index = index_rows(idx_ref)
    extra = interface_sum(arrived, coef_ref[...], ohi_ref, index)
    first, local, right = pair(first_ref), pair(local_ref), pair(right_ref)
    change = complex_times(pair(scale_ref), [right[c] - local[c] - extra[c] for c in range(2)])
    second = (first[0] + change[0], first[1] + change[1])
    keep(second_ref, second)
    hand_out(m, interface_messages(second, ohi_ref, index))


def smooth_first_kernel(
    a0, a1, a2, a3, own_ref, ohi_ref, coef_ref, idx_ref, first_ref, local_ref, scale_ref, right_ref,
    m0, m1, m2, m3, second_ref, ninv_ref, ends_ref, oha_ref,
):
    arrived = collect((a0, a1, a2, a3))
    smooth(arrived, ohi_ref, coef_ref, idx_ref, first_ref, local_ref, scale_ref, right_ref, (m0, m1, m2, m3), second_ref)
    sums = own_ref[0:4]
    for part in collect((a0, a1, a2, a3), 4):
        sums = sums + part
    inverse = complex_inverse((sums[0:2], sums[2:4]))
    ninv_ref[0:2] = inverse[0]
    ninv_ref[2:4] = inverse[1]
    for d, part in enumerate(collect((a0, a1, a2, a3), 8)):
        for k in range(2):
            row = jnp.concatenate([part[2 * k : 2 * k + 1], part[2 * k + 1 : 2 * k + 2]], axis=1)
            row = row.astype(jnp.int32)
            at = (2 * d + k) * IFC
            ends_ref[:, at : at + IFC] = row
            oha_ref[:, at : at + IFC] = lane_onehot(row)


def smooth_kernel(
    a0, a1, a2, a3, ohi_ref, coef_ref, idx_ref, first_ref, local_ref, scale_ref, right_ref,
    m0, m1, m2, m3, second_ref,
):
    arrived = collect((a0, a1, a2, a3))
    smooth(arrived, ohi_ref, coef_ref, idx_ref, first_ref, local_ref, scale_ref, right_ref, (m0, m1, m2, m3), second_ref)


def restrict_kernel(
    a0, a1, a2, a3, ohi_ref, oht_ref, ohh_ref, coef_ref, idx_ref, nodes_ref, local_ref, right_ref,
    far_ref, core_ref, row_ref, extra_ref,
):
    index = index_rows(idx_ref)
    extra = interface_sum(collect((a0, a1, a2, a3)), coef_ref[...], ohi_ref, index)
    keep(extra_ref, extra)
    local, right = pair(local_ref), pair(right_ref)
    rows = [lanes(right[c] - local[c] - extra[c], EB) for c in range(2)]
    own, towards = nodal(rows, ohh_ref, oht_ref, nodes_ref, -1.0)
    even_lat, _ = parities()
    far_ref[...] = jnp.where(even_lat, towards[0], towards[1])
    core_ref[...] = jnp.where(even_lat, towards[1], towards[0])
    for k, part in enumerate((own, towards[2], towards[3])):
        row_ref[k] = part


def row_kernel(far_ref, core_ref, row_ref, *refs):
    out_ref = refs[-1]
    even_lat, _ = parities()
    core = jnp.where(even_lat, core_ref[1], core_ref[0])
    parts = [row_ref[0] + far_ref[...] + core, row_ref[1], row_ref[2]]
    parts += [ref[...] for ref in refs[:-1]]
    for k, part in enumerate(parts):
        out_ref[:, k] = jnp.broadcast_to(part[None], (out_ref.shape[0], 4, BS))


def column_kernel(known, lon, row_ref, *refs):
    inverse_ref, near_ref, out_ref = refs if known else (refs[2], refs[0], refs[1])
    me = lax.axis_index("lon")

    def at(step):
        return lax.rem(me + (lon + step), lon)

    for k in range(5):
        sums = row_ref[at(k - 2), 0] + row_ref[at(k - 1), 1] + row_ref[at(k - 3), 2]
        if not known:
            inverse_ref[k] = row_ref[at(k - 2), 3]
        inverse = inverse_ref[k]
        result = complex_times((inverse[0:2], inverse[2:4]), (sums[0:2], sums[2:4]))
        near_ref[k] = jnp.concatenate(result, axis=0)
    for k in range(3):
        out_ref[k] = near_ref[k + 1]


def extend(nodes, ref):
    for d in range(5):
        for c in range(2):
            ref[EB * c + 2 * d : EB * c + 2 * d + 2] = nodes[d][2 * c : 2 * c + 2]
    return pair(ref)


def gradient(nodes, ref, onehot_head, onehot_tail, heads, tails):
    low = take(extend(nodes, ref), onehot_tail, block_mask(tails // BS, EB))
    high = take_heads(jnp.concatenate([nodes[0], nodes[0]], axis=0), onehot_head, heads // BS)
    return [high[c] - low[c] for c in range(2)]


def prolong(
    lat, chip_ref, away_ref, near_ref, ohi_ref, oht_ref, ohh_ref, coef_ref, idx_ref, nodes_ref, second_ref, extra_ref,
    ends_ref, oha_ref, value_ref, w_ref, direction_ref, blocks, ext, wide, out, column,
):
    me = lax.axis_index("lat")

    for k in range(2):
        column[k] = away_ref[0, 3 * k : 3 * k + 3]
        column[2 + k] = chip_ref[k]
        column[4 + k] = away_ref[1, 3 * k : 3 * k + 3]
    here = 2 + me % 2

    def node(down, right):
        if down == 0:
            return near_ref[right + 2]
        return column[here + down, right + 1]

    def around(down, right):
        steps = ((0, 0), (-1, 0), (1, 0), (0, -1), (0, 1))
        return [node(down + i, right + j) for i, j in steps]

    ext[...] = jnp.zeros((2 * EB, BS), F32)
    rise = gradient(around(0, 0), ext, ohh_ref, oht_ref, nodes_ref[0, 0, 1:2], nodes_ref[0, 0, 0:1])
    second = pair(second_ref)
    direction = [second[c] + to_blocks(rise[c], blocks) for c in range(2)]
    keep(direction_ref, direction)
    rises = []
    for d, step in enumerate(((-1, 0), (1, 0), (0, -1), (0, 1))):
        spots = [pl.ds((2 * d + k) * IFC, IFC) for k in range(2)]
        rise = gradient(
            around(*step), ext, oha_ref.at[:, spots[0]], oha_ref.at[:, spots[1]],
            ends_ref[:, spots[0]], ends_ref[:, spots[1]],
        )
        if d < 2:
            there = me + step[0]
            real = (there >= 0) & (there < lat)
            rise = [jnp.where(real, part, 0.0) for part in rise]
        rises.append(rise)
    rows = [jnp.concatenate([rise[c] for rise in rises], axis=1) * coef_ref[...] for c in range(2)]
    more = put(rows, ohi_ref, block_mask(index_rows(idx_ref) // BS, EB))
    extra = pair(extra_ref)
    local = stiffness(direction, pair(value_ref), w_ref, wide, out)
    return [local[c] + extra[c] + more[c] for c in range(2)]


def prolong_first_kernel(
    lat, chip_ref, away_ref, near_ref, ohi_ref, oht_ref, ohh_ref, coef_ref, idx_ref, nodes_ref, second_ref, extra_ref,
    ends_ref, oha_ref, value_ref, w_ref, scale_ref,
    m0, m1, m2, m3, direction_ref, image_ref, first_ref,
    *scratch,
):
    image = prolong(
        lat, chip_ref, away_ref, near_ref, ohi_ref, oht_ref, ohh_ref, coef_ref, idx_ref, nodes_ref, second_ref, extra_ref,
        ends_ref, oha_ref, value_ref, w_ref, direction_ref, *scratch,
    )
    keep(image_ref, image)
    first = complex_times(pair(scale_ref), image)
    keep(first_ref, first)
    hand_out((m0, m1, m2, m3), interface_messages(first, ohi_ref, index_rows(idx_ref)))


def total(x):
    return jnp.sum(jnp.sum(x, axis=0, keepdims=True), axis=1, keepdims=True)


def inner(a, b):
    return total(a[0] * b[0] + a[1] * b[1]), total(a[0] * b[1] - a[1] * b[0])


def prolong_last_kernel(
    lat, chip_ref, away_ref, near_ref, ohi_ref, oht_ref, ohh_ref, coef_ref, idx_ref, nodes_ref, second_ref, extra_ref,
    ends_ref, oha_ref, value_ref, w_ref, right_ref, image_ref,
    direction_ref, image2_ref, sums_ref,
    *scratch,
):
    image2 = prolong(
        lat, chip_ref, away_ref, near_ref, ohi_ref, oht_ref, ohh_ref, coef_ref, idx_ref, nodes_ref, second_ref, extra_ref,
        ends_ref, oha_ref, value_ref, w_ref, direction_ref, *scratch,
    )
    right, image = pair(right_ref), pair(image_ref)
    keep(image2_ref, image2)
    rest = (right[0] - image[0], right[1] - image[1])
    turn = (image[0] - image2[0], image[1] - image2[1])
    found = [inner(right, right)[0], inner(image, image)[0], inner(rest, rest)[0], inner(turn, turn)[0]]
    found += [*inner(image, rest), *inner(turn, rest), *inner(turn, image)]
    lane = lax.broadcasted_iota(jnp.int32, (1, BS), 1)
    row = jnp.zeros((1, BS), F32)
    for k, value in enumerate(found):
        row = jnp.where(lane == k, value, row)
    sums_ref[...] = jnp.broadcast_to(row[None], sums_ref.shape)


def finish_kernel(
    sums_ref, right_ref, image_ref, image2_ref, direction_ref, direction2_ref,
    solution_ref, residual_ref, history_ref,
):
    row = jnp.sum(sums_ref[...], axis=0)
    lane = lax.broadcasted_iota(jnp.int32, (1, BS), 1)
    found = [jnp.sum(jnp.where(lane == k, row, 0.0), axis=1, keepdims=True) for k in range(10)]
    start, ww, rr, tt = found[:4]
    wr, tr, tw = found[4:6], found[6:8], found[8:10]
    extra = (wr[0] / ww, wr[1] / ww)
    alpha = (1.0 + extra[0], extra[1])
    fresh = rr - (wr[0] * extra[0] + wr[1] * extra[1])
    moved = complex_times(extra, tw)
    c2 = complex_times((alpha[0], -alpha[1]), (tr[0] - moved[0], tr[1] - moved[1]))
    cross = complex_times(complex_times((extra[0], -extra[1]), alpha), (tw[0], -tw[1]))
    ww2 = (alpha[0] * alpha[0] + alpha[1] * alpha[1]) * tt
    ww2 = ww2 + (extra[0] * extra[0] + extra[1] * extra[1]) * ww - 2.0 * cross[0]
    alpha2 = (c2[0] / ww2, c2[1] / ww2)
    fresh2 = fresh - (c2[0] * alpha2[0] + c2[1] * alpha2[1])
    history_ref[...] = jnp.where(lane == 0, fresh / start, fresh2 / start)
    right, image, image2 = pair(right_ref), pair(image_ref), pair(image2_ref)
    direction, direction2 = pair(direction_ref), pair(direction2_ref)
    step = complex_times(alpha, direction)
    other = complex_times(alpha, direction2)
    step2 = complex_times(alpha2, (direction[0] - other[0], direction[1] - other[1]))
    away = complex_times(extra, image)
    other = complex_times(alpha, image2)
    away2 = complex_times(alpha2, (image[0] - other[0], image[1] - other[1]))
    for c in range(2):
        solution_ref[c, 0] = lanes(step[c] + step2[c], EB)
        residual_ref[c, 0] = lanes(right[c] - image[c] - away[c] - away2[c], EB)


def shape(*dims, dtype=F32):
    return jax.ShapeDtypeStruct(dims, dtype)


FIELD = shape(2 * EB, BS)
MESSAGES = [shape(4, BS)] * 4


def call(body, outs, args, name, scratch=(), space=pltpu.VMEM, limit=LIMIT, flops=0):
    specs = [pl.BlockSpec(memory_space=space)] * len(args)
    moved = sum(a.size * a.dtype.itemsize for a in args)
    return pl.pallas_call(
        body,
        out_shape=outs,
        in_specs=specs,
        out_specs=[pl.BlockSpec(memory_space=pltpu.VMEM)] * len(outs),
        scratch_shapes=scratch,
        compiler_params=pltpu.CompilerParams(vmem_limit_bytes=limit),
        cost_estimate=pl.CostEstimate(flops=flops, bytes_accessed=moved, transcendentals=0),
        name=name,
    )(*args)


def swap(pairs):
    return [(a, b) for a, b in pairs] + [(b, a) for a, b in pairs]


def lat_pairs(first):
    return [(k, k + 1) for k in range(first, lax.axis_size("lat") - 1, 2)]


def swap_far(message):
    return lax.ppermute(message, "lat", swap(lat_pairs(1)))


def on_chip(message):
    return lax.all_gather(message, "lat", axis_index_groups=lat_pairs(0))


def exchange(messages):
    lon = lax.axis_size("lon")
    return [
        lax.ppermute(messages[0], "lon", swap([(k, (k + 1) % lon) for k in range(1, lon, 2)])),
        lax.ppermute(messages[1], "lon", swap([(k, k + 1) for k in range(0, lon, 2)])),
        swap_far(messages[2]),
        lax.ppermute(messages[3], "lat", swap(lat_pairs(0))),
    ]


def everywhere(row, axis):
    return lax.all_to_all(row, axis, 0, 0)


def on_device(rhs, cond, blk_diag, blk_off, idx, cnt, coup, nodes):
    blocks = pltpu.VMEM((EB, BS), F32)
    wide = pltpu.VMEM((8 * (EB + 2), BS), F32)
    out = pltpu.VMEM((8 * EB, BS), F32)
    onehots = [(BS, 4 * IFC), (BS, E), (BS, E)]
    *sent, coef, value, scale, right, first, own = call(
        begin_kernel,
        [shape(12, BS)] * 4 + [shape(1, 4 * IFC)] + [FIELD] * 4 + [shape(4, BS)],
        (rhs, cond, blk_diag, idx, cnt, coup, nodes),
        "begin",
        scratch=[pltpu.VMEM(dims, BF16) for dims in onehots]
        + [blocks]
        + [pltpu.VMEM(part.shape, part.dtype) for part in (rhs, cond, blk_diag, idx)]
        + [pltpu.SMEM(cnt.shape, cnt.dtype)]
        + [pltpu.VMEM(part.shape, part.dtype) for part in (coup, nodes)]
        + [pltpu.SemaphoreType.DMA((7,))],
        space=pltpu.HBM,
        limit=BEGIN_LIMIT,
    )
    arrived = exchange(sent)
    weights, ohi, oht, ohh = call(
        weight_kernel,
        [shape(EB, 3 * BS, 2 * BS, dtype=BF16)] + [shape(*dims, dtype=BF16) for dims in onehots],
        (blk_diag, blk_off, idx, nodes),
        "weights",
        flops=10**7,
    )

    def local(field):
        return call(
            local_kernel, [FIELD], (field, value, weights), "local", scratch=[wide, out], flops=2 * 8 * EB * 3 * BS * 2 * BS
        )[0]

    lat, lon = lax.axis_size("lat"), lax.axis_size("lon")
    scratch = [blocks, pltpu.VMEM((2 * EB, BS), F32), wide, out, pltpu.VMEM((6, 3, 4, BS), F32)]
    directions = []
    for step in range(ITERS):
        stiff = local(first)
        if step == 0:
            *sent, second, ninv, ends, oha = call(
                smooth_first_kernel,
                MESSAGES + [FIELD, shape(4, BS), shape(1, 8 * IFC, dtype=jnp.int32), shape(BS, 8 * IFC, dtype=BF16)],
                (*arrived, own, ohi, coef, idx, first, stiff, scale, right),
                "smooth_first",
            )
            source = right
        else:
            *sent, second = call(
                smooth_kernel,
                MESSAGES + [FIELD],
                (*arrived, ohi, coef, idx, first, stiff, scale, source),
                "smooth",
            )
        arrived = exchange(sent)
        stiff = local(second)
        far, core, row, extra = call(
            restrict_kernel,
            MESSAGES[:2] + [shape(3, 4, BS), FIELD],
            (*arrived, ohi, oht, ohh, coef, idx, nodes, stiff, source),
            "restrict",
        )
        known = step > 0
        (row,) = call(
            row_kernel,
            [shape(lon, 3 if known else 4, 4, BS)],
            (swap_far(far), on_chip(core), row) + (() if known else (ninv,)),
            "row",
        )
        near, column, *found = call(
            functools.partial(column_kernel, known, lon),
            [shape(5, 4, BS), shape(3, 4, BS)] + ([] if known else [shape(5, 4, BS)]),
            (everywhere(row, "lon"),) + ((inverses,) if known else ()),
            "column",
        )
        chip = on_chip(column)
        away = on_chip(swap_far(chip.reshape(6, 4, BS)))
        args = (chip, away, near, ohi, oht, ohh, coef, idx, nodes, second, extra, ends, oha, value, weights)
        if step == 0:
            (inverses,) = found
            *sent, direction, image, first = call(
                functools.partial(prolong_first_kernel, lat),
                MESSAGES + [FIELD] * 3,
                args + (scale,),
                "prolong_first",
                scratch=scratch,
            )
            source = image
            arrived = exchange(sent)
        else:
            direction, image2, sums = call(
                functools.partial(prolong_last_kernel, lat),
                [FIELD, FIELD, shape(lat, 1, BS)],
                args + (right, image),
                "prolong_last",
                scratch=scratch,
            )
        directions.append(direction)
    sums = jnp.sum(everywhere(sums, "lat"), axis=0, keepdims=True)
    sums = everywhere(jnp.broadcast_to(sums, (lax.axis_size("lon"), 1, BS)), "lon")
    solution, residual, history = call(
        finish_kernel,
        [shape(2, 1, 1, E), shape(2, 1, 1, E), shape(1, BS)],
        (sums, right, image, image2, directions[0], directions[1]),
        "finish",
    )
    return solution, residual, history[0, :ITERS]


def solution(mesh):
    placed = (
        P(None, "lat", "lon", None),
        P("lat", "lon", None),
        P("lat", "lon", None, None, None),
        P("lat", "lon", None, None, None),
        P("lat", "lon", None, None),
        P("lat", "lon", None),
        P("lat", "lon", None, None),
        P("lat", "lon", None, None),
    )
    return jax.shard_map(
        on_device,
        mesh=mesh,
        in_specs=placed,
        out_specs=(P(None, "lat", "lon", None), P(None, "lat", "lon", None), P()),
        check_vma=False,
    )
```

```python
import functools

import jax
import jax.numpy as jnp
from jax import lax
from jax.experimental import pallas as pl
from jax.experimental.pallas import tpu as pltpu
from jax.sharding import PartitionSpec as P

ITERS = 2
EB = 16
BS = 128
E = EB * BS
ND = 256
IFC = 256
OMEGA = 0.8
F32 = jnp.float32
BF16 = jnp.bfloat16
LIMIT = 20 * 1024 * 1024
PACK_LIMIT = 60 * 1024 * 1024
RIGHT, COND, COEF, INDEX, TAILS, HEADS, PACKED = 0, 32, 48, 56, 64, 80, 96
NT = (((1,), (1,)), ((), ()))


def complex_times(a, b):
    return a[0] * b[0] - a[1] * b[1], a[0] * b[1] + a[1] * b[0]


def complex_inverse(a):
    scale = a[0] * a[0] + a[1] * a[1]
    return a[0] / scale, -a[1] / scale


def pieces(x):
    first = x.astype(BF16).astype(F32)
    rest = x - first
    second = rest.astype(BF16).astype(F32)
    return first, second, rest - second


def split(block):
    high = block.astype(BF16)
    return jnp.concatenate([high, (block - high.astype(F32)).astype(BF16)], axis=1)


def lanes(x, count):
    return jnp.concatenate([x[k : k + 1] for k in range(count)], axis=1)


def to_blocks(row, ref):
    for k in range(EB):
        ref[k : k + 1] = row[:, k * BS : (k + 1) * BS]
    return ref[...]


def block_mask(blocks, rows):
    return lax.broadcasted_iota(jnp.int32, (rows, blocks.shape[1]), 0) == blocks


def lane_onehot(index):
    spot = lax.broadcasted_iota(jnp.int32, (BS, index.shape[1]), 0)
    return jnp.where(spot == index % BS, 1.0, 0.0).astype(BF16)


def take(field, onehot, mask):
    parts = [pieces(part) for part in field]
    stack = jnp.concatenate([parts[c][p] for p in range(3) for c in range(2)], axis=0)
    got = jnp.dot(stack.astype(BF16), onehot[...], preferred_element_type=F32)
    got = got[:32] + got[32:64] + got[64:]
    return [
        jnp.sum(jnp.where(mask, got[16 * c : 16 * c + 16], 0.0), axis=0, keepdims=True)
        for c in range(2)
    ]


def put(rows, onehot, mask):
    parts = [pieces(part) for part in rows]
    stack = jnp.concatenate(
        [jnp.where(mask, parts[c][p], 0.0) for p in range(3) for c in range(2)], axis=0
    )
    got = lax.dot_general(stack.astype(BF16), onehot[...], NT, preferred_element_type=F32)
    got = got[:32] + got[32:64] + got[64:]
    return got[:16], got[16:]


def put_heads(rows, onehot, block):
    spot = lax.broadcasted_iota(jnp.int32, (8, block.shape[1]), 0)
    right = [pieces(part) for part in rows]
    match = (spot % 2 == block) & (spot < 4)
    stack = jnp.concatenate(
        [
            jnp.where(match, jnp.where(spot < 2, right[0][p], right[1][p]), 0.0)
            for p in range(3)
        ],
        axis=0,
    )
    got = lax.dot_general(stack.astype(BF16), onehot[...], NT, preferred_element_type=F32)
    return got[:8] + got[8:16] + got[16:]


def take_heads(own, onehot, block):
    stack = jnp.concatenate(pieces(own), axis=0)
    got = jnp.dot(stack.astype(BF16), onehot[...], preferred_element_type=F32)
    got = got[:8] + got[8:16] + got[16:]
    low = block == 0
    return [jnp.where(low, got[2 * c : 2 * c + 1], got[2 * c + 1 : 2 * c + 2]) for c in range(2)]


def parities():
    return lax.axis_index("lat") % 2 == 0, lax.axis_index("lon") % 2 == 0


def hand_out(refs, towards, at=0):
    even_lat, even_lon = parities()
    refs[0][at : at + 4] = jnp.where(even_lon, towards[2], towards[3])
    refs[1][at : at + 4] = jnp.where(even_lon, towards[3], towards[2])
    refs[2][at : at + 4] = jnp.where(even_lat, towards[0], towards[1])
    refs[3][at : at + 4] = jnp.where(even_lat, towards[1], towards[0])


def collect(refs, at=0):
    even_lat, even_lon = parities()
    wide, near, far, core = [ref[at : at + 4] for ref in refs]
    return (
        jnp.where(even_lat, far, core),
        jnp.where(even_lat, core, far),
        jnp.where(even_lon, wide, near),
        jnp.where(even_lon, near, wide),
    )


def index_rows(pack_ref):
    return lanes(pack_ref[INDEX : INDEX + 8], 8).astype(jnp.int32)


def ends_rows(pack_ref):
    return [lanes(pack_ref[at : at + EB], EB).astype(jnp.int32) for at in (TAILS, HEADS)]


def coef_row(pack_ref):
    return lanes(pack_ref[COEF : COEF + 8], 8)


def interface_messages(field, onehot, index):
    got = take(field, onehot, block_mask(index // BS, EB))
    return [
        jnp.concatenate(
            [
                got[c][:, d * IFC + h * BS : d * IFC + (h + 1) * BS]
                for c in range(2)
                for h in range(2)
            ],
            axis=0,
        )
        for d in range(4)
    ]


def interface_sum(arrived, coefs, onehot, index):
    rows = [
        jnp.concatenate(
            [arrived[d][2 * c + h : 2 * c + h + 1] for d in range(4) for h in range(2)], axis=1
        )
        * coefs
        for c in range(2)
    ]
    return put(rows, onehot, block_mask(index // BS, EB))


def pair(ref, at=0):
    return ref[at : at + EB], ref[at + EB : at + 2 * EB]


def keep(ref, value):
    ref[0:EB] = value[0]
    ref[EB : 2 * EB] = value[1]


def nodal(rows, onehot_head, onehot_tail, pack_ref, sign):
    tails, heads = ends_rows(pack_ref)
    own = put_heads(rows, onehot_head, heads // BS)
    ext = put(rows, onehot_tail, block_mask(tails // BS, EB))
    parts = [
        sign * jnp.concatenate([ext[0][2 * d : 2 * d + 2], ext[1][2 * d : 2 * d + 2]], axis=0)
        for d in range(5)
    ]
    return own[0:4] + parts[0], parts[1:]


def pack_kernel(
    rhs_ref, cond_ref, coup_ref, cnt_ref, idx_ref, nodes_ref, pack_ref,
    rhs_got, cond_got, coup_got, cnt_got, idx_got, nodes_got, sems,
):
    pairs = (
        (rhs_ref, rhs_got), (cond_ref, cond_got), (coup_ref, coup_got),
        (cnt_ref, cnt_got), (idx_ref, idx_got), (nodes_ref, nodes_got),
    )
    copies = [pltpu.make_async_copy(here, there, sems.at[k]) for k, (here, there) in enumerate(pairs)]
    for copy in copies:
        copy.start()
    for copy in copies:
        copy.wait()

    def rows(at, row):
        for k in range(row.shape[1] // BS):
            pack_ref[at + k : at + k + 1] = row[:, k * BS : (k + 1) * BS]

    for c in range(2):
        rows(RIGHT + EB * c, rhs_got[c, 0])
        rows((TAILS, HEADS)[c], nodes_got[0, 0, c : c + 1].astype(F32))
    rows(COND, cond_got[0])
    slot = lax.broadcasted_iota(jnp.int32, (1, IFC), 1)
    for d in range(4):
        rows(COEF + 2 * d, jnp.where(slot < cnt_got[0, 0, d], coup_got[0, 0, d : d + 1], 0.0))
        rows(INDEX + 2 * d, idx_got[0, 0, d : d + 1].astype(F32))


def begin_kernel(
    pack_ref, diag_ref,
    m0, m1, m2, m3, value_ref, scale_ref, first_ref, own_ref,
    ohi_ref, oht_ref, ohh_ref, wd_ref,
):
    messages = (m0, m1, m2, m3)
    index = index_rows(pack_ref)
    tails, heads = ends_rows(pack_ref)
    ohi_ref[...] = lane_onehot(index)
    oht_ref[...] = lane_onehot(tails)
    ohh_ref[...] = lane_onehot(heads)
    eye = lax.broadcasted_iota(jnp.int32, (BS, BS), 0) == lax.broadcasted_iota(jnp.int32, (BS, BS), 1)
    for b in range(EB):
        block = diag_ref[0, 0, b]
        value_ref[b : b + 1] = jnp.sum(jnp.where(eye, block, 0.0), axis=0, keepdims=True)
        wd_ref[b] = split(jnp.where(eye, 0.0, block))
    value_ref[EB : 2 * EB] = pack_ref[COND : COND + EB]
    value = pair(value_ref)
    inverse = complex_inverse(value)
    scale = (OMEGA * inverse[0], OMEGA * inverse[1])
    keep(scale_ref, scale)
    first = complex_times(scale, pair(pack_ref, RIGHT))
    keep(first_ref, first)
    hand_out(messages, interface_messages(first, ohi_ref, index), 0)
    rows = [lanes(value[c], EB) for c in range(2)]
    own, towards = nodal(rows, ohh_ref, oht_ref, pack_ref, 1.0)
    own_ref[0:4] = own
    hand_out(messages, towards, 4)
    ends = [pack_ref[at : at + EB] for at in (HEADS, TAILS)]
    hand_out(messages, interface_messages(ends, ohi_ref, index), 8)


def weight_kernel(off_ref, wo_ref):
    zero = jnp.zeros((BS, 2 * BS), BF16)
    wo_ref[0, 0:BS] = zero
    wo_ref[EB - 1, BS:] = zero
    for b in range(EB - 1):
        off = off_ref[0, 0, b]
        wo_ref[b + 1, 0:BS] = split(off)
        wo_ref[b, BS:] = split(off.T)


def stiffness(field, value, wd_ref, wo_ref, wide, out):
    wide[0:8] = jnp.zeros((8, BS), F32)
    wide[8 * (EB + 1) :] = jnp.zeros((8, BS), F32)
    for c in range(2):
        for p, piece in enumerate(pieces(field[c])):
            wide[pl.ds(8 + 2 * p + c, EB, stride=8)] = piece
    for k in (6, 7):
        wide[pl.ds(8 + k, EB, stride=8)] = jnp.zeros((EB, BS), F32)
    for b in range(EB):
        low, here, high = [wide[8 * (b + k) : 8 * (b + k) + 8] for k in range(3)]
        beside = jnp.concatenate([low, high], axis=1)
        got = jnp.dot(here.astype(BF16), wd_ref[b], preferred_element_type=F32)
        got = got + jnp.dot(beside.astype(BF16), wo_ref[b], preferred_element_type=F32)
        out[8 * b : 8 * b + 8] = got[:, :BS] + got[:, BS:]
    sums = [
        out[pl.ds(c, EB, stride=8)] + out[pl.ds(2 + c, EB, stride=8)] + out[pl.ds(4 + c, EB, stride=8)]
        for c in range(2)
    ]
    turned = complex_times(value, field)
    return sums[0] + turned[0], sums[1] + turned[1]


def local_kernel(field_ref, value_ref, wd_ref, wo_ref, out_ref, wide, out):
    keep(out_ref, stiffness(pair(field_ref), pair(value_ref), wd_ref, wo_ref, wide, out))


def smooth(arrived, ohi_ref, pack_ref, first_ref, local_ref, scale_ref, right_ref, m, second_ref):
    index = index_rows(pack_ref)
    extra = interface_sum(arrived, coef_row(pack_ref), ohi_ref, index)
    first, local, right = pair(first_ref), pair(local_ref), pair(right_ref)
    change = complex_times(pair(scale_ref), [right[c] - local[c] - extra[c] for c in range(2)])
    second = (first[0] + change[0], first[1] + change[1])
    keep(second_ref, second)
    hand_out(m, interface_messages(second, ohi_ref, index))


def smooth_first_kernel(
    a0, a1, a2, a3, own_ref, ohi_ref, pack_ref, first_ref, local_ref, scale_ref,
    m0, m1, m2, m3, second_ref, ninv_ref, ends_ref, oha_ref,
):
    arrived = collect((a0, a1, a2, a3))
    smooth(arrived, ohi_ref, pack_ref, first_ref, local_ref, scale_ref, pack_ref, (m0, m1, m2, m3), second_ref)
    sums = own_ref[0:4]
    for part in collect((a0, a1, a2, a3), 4):
        sums = sums + part
    inverse = complex_inverse((sums[0:2], sums[2:4]))
    ninv_ref[0:2] = inverse[0]
    ninv_ref[2:4] = inverse[1]
    for d, part in enumerate(collect((a0, a1, a2, a3), 8)):
        for k in range(2):
            row = jnp.concatenate([part[2 * k : 2 * k + 1], part[2 * k + 1 : 2 * k + 2]], axis=1)
            row = row.astype(jnp.int32)
            at = (2 * d + k) * IFC
            ends_ref[:, at : at + IFC] = row
            oha_ref[:, at : at + IFC] = lane_onehot(row)


def smooth_kernel(
    a0, a1, a2, a3, ohi_ref, pack_ref, first_ref, local_ref, scale_ref, right_ref,
    m0, m1, m2, m3, second_ref,
):
    arrived = collect((a0, a1, a2, a3))
    smooth(arrived, ohi_ref, pack_ref, first_ref, local_ref, scale_ref, right_ref, (m0, m1, m2, m3), second_ref)


def restrict_kernel(
    a0, a1, a2, a3, ohi_ref, oht_ref, ohh_ref, pack_ref, local_ref, right_ref,
    far_ref, core_ref, row_ref, extra_ref,
):
    index = index_rows(pack_ref)
    extra = interface_sum(collect((a0, a1, a2, a3)), coef_row(pack_ref), ohi_ref, index)
    keep(extra_ref, extra)
    local, right = pair(local_ref), pair(right_ref)
    rows = [lanes(right[c] - local[c] - extra[c], EB) for c in range(2)]
    own, towards = nodal(rows, ohh_ref, oht_ref, pack_ref, -1.0)
    even_lat, _ = parities()
    far_ref[...] = jnp.where(even_lat, towards[0], towards[1])
    core_ref[...] = jnp.where(even_lat, towards[1], towards[0])
    for k, part in enumerate((own, towards[2], towards[3])):
        row_ref[k] = part


def row_kernel(far_ref, core_ref, row_ref, *refs):
    out_ref = refs[-1]
    even_lat, _ = parities()
    core = jnp.where(even_lat, core_ref[1], core_ref[0])
    parts = [row_ref[0] + far_ref[...] + core, row_ref[1], row_ref[2]]
    parts += [ref[...] for ref in refs[:-1]]
    for k, part in enumerate(parts):
        out_ref[:, k] = jnp.broadcast_to(part[None], (out_ref.shape[0], 4, BS))


def column_kernel(known, lon, row_ref, *refs):
    inverse_ref, near_ref, out_ref = refs if known else (refs[2], refs[0], refs[1])
    me = lax.axis_index("lon")

    def at(step):
        return lax.rem(me + (lon + step), lon)

    for k in range(5):
        sums = row_ref[at(k - 2), 0] + row_ref[at(k - 1), 1] + row_ref[at(k - 3), 2]
        if not known:
            inverse_ref[k] = row_ref[at(k - 2), 3]
        inverse = inverse_ref[k]
        result = complex_times((inverse[0:2], inverse[2:4]), (sums[0:2], sums[2:4]))
        near_ref[k] = jnp.concatenate(result, axis=0)
    for k in range(3):
        out_ref[k] = near_ref[k + 1]


def extend(nodes, ref):
    for d in range(5):
        for c in range(2):
            ref[EB * c + 2 * d : EB * c + 2 * d + 2] = nodes[d][2 * c : 2 * c + 2]
    return pair(ref)


def gradient(nodes, ref, onehot_head, onehot_tail, heads, tails):
    low = take(extend(nodes, ref), onehot_tail, block_mask(tails // BS, EB))
    high = take_heads(jnp.concatenate([nodes[0], nodes[0]], axis=0), onehot_head, heads // BS)
    return [high[c] - low[c] for c in range(2)]


def prolong(
    lat, chip_ref, away_ref, near_ref, ohi_ref, oht_ref, ohh_ref, pack_ref, second_ref, extra_ref,
    ends_ref, oha_ref, value_ref, wd_ref, wo_ref, direction_ref, blocks, ext, wide, out, column,
):
    me = lax.axis_index("lat")

    for k in range(2):
        column[k] = away_ref[0, 3 * k : 3 * k + 3]
        column[2 + k] = chip_ref[k]
        column[4 + k] = away_ref[1, 3 * k : 3 * k + 3]
    here = 2 + me % 2

    def node(down, right):
        if down == 0:
            return near_ref[right + 2]
        return column[here + down, right + 1]

    def around(down, right):
        steps = ((0, 0), (-1, 0), (1, 0), (0, -1), (0, 1))
        return [node(down + i, right + j) for i, j in steps]

    ext[...] = jnp.zeros((2 * EB, BS), F32)
    tails, heads = ends_rows(pack_ref)
    rise = gradient(around(0, 0), ext, ohh_ref, oht_ref, heads, tails)
    second = pair(second_ref)
    direction = [second[c] + to_blocks(rise[c], blocks) for c in range(2)]
    keep(direction_ref, direction)
    rises = []
    for d, step in enumerate(((-1, 0), (1, 0), (0, -1), (0, 1))):
        spots = [pl.ds((2 * d + k) * IFC, IFC) for k in range(2)]
        rise = gradient(
            around(*step), ext, oha_ref.at[:, spots[0]], oha_ref.at[:, spots[1]],
            ends_ref[:, spots[0]], ends_ref[:, spots[1]],
        )
        if d < 2:
            there = me + step[0]
            real = (there >= 0) & (there < lat)
            rise = [jnp.where(real, part, 0.0) for part in rise]
        rises.append(rise)
    rows = [jnp.concatenate([rise[c] for rise in rises], axis=1) * coef_row(pack_ref) for c in range(2)]
    more = put(rows, ohi_ref, block_mask(index_rows(pack_ref) // BS, EB))
    extra = pair(extra_ref)
    local = stiffness(direction, pair(value_ref), wd_ref, wo_ref, wide, out)
    return [local[c] + extra[c] + more[c] for c in range(2)]


def prolong_first_kernel(
    lat, chip_ref, away_ref, near_ref, ohi_ref, oht_ref, ohh_ref, pack_ref, second_ref, extra_ref,
    ends_ref, oha_ref, value_ref, wd_ref, wo_ref, scale_ref,
    m0, m1, m2, m3, direction_ref, image_ref, first_ref,
    *scratch,
):
    image = prolong(
        lat, chip_ref, away_ref, near_ref, ohi_ref, oht_ref, ohh_ref, pack_ref, second_ref, extra_ref,
        ends_ref, oha_ref, value_ref, wd_ref, wo_ref, direction_ref, *scratch,
    )
    keep(image_ref, image)
    first = complex_times(pair(scale_ref), image)
    keep(first_ref, first)
    hand_out((m0, m1, m2, m3), interface_messages(first, ohi_ref, index_rows(pack_ref)))


def total(x):
    return jnp.sum(jnp.sum(x, axis=0, keepdims=True), axis=1, keepdims=True)


def inner(a, b):
    return total(a[0] * b[0] + a[1] * b[1]), total(a[0] * b[1] - a[1] * b[0])


def prolong_last_kernel(
    lat, chip_ref, away_ref, near_ref, ohi_ref, oht_ref, ohh_ref, pack_ref, second_ref, extra_ref,
    ends_ref, oha_ref, value_ref, wd_ref, wo_ref, image_ref,
    direction_ref, image2_ref, sums_ref,
    *scratch,
):
    image2 = prolong(
        lat, chip_ref, away_ref, near_ref, ohi_ref, oht_ref, ohh_ref, pack_ref, second_ref, extra_ref,
        ends_ref, oha_ref, value_ref, wd_ref, wo_ref, direction_ref, *scratch,
    )
    right, image = pair(pack_ref, RIGHT), pair(image_ref)
    keep(image2_ref, image2)
    rest = (right[0] - image[0], right[1] - image[1])
    turn = (image[0] - image2[0], image[1] - image2[1])
    found = [inner(right, right)[0], inner(image, image)[0], inner(rest, rest)[0], inner(turn, turn)[0]]
    found += [*inner(image, rest), *inner(turn, rest), *inner(turn, image)]
    lane = lax.broadcasted_iota(jnp.int32, (1, BS), 1)
    row = jnp.zeros((1, BS), F32)
    for k, value in enumerate(found):
        row = jnp.where(lane == k, value, row)
    sums_ref[...] = jnp.broadcast_to(row[None], sums_ref.shape)


def finish_kernel(
    sums_ref, pack_ref, image_ref, image2_ref, direction_ref, direction2_ref,
    solution_ref, residual_ref, history_ref,
):
    row = jnp.sum(sums_ref[...], axis=0)
    lane = lax.broadcasted_iota(jnp.int32, (1, BS), 1)
    found = [jnp.sum(jnp.where(lane == k, row, 0.0), axis=1, keepdims=True) for k in range(10)]
    start, ww, rr, tt = found[:4]
    wr, tr, tw = found[4:6], found[6:8], found[8:10]
    extra = (wr[0] / ww, wr[1] / ww)
    alpha = (1.0 + extra[0], extra[1])
    fresh = rr - (wr[0] * extra[0] + wr[1] * extra[1])
    moved = complex_times(extra, tw)
    c2 = complex_times((alpha[0], -alpha[1]), (tr[0] - moved[0], tr[1] - moved[1]))
    cross = complex_times(complex_times((extra[0], -extra[1]), alpha), (tw[0], -tw[1]))
    ww2 = (alpha[0] * alpha[0] + alpha[1] * alpha[1]) * tt
    ww2 = ww2 + (extra[0] * extra[0] + extra[1] * extra[1]) * ww - 2.0 * cross[0]
    alpha2 = (c2[0] / ww2, c2[1] / ww2)
    fresh2 = fresh - (c2[0] * alpha2[0] + c2[1] * alpha2[1])
    history_ref[0] = (fresh / start)[0, 0]
    history_ref[1] = (fresh2 / start)[0, 0]
    right, image, image2 = pair(pack_ref, RIGHT), pair(image_ref), pair(image2_ref)
    direction, direction2 = pair(direction_ref), pair(direction2_ref)
    step = complex_times(alpha, direction)
    other = complex_times(alpha, direction2)
    step2 = complex_times(alpha2, (direction[0] - other[0], direction[1] - other[1]))
    away = complex_times(extra, image)
    other = complex_times(alpha, image2)
    away2 = complex_times(alpha2, (image[0] - other[0], image[1] - other[1]))
    for c in range(2):
        solution_ref[c, 0] = lanes(step[c] + step2[c], EB)
        residual_ref[c, 0] = lanes(right[c] - image[c] - away[c] - away2[c], EB)


def shape(*dims, dtype=F32):
    return jax.ShapeDtypeStruct(dims, dtype)


FIELD = shape(2 * EB, BS)
MESSAGES = [shape(4, BS)] * 4


def call(body, outs, args, name, scratch=(), space=pltpu.VMEM, out_spaces=None, limit=LIMIT, flops=0):
    specs = [pl.BlockSpec(memory_space=space)] * len(args)
    moved = sum(a.size * a.dtype.itemsize for a in args)
    return pl.pallas_call(
        body,
        out_shape=outs,
        in_specs=specs,
        out_specs=[pl.BlockSpec(memory_space=place) for place in out_spaces or [pltpu.VMEM] * len(outs)],
        scratch_shapes=scratch,
        compiler_params=pltpu.CompilerParams(vmem_limit_bytes=limit),
        cost_estimate=pl.CostEstimate(flops=flops, bytes_accessed=moved, transcendentals=0),
        name=name,
    )(*args)


def swap(pairs):
    return [(a, b) for a, b in pairs] + [(b, a) for a, b in pairs]


def lat_pairs(first):
    return [(k, k + 1) for k in range(first, lax.axis_size("lat") - 1, 2)]


def swap_far(message):
    return lax.ppermute(message, "lat", swap(lat_pairs(1)))


def on_chip(message):
    return lax.all_gather(message, "lat", axis_index_groups=lat_pairs(0))


def exchange(messages):
    lon = lax.axis_size("lon")
    return [
        lax.ppermute(messages[0], "lon", swap([(k, (k + 1) % lon) for k in range(1, lon, 2)])),
        lax.ppermute(messages[1], "lon", swap([(k, k + 1) for k in range(0, lon, 2)])),
        swap_far(messages[2]),
        lax.ppermute(messages[3], "lat", swap(lat_pairs(0))),
    ]


def everywhere(row, axis):
    return lax.all_to_all(row, axis, 0, 0)


def on_device(rhs, cond, blk_diag, blk_off, idx, cnt, coup, nodes):
    blocks = pltpu.VMEM((EB, BS), F32)
    wide = pltpu.VMEM((8 * (EB + 2), BS), F32)
    out = pltpu.VMEM((8 * EB, BS), F32)
    small = (rhs, cond, coup, cnt, idx, nodes)
    (pack,) = call(
        pack_kernel,
        [shape(PACKED, BS)],
        small,
        "pack",
        scratch=[(pltpu.SMEM if part is cnt else pltpu.VMEM)(part.shape, part.dtype) for part in small]
        + [pltpu.SemaphoreType.DMA((6,))],
        space=pltpu.HBM,
        limit=PACK_LIMIT,
    )
    onehots = [(BS, 4 * IFC), (BS, E), (BS, E)]
    *sent, value, scale, first, own, ohi, oht, ohh, inside = call(
        begin_kernel,
        [shape(12, BS)] * 4 + [FIELD] * 3 + [shape(4, BS)] + [shape(*dims, dtype=BF16) for dims in onehots]
        + [shape(EB, BS, 2 * BS, dtype=BF16)],
        (pack, blk_diag),
        "begin",
    )
    arrived = exchange(sent)
    (beside,) = call(weight_kernel, [shape(EB, 2 * BS, 2 * BS, dtype=BF16)], (blk_off,), "weights", flops=10**7)

    def local(field):
        return call(
            local_kernel, [FIELD], (field, value, inside, beside), "local", scratch=[wide, out], flops=2 * 8 * EB * 3 * BS * 2 * BS
        )[0]

    lat, lon = lax.axis_size("lat"), lax.axis_size("lon")
    scratch = [blocks, pltpu.VMEM((2 * EB, BS), F32), wide, out, pltpu.VMEM((6, 3, 4, BS), F32)]
    directions = []
    for step in range(ITERS):
        stiff = local(first)
        if step == 0:
            *sent, second, ninv, ends, oha = call(
                smooth_first_kernel,
                MESSAGES + [FIELD, shape(4, BS), shape(1, 8 * IFC, dtype=jnp.int32), shape(BS, 8 * IFC, dtype=BF16)],
                (*arrived, own, ohi, pack, first, stiff, scale),
                "smooth_first",
            )
            source = pack
        else:
            *sent, second = call(
                smooth_kernel,
                MESSAGES + [FIELD],
                (*arrived, ohi, pack, first, stiff, scale, source),
                "smooth",
            )
        arrived = exchange(sent)
        stiff = local(second)
        far, core, row, extra = call(
            restrict_kernel,
            MESSAGES[:2] + [shape(3, 4, BS), FIELD],
            (*arrived, ohi, oht, ohh, pack, stiff, source),
            "restrict",
        )
        known = step > 0
        (row,) = call(
            row_kernel,
            [shape(lon, 3 if known else 4, 4, BS)],
            (swap_far(far), on_chip(core), row) + (() if known else (ninv,)),
            "row",
        )
        near, column, *found = call(
            functools.partial(column_kernel, known, lon),
            [shape(5, 4, BS), shape(3, 4, BS)] + ([] if known else [shape(5, 4, BS)]),
            (everywhere(row, "lon"),) + ((inverses,) if known else ()),
            "column",
        )
        chip = on_chip(column)
        away = on_chip(swap_far(chip.reshape(6, 4, BS)))
        args = (chip, away, near, ohi, oht, ohh, pack, second, extra, ends, oha, value, inside, beside)
        if step == 0:
            (inverses,) = found
            *sent, direction, image, first = call(
                functools.partial(prolong_first_kernel, lat),
                MESSAGES + [FIELD] * 3,
                args + (scale,),
                "prolong_first",
                scratch=scratch,
            )
            source = image
            arrived = exchange(sent)
        else:
            direction, image2, sums = call(
                functools.partial(prolong_last_kernel, lat),
                [FIELD, FIELD, shape(lat, 1, BS)],
                args + (image,),
                "prolong_last",
                scratch=scratch,
            )
        directions.append(direction)
    sums = jnp.sum(everywhere(sums, "lat"), axis=0, keepdims=True)
    sums = everywhere(jnp.broadcast_to(sums, (lax.axis_size("lon"), 1, BS)), "lon")
    solution, residual, history = call(
        finish_kernel,
        [shape(2, 1, 1, E), shape(2, 1, 1, E), shape(ITERS)],
        (sums, pack, image, image2, directions[0], directions[1]),
        "finish",
        out_spaces=[pltpu.VMEM, pltpu.VMEM, pltpu.SMEM],
    )
    return solution, residual, history


def solution(mesh):
    placed = (
        P(None, "lat", "lon", None),
        P("lat", "lon", None),
        P("lat", "lon", None, None, None),
        P("lat", "lon", None, None, None),
        P("lat", "lon", None, None),
        P("lat", "lon", None),
        P("lat", "lon", None, None),
        P("lat", "lon", None, None),
    )
    return jax.shard_map(
        on_device,
        mesh=mesh,
        in_specs=placed,
        out_specs=(P(None, "lat", "lon", None), P(None, "lat", "lon", None), P()),
        check_vma=False,
    )
```

```python
import functools

import jax
import jax.numpy as jnp
from jax import lax
from jax.experimental import pallas as pl
from jax.experimental.pallas import tpu as pltpu
from jax.sharding import PartitionSpec as P

ITERS = 2
EB = 16
BS = 128
E = EB * BS
ND = 256
IFC = 256
OMEGA = 0.8
F32 = jnp.float32
BF16 = jnp.bfloat16
LIMIT = 20 * 1024 * 1024
PACK_LIMIT = 60 * 1024 * 1024
RIGHT, COND, COEF, INDEX, TAILS, HEADS, PACKED = 0, 32, 48, 56, 64, 80, 96
NT = (((1,), (1,)), ((), ()))


def complex_times(a, b):
    return a[0] * b[0] - a[1] * b[1], a[0] * b[1] + a[1] * b[0]


def complex_inverse(a):
    scale = a[0] * a[0] + a[1] * a[1]
    return a[0] / scale, -a[1] / scale


def pieces(x):
    first = x.astype(BF16).astype(F32)
    rest = x - first
    second = rest.astype(BF16).astype(F32)
    return first, second, rest - second


def split(block):
    high = block.astype(BF16)
    return jnp.concatenate([high, (block - high.astype(F32)).astype(BF16)], axis=1)


def lanes(x, count):
    return jnp.concatenate([x[k : k + 1] for k in range(count)], axis=1)


def to_blocks(row, ref):
    for k in range(EB):
        ref[k : k + 1] = row[:, k * BS : (k + 1) * BS]
    return ref[...]


def block_mask(blocks, rows):
    return lax.broadcasted_iota(jnp.int32, (rows, blocks.shape[1]), 0) == blocks


def lane_onehot(index):
    spot = lax.broadcasted_iota(jnp.int32, (BS, index.shape[1]), 0)
    return jnp.where(spot == index % BS, 1.0, 0.0).astype(BF16)


def take(field, onehot, mask):
    parts = [pieces(part) for part in field]
    stack = jnp.concatenate([parts[c][p] for p in range(3) for c in range(2)], axis=0)
    got = jnp.dot(stack.astype(BF16), onehot[...], preferred_element_type=F32)
    got = got[:32] + got[32:64] + got[64:]
    return [
        jnp.sum(jnp.where(mask, got[16 * c : 16 * c + 16], 0.0), axis=0, keepdims=True)
        for c in range(2)
    ]


def put(rows, onehot, mask):
    parts = [pieces(part) for part in rows]
    stack = jnp.concatenate(
        [jnp.where(mask, parts[c][p], 0.0) for p in range(3) for c in range(2)], axis=0
    )
    got = lax.dot_general(stack.astype(BF16), onehot[...], NT, preferred_element_type=F32)
    got = got[:32] + got[32:64] + got[64:]
    return got[:16], got[16:]


def put_heads(rows, onehot, block):
    spot = lax.broadcasted_iota(jnp.int32, (8, block.shape[1]), 0)
    right = [pieces(part) for part in rows]
    match = (spot % 2 == block) & (spot < 4)
    stack = jnp.concatenate(
        [
            jnp.where(match, jnp.where(spot < 2, right[0][p], right[1][p]), 0.0)
            for p in range(3)
        ],
        axis=0,
    )
    got = lax.dot_general(stack.astype(BF16), onehot[...], NT, preferred_element_type=F32)
    return got[:8] + got[8:16] + got[16:]


def take_heads(own, onehot, block):
    stack = jnp.concatenate(pieces(own), axis=0)
    got = jnp.dot(stack.astype(BF16), onehot[...], preferred_element_type=F32)
    got = got[:8] + got[8:16] + got[16:]
    low = block == 0
    return [jnp.where(low, got[2 * c : 2 * c + 1], got[2 * c + 1 : 2 * c + 2]) for c in range(2)]


def parities():
    return lax.axis_index("lat") % 2 == 0, lax.axis_index("lon") % 2 == 0


def hand_out(refs, towards, at=0):
    even_lat, even_lon = parities()
    refs[0][at : at + 4] = jnp.where(even_lon, towards[2], towards[3])
    refs[1][at : at + 4] = jnp.where(even_lon, towards[3], towards[2])
    refs[2][at : at + 4] = jnp.where(even_lat, towards[0], towards[1])
    refs[3][at : at + 4] = jnp.where(even_lat, towards[1], towards[0])


def collect(refs, at=0):
    even_lat, even_lon = parities()
    wide, near, far, core = [ref[at : at + 4] for ref in refs]
    return (
        jnp.where(even_lat, far, core),
        jnp.where(even_lat, core, far),
        jnp.where(even_lon, wide, near),
        jnp.where(even_lon, near, wide),
    )


def index_rows(pack_ref):
    return lanes(pack_ref[INDEX : INDEX + 8], 8).astype(jnp.int32)


def ends_rows(pack_ref):
    return [lanes(pack_ref[at : at + EB], EB).astype(jnp.int32) for at in (TAILS, HEADS)]


def coef_row(pack_ref):
    return lanes(pack_ref[COEF : COEF + 8], 8)


def interface_messages(field, onehot, index):
    got = take(field, onehot, block_mask(index // BS, EB))
    return [
        jnp.concatenate(
            [
                got[c][:, d * IFC + h * BS : d * IFC + (h + 1) * BS]
                for c in range(2)
                for h in range(2)
            ],
            axis=0,
        )
        for d in range(4)
    ]


def interface_sum(arrived, coefs, onehot, index):
    rows = [
        jnp.concatenate(
            [arrived[d][2 * c + h : 2 * c + h + 1] for d in range(4) for h in range(2)], axis=1
        )
        * coefs
        for c in range(2)
    ]
    return put(rows, onehot, block_mask(index // BS, EB))


def pair(ref, at=0):
    return ref[at : at + EB], ref[at + EB : at + 2 * EB]


def keep(ref, value):
    ref[0:EB] = value[0]
    ref[EB : 2 * EB] = value[1]


def nodal(rows, onehot_head, onehot_tail, pack_ref, sign):
    tails, heads = ends_rows(pack_ref)
    own = put_heads(rows, onehot_head, heads // BS)
    ext = put(rows, onehot_tail, block_mask(tails // BS, EB))
    parts = [
        sign * jnp.concatenate([ext[0][2 * d : 2 * d + 2], ext[1][2 * d : 2 * d + 2]], axis=0)
        for d in range(5)
    ]
    return own[0:4] + parts[0], parts[1:]


def pack_kernel(
    rhs_ref, cond_ref, coup_ref, cnt_ref, idx_ref, nodes_ref, pack_ref,
    rhs_got, cond_got, coup_got, cnt_got, idx_got, nodes_got, sems,
):
    pairs = (
        (rhs_ref, rhs_got), (cond_ref, cond_got), (coup_ref, coup_got),
        (cnt_ref, cnt_got), (idx_ref, idx_got), (nodes_ref, nodes_got),
    )
    copies = [pltpu.make_async_copy(here, there, sems.at[k]) for k, (here, there) in enumerate(pairs)]
    for copy in copies:
        copy.start()
    for copy in copies:
        copy.wait()

    def rows(at, row):
        for k in range(row.shape[1] // BS):
            pack_ref[at + k : at + k + 1] = row[:, k * BS : (k + 1) * BS]

    for c in range(2):
        rows(RIGHT + EB * c, rhs_got[c, 0])
        rows((TAILS, HEADS)[c], nodes_got[0, 0, c : c + 1].astype(F32))
    rows(COND, cond_got[0])
    slot = lax.broadcasted_iota(jnp.int32, (1, IFC), 1)
    for d in range(4):
        rows(COEF + 2 * d, jnp.where(slot < cnt_got[0, 0, d], coup_got[0, 0, d : d + 1], 0.0))
        rows(INDEX + 2 * d, idx_got[0, 0, d : d + 1].astype(F32))


def begin_kernel(
    pack_ref, diag_ref,
    m0, m1, m2, m3, value_ref, scale_ref, first_ref, own_ref,
    ohi_ref, oht_ref, ohh_ref, wd_ref,
):
    messages = (m0, m1, m2, m3)
    index = index_rows(pack_ref)
    tails, heads = ends_rows(pack_ref)
    ohi_ref[...] = lane_onehot(index)
    oht_ref[...] = lane_onehot(tails)
    ohh_ref[...] = lane_onehot(heads)
    eye = lax.broadcasted_iota(jnp.int32, (BS, BS), 0) == lax.broadcasted_iota(jnp.int32, (BS, BS), 1)
    for b in range(EB):
        block = diag_ref[0, 0, b]
        value_ref[b : b + 1] = jnp.sum(jnp.where(eye, block, 0.0), axis=0, keepdims=True)
        wd_ref[b] = split(jnp.where(eye, 0.0, block))
    value_ref[EB : 2 * EB] = pack_ref[COND : COND + EB]
    value = pair(value_ref)
    inverse = complex_inverse(value)
    scale = (OMEGA * inverse[0], OMEGA * inverse[1])
    keep(scale_ref, scale)
    first = complex_times(scale, pair(pack_ref, RIGHT))
    keep(first_ref, first)
    hand_out(messages, interface_messages(first, ohi_ref, index), 0)
    rows = [lanes(value[c], EB) for c in range(2)]
    own, towards = nodal(rows, ohh_ref, oht_ref, pack_ref, 1.0)
    own_ref[0:4] = own
    hand_out(messages, towards, 4)
    ends = [pack_ref[at : at + EB] for at in (HEADS, TAILS)]
    hand_out(messages, interface_messages(ends, ohi_ref, index), 8)


def weight_kernel(off_ref, wo_ref):
    zero = jnp.zeros((BS, 2 * BS), BF16)
    wo_ref[0, 0:BS] = zero
    wo_ref[EB - 1, BS:] = zero
    for b in range(EB - 1):
        off = off_ref[0, 0, b]
        wo_ref[b + 1, 0:BS] = split(off)
        wo_ref[b, BS:] = split(off.T)


def stiffness(field, value, wd_ref, wo_ref, wide, out):
    wide[0:8] = jnp.zeros((8, BS), F32)
    wide[8 * (EB + 1) :] = jnp.zeros((8, BS), F32)
    for c in range(2):
        for p, piece in enumerate(pieces(field[c])):
            wide[pl.ds(8 + 2 * p + c, EB, stride=8)] = piece
    for k in (6, 7):
        wide[pl.ds(8 + k, EB, stride=8)] = jnp.zeros((EB, BS), F32)
    for b in range(EB):
        low, here, high = [wide[8 * (b + k) : 8 * (b + k) + 8] for k in range(3)]
        beside = jnp.concatenate([low, high], axis=1)
        got = jnp.dot(here.astype(BF16), wd_ref[b], preferred_element_type=F32)
        got = got + jnp.dot(beside.astype(BF16), wo_ref[b], preferred_element_type=F32)
        out[8 * b : 8 * b + 8] = got[:, :BS] + got[:, BS:]
    sums = [
        out[pl.ds(c, EB, stride=8)] + out[pl.ds(2 + c, EB, stride=8)] + out[pl.ds(4 + c, EB, stride=8)]
        for c in range(2)
    ]
    turned = complex_times(value, field)
    return sums[0] + turned[0], sums[1] + turned[1]


def local_kernel(field_ref, value_ref, wd_ref, wo_ref, out_ref, wide, out):
    keep(out_ref, stiffness(pair(field_ref), pair(value_ref), wd_ref, wo_ref, wide, out))


def smooth(arrived, ohi_ref, pack_ref, first_ref, local_ref, scale_ref, right_ref, m, second_ref):
    index = index_rows(pack_ref)
    extra = interface_sum(arrived, coef_row(pack_ref), ohi_ref, index)
    first, local, right = pair(first_ref), pair(local_ref), pair(right_ref)
    change = complex_times(pair(scale_ref), [right[c] - local[c] - extra[c] for c in range(2)])
    second = (first[0] + change[0], first[1] + change[1])
    keep(second_ref, second)
    hand_out(m, interface_messages(second, ohi_ref, index))


def smooth_first_kernel(
    a0, a1, a2, a3, own_ref, ohi_ref, pack_ref, first_ref, local_ref, scale_ref,
    m0, m1, m2, m3, second_ref, ninv_ref, ends_ref, oha_ref,
):
    arrived = collect((a0, a1, a2, a3))
    smooth(arrived, ohi_ref, pack_ref, first_ref, local_ref, scale_ref, pack_ref, (m0, m1, m2, m3), second_ref)
    sums = own_ref[0:4]
    for part in collect((a0, a1, a2, a3), 4):
        sums = sums + part
    inverse = complex_inverse((sums[0:2], sums[2:4]))
    ninv_ref[0:2] = inverse[0]
    ninv_ref[2:4] = inverse[1]
    for ref in (m0, m1):
        ref[4:8] = ninv_ref[...]
    for d, part in enumerate(collect((a0, a1, a2, a3), 8)):
        for k in range(2):
            row = jnp.concatenate([part[2 * k : 2 * k + 1], part[2 * k + 1 : 2 * k + 2]], axis=1)
            row = row.astype(jnp.int32)
            at = (2 * d + k) * IFC
            ends_ref[:, at : at + IFC] = row
            oha_ref[:, at : at + IFC] = lane_onehot(row)


def smooth_kernel(
    a0, a1, a2, a3, ohi_ref, pack_ref, first_ref, local_ref, scale_ref, right_ref,
    m0, m1, m2, m3, second_ref,
):
    arrived = collect((a0, a1, a2, a3))
    smooth(arrived, ohi_ref, pack_ref, first_ref, local_ref, scale_ref, right_ref, (m0, m1, m2, m3), second_ref)


def times_inverse(inverse, value):
    result = complex_times((inverse[0:2], inverse[2:4]), (value[0:2], value[2:4]))
    return jnp.concatenate(result, axis=0)


def restrict_kernel(known, a0, a1, a2, a3, ohi_ref, oht_ref, ohh_ref, pack_ref, local_ref, right_ref, beside_ref, *refs):
    far_ref, core_ref, row_ref, extra_ref = refs[:4]
    even_lat, even_lon = parities()
    if known:
        west, east = beside_ref[0], beside_ref[1]
    else:
        wide, near = a0[4:8], a1[4:8]
        west, east = jnp.where(even_lon, wide, near), jnp.where(even_lon, near, wide)
        refs[4][0] = west
        refs[4][1] = east
    index = index_rows(pack_ref)
    extra = interface_sum(collect((a0, a1, a2, a3)), coef_row(pack_ref), ohi_ref, index)
    keep(extra_ref, extra)
    local, right = pair(local_ref), pair(right_ref)
    rows = [lanes(right[c] - local[c] - extra[c], EB) for c in range(2)]
    own, towards = nodal(rows, ohh_ref, oht_ref, pack_ref, -1.0)
    far_ref[...] = jnp.where(even_lat, towards[0], towards[1])
    core_ref[...] = jnp.where(even_lat, towards[1], towards[0])
    row_ref[0] = own
    row_ref[1] = times_inverse(west, towards[2])
    row_ref[2] = times_inverse(east, towards[3])


def row_kernel(far_ref, core_ref, row_ref, ninv_ref, out_ref):
    even_lat, _ = parities()
    core = jnp.where(even_lat, core_ref[1], core_ref[0])
    mine = times_inverse(ninv_ref[...], row_ref[0] + far_ref[...] + core)
    for k, part in enumerate((mine, row_ref[1], row_ref[2])):
        out_ref[:, k] = jnp.broadcast_to(part[None], (out_ref.shape[0], 4, BS))


def column_kernel(lon, row_ref, near_ref, out_ref):
    me = lax.axis_index("lon")

    def at(step):
        return lax.rem(me + (lon + step), lon)

    for k in range(5):
        near_ref[k] = row_ref[at(k - 2), 0] + row_ref[at(k - 1), 1] + row_ref[at(k - 3), 2]
    for k in range(3):
        out_ref[k] = near_ref[k + 1]


def extend(nodes, ref):
    for d in range(5):
        for c in range(2):
            ref[EB * c + 2 * d : EB * c + 2 * d + 2] = nodes[d][2 * c : 2 * c + 2]
    return pair(ref)


def gradient(nodes, ref, onehot_head, onehot_tail, heads, tails):
    low = take(extend(nodes, ref), onehot_tail, block_mask(tails // BS, EB))
    high = take_heads(jnp.concatenate([nodes[0], nodes[0]], axis=0), onehot_head, heads // BS)
    return [high[c] - low[c] for c in range(2)]


def prolong(
    lat, chip_ref, away_ref, near_ref, ohi_ref, oht_ref, ohh_ref, pack_ref, second_ref, extra_ref,
    ends_ref, oha_ref, value_ref, wd_ref, wo_ref, direction_ref, blocks, ext, wide, out, column,
):
    me = lax.axis_index("lat")

    for k in range(2):
        column[k] = away_ref[0, 3 * k : 3 * k + 3]
        column[2 + k] = chip_ref[k]
        column[4 + k] = away_ref[1, 3 * k : 3 * k + 3]
    here = 2 + me % 2

    def node(down, right):
        if down == 0:
            return near_ref[right + 2]
        return column[here + down, right + 1]

    def around(down, right):
        steps = ((0, 0), (-1, 0), (1, 0), (0, -1), (0, 1))
        return [node(down + i, right + j) for i, j in steps]

    ext[...] = jnp.zeros((2 * EB, BS), F32)
    tails, heads = ends_rows(pack_ref)
    rise = gradient(around(0, 0), ext, ohh_ref, oht_ref, heads, tails)
    second = pair(second_ref)
    direction = [second[c] + to_blocks(rise[c], blocks) for c in range(2)]
    keep(direction_ref, direction)
    rises = []
    for d, step in enumerate(((-1, 0), (1, 0), (0, -1), (0, 1))):
        spots = [pl.ds((2 * d + k) * IFC, IFC) for k in range(2)]
        rise = gradient(
            around(*step), ext, oha_ref.at[:, spots[0]], oha_ref.at[:, spots[1]],
            ends_ref[:, spots[0]], ends_ref[:, spots[1]],
        )
        if d < 2:
            there = me + step[0]
            real = (there >= 0) & (there < lat)
            rise = [jnp.where(real, part, 0.0) for part in rise]
        rises.append(rise)
    rows = [jnp.concatenate([rise[c] for rise in rises], axis=1) * coef_row(pack_ref) for c in range(2)]
    more = put(rows, ohi_ref, block_mask(index_rows(pack_ref) // BS, EB))
    extra = pair(extra_ref)
    local = stiffness(direction, pair(value_ref), wd_ref, wo_ref, wide, out)
    return [local[c] + extra[c] + more[c] for c in range(2)]


def prolong_first_kernel(
    lat, chip_ref, away_ref, near_ref, ohi_ref, oht_ref, ohh_ref, pack_ref, second_ref, extra_ref,
    ends_ref, oha_ref, value_ref, wd_ref, wo_ref, scale_ref,
    m0, m1, m2, m3, direction_ref, image_ref, first_ref,
    *scratch,
):
    image = prolong(
        lat, chip_ref, away_ref, near_ref, ohi_ref, oht_ref, ohh_ref, pack_ref, second_ref, extra_ref,
        ends_ref, oha_ref, value_ref, wd_ref, wo_ref, direction_ref, *scratch,
    )
    keep(image_ref, image)
    first = complex_times(pair(scale_ref), image)
    keep(first_ref, first)
    hand_out((m0, m1, m2, m3), interface_messages(first, ohi_ref, index_rows(pack_ref)))


def total(x):
    return jnp.sum(jnp.sum(x, axis=0, keepdims=True), axis=1, keepdims=True)


def inner(a, b):
    return total(a[0] * b[0] + a[1] * b[1]), total(a[0] * b[1] - a[1] * b[0])


def prolong_last_kernel(
    lat, chip_ref, away_ref, near_ref, ohi_ref, oht_ref, ohh_ref, pack_ref, second_ref, extra_ref,
    ends_ref, oha_ref, value_ref, wd_ref, wo_ref, image_ref,
    direction_ref, image2_ref, sums_ref,
    *scratch,
):
    image2 = prolong(
        lat, chip_ref, away_ref, near_ref, ohi_ref, oht_ref, ohh_ref, pack_ref, second_ref, extra_ref,
        ends_ref, oha_ref, value_ref, wd_ref, wo_ref, direction_ref, *scratch,
    )
    right, image = pair(pack_ref, RIGHT), pair(image_ref)
    keep(image2_ref, image2)
    rest = (right[0] - image[0], right[1] - image[1])
    turn = (image[0] - image2[0], image[1] - image2[1])
    found = [inner(right, right)[0], inner(image, image)[0], inner(rest, rest)[0], inner(turn, turn)[0]]
    found += [*inner(image, rest), *inner(turn, rest), *inner(turn, image)]
    lane = lax.broadcasted_iota(jnp.int32, (1, BS), 1)
    row = jnp.zeros((1, BS), F32)
    for k, value in enumerate(found):
        row = jnp.where(lane == k, value, row)
    sums_ref[...] = jnp.broadcast_to(row[None], sums_ref.shape)


def finish_kernel(
    sums_ref, pack_ref, image_ref, image2_ref, direction_ref, direction2_ref,
    solution_ref, residual_ref, history_ref,
):
    row = jnp.sum(sums_ref[...], axis=0)
    lane = lax.broadcasted_iota(jnp.int32, (1, BS), 1)
    found = [jnp.sum(jnp.where(lane == k, row, 0.0), axis=1, keepdims=True) for k in range(10)]
    start, ww, rr, tt = found[:4]
    wr, tr, tw = found[4:6], found[6:8], found[8:10]
    extra = (wr[0] / ww, wr[1] / ww)
    alpha = (1.0 + extra[0], extra[1])
    fresh = rr - (wr[0] * extra[0] + wr[1] * extra[1])
    moved = complex_times(extra, tw)
    c2 = complex_times((alpha[0], -alpha[1]), (tr[0] - moved[0], tr[1] - moved[1]))
    cross = complex_times(complex_times((extra[0], -extra[1]), alpha), (tw[0], -tw[1]))
    ww2 = (alpha[0] * alpha[0] + alpha[1] * alpha[1]) * tt
    ww2 = ww2 + (extra[0] * extra[0] + extra[1] * extra[1]) * ww - 2.0 * cross[0]
    alpha2 = (c2[0] / ww2, c2[1] / ww2)
    fresh2 = fresh - (c2[0] * alpha2[0] + c2[1] * alpha2[1])
    history_ref[0] = (fresh / start)[0, 0]
    history_ref[1] = (fresh2 / start)[0, 0]
    right, image, image2 = pair(pack_ref, RIGHT), pair(image_ref), pair(image2_ref)
    direction, direction2 = pair(direction_ref), pair(direction2_ref)
    step = complex_times(alpha, direction)
    other = complex_times(alpha, direction2)
    step2 = complex_times(alpha2, (direction[0] - other[0], direction[1] - other[1]))
    away = complex_times(extra, image)
    other = complex_times(alpha, image2)
    away2 = complex_times(alpha2, (image[0] - other[0], image[1] - other[1]))
    for c in range(2):
        solution_ref[c, 0] = lanes(step[c] + step2[c], EB)
        residual_ref[c, 0] = lanes(right[c] - image[c] - away[c] - away2[c], EB)


def shape(*dims, dtype=F32):
    return jax.ShapeDtypeStruct(dims, dtype)


FIELD = shape(2 * EB, BS)
MESSAGES = [shape(4, BS)] * 4


def call(body, outs, args, name, scratch=(), space=pltpu.VMEM, out_spaces=None, limit=LIMIT, flops=0):
    specs = [pl.BlockSpec(memory_space=space)] * len(args)
    moved = sum(a.size * a.dtype.itemsize for a in args)
    return pl.pallas_call(
        body,
        out_shape=outs,
        in_specs=specs,
        out_specs=[pl.BlockSpec(memory_space=place) for place in out_spaces or [pltpu.VMEM] * len(outs)],
        scratch_shapes=scratch,
        compiler_params=pltpu.CompilerParams(vmem_limit_bytes=limit),
        cost_estimate=pl.CostEstimate(flops=flops, bytes_accessed=moved, transcendentals=0),
        name=name,
    )(*args)


def swap(pairs):
    return [(a, b) for a, b in pairs] + [(b, a) for a, b in pairs]


def lat_pairs(first):
    return [(k, k + 1) for k in range(first, lax.axis_size("lat") - 1, 2)]


def swap_far(message):
    return lax.ppermute(message, "lat", swap(lat_pairs(1)))


def on_chip(message):
    return lax.all_gather(message, "lat", axis_index_groups=lat_pairs(0))


def exchange(messages):
    lon = lax.axis_size("lon")
    return [
        lax.ppermute(messages[0], "lon", swap([(k, (k + 1) % lon) for k in range(1, lon, 2)])),
        lax.ppermute(messages[1], "lon", swap([(k, k + 1) for k in range(0, lon, 2)])),
        swap_far(messages[2]),
        lax.ppermute(messages[3], "lat", swap(lat_pairs(0))),
    ]


def everywhere(row, axis):
    return lax.all_to_all(row, axis, 0, 0)


def on_device(rhs, cond, blk_diag, blk_off, idx, cnt, coup, nodes):
    blocks = pltpu.VMEM((EB, BS), F32)
    wide = pltpu.VMEM((8 * (EB + 2), BS), F32)
    out = pltpu.VMEM((8 * EB, BS), F32)
    small = (rhs, cond, coup, cnt, idx, nodes)
    (pack,) = call(
        pack_kernel,
        [shape(PACKED, BS)],
        small,
        "pack",
        scratch=[(pltpu.SMEM if part is cnt else pltpu.VMEM)(part.shape, part.dtype) for part in small]
        + [pltpu.SemaphoreType.DMA((6,))],
        space=pltpu.HBM,
        limit=PACK_LIMIT,
    )
    onehots = [(BS, 4 * IFC), (BS, E), (BS, E)]
    *sent, value, scale, first, own, ohi, oht, ohh, inside = call(
        begin_kernel,
        [shape(12, BS)] * 4 + [FIELD] * 3 + [shape(4, BS)] + [shape(*dims, dtype=BF16) for dims in onehots]
        + [shape(EB, BS, 2 * BS, dtype=BF16)],
        (pack, blk_diag),
        "begin",
    )
    arrived = exchange(sent)
    (beside,) = call(weight_kernel, [shape(EB, 2 * BS, 2 * BS, dtype=BF16)], (blk_off,), "weights", flops=10**7)

    def local(field):
        return call(
            local_kernel, [FIELD], (field, value, inside, beside), "local", scratch=[wide, out], flops=2 * 8 * EB * 3 * BS * 2 * BS
        )[0]

    lat, lon = lax.axis_size("lat"), lax.axis_size("lon")
    scratch = [blocks, pltpu.VMEM((2 * EB, BS), F32), wide, out, pltpu.VMEM((6, 3, 4, BS), F32)]
    directions = []
    for step in range(ITERS):
        stiff = local(first)
        if step == 0:
            *sent, second, ninv, ends, oha = call(
                smooth_first_kernel,
                [shape(8, BS)] * 2 + MESSAGES[2:] + [FIELD, shape(4, BS), shape(1, 8 * IFC, dtype=jnp.int32), shape(BS, 8 * IFC, dtype=BF16)],
                (*arrived, own, ohi, pack, first, stiff, scale),
                "smooth_first",
            )
            source = pack
        else:
            *sent, second = call(
                smooth_kernel,
                MESSAGES + [FIELD],
                (*arrived, ohi, pack, first, stiff, scale, source),
                "smooth",
            )
        arrived = exchange(sent)
        stiff = local(second)
        known = step > 0
        far, core, row, extra, *found = call(
            functools.partial(restrict_kernel, known),
            MESSAGES[:2] + [shape(3, 4, BS), FIELD] + ([] if known else [shape(2, 4, BS)]),
            (*arrived, ohi, oht, ohh, pack, stiff, source, sides if known else ninv),
            "restrict",
        )
        if not known:
            (sides,) = found
        (row,) = call(
            row_kernel, [shape(lon, 3, 4, BS)], (swap_far(far), on_chip(core), row, ninv), "row"
        )
        near, column = call(
            functools.partial(column_kernel, lon),
            [shape(5, 4, BS), shape(3, 4, BS)],
            (everywhere(row, "lon"),),
            "column",
        )
        chip = on_chip(column)
        away = on_chip(swap_far(chip.reshape(6, 4, BS)))
        args = (chip, away, near, ohi, oht, ohh, pack, second, extra, ends, oha, value, inside, beside)
        if step == 0:
            *sent, direction, image, first = call(
                functools.partial(prolong_first_kernel, lat),
                MESSAGES + [FIELD] * 3,
                args + (scale,),
                "prolong_first",
                scratch=scratch,
            )
            source = image
            arrived = exchange(sent)
        else:
            direction, image2, sums = call(
                functools.partial(prolong_last_kernel, lat),
                [FIELD, FIELD, shape(lat, 1, BS)],
                args + (image,),
                "prolong_last",
                scratch=scratch,
            )
        directions.append(direction)
    sums = jnp.sum(everywhere(sums, "lat"), axis=0, keepdims=True)
    sums = everywhere(jnp.broadcast_to(sums, (lax.axis_size("lon"), 1, BS)), "lon")
    solution, residual, history = call(
        finish_kernel,
        [shape(2, 1, 1, E), shape(2, 1, 1, E), shape(ITERS)],
        (sums, pack, image, image2, directions[0], directions[1]),
        "finish",
        out_spaces=[pltpu.VMEM, pltpu.VMEM, pltpu.SMEM],
    )
    return solution, residual, history


def solution(mesh):
    placed = (
        P(None, "lat", "lon", None),
        P("lat", "lon", None),
        P("lat", "lon", None, None, None),
        P("lat", "lon", None, None, None),
        P("lat", "lon", None, None),
        P("lat", "lon", None),
        P("lat", "lon", None, None),
        P("lat", "lon", None, None),
    )
    return jax.shard_map(
        on_device,
        mesh=mesh,
        in_specs=placed,
        out_specs=(P(None, "lat", "lon", None), P(None, "lat", "lon", None), P()),
        check_vma=False,
    )
```

```python
import functools

import jax
import jax.numpy as jnp
from jax import lax
from jax.experimental import pallas as pl
from jax.experimental.pallas import tpu as pltpu
from jax.sharding import PartitionSpec as P

ITERS = 2
EB = 16
BS = 128
E = EB * BS
ND = 256
IFC = 256
OMEGA = 0.8
F32 = jnp.float32
BF16 = jnp.bfloat16
LIMIT = 20 * 1024 * 1024
PACK_LIMIT = 60 * 1024 * 1024
RIGHT, COND, COEF, INDEX, TAILS, HEADS, PACKED = 0, 32, 48, 56, 64, 80, 96
NT = (((1,), (1,)), ((), ()))


def complex_times(a, b):
    return a[0] * b[0] - a[1] * b[1], a[0] * b[1] + a[1] * b[0]


def complex_inverse(a):
    scale = a[0] * a[0] + a[1] * a[1]
    return a[0] / scale, -a[1] / scale


def pieces(x):
    first = x.astype(BF16).astype(F32)
    rest = x - first
    second = rest.astype(BF16).astype(F32)
    return first, second, rest - second


def split(block):
    high = block.astype(BF16)
    return jnp.concatenate([high, (block - high.astype(F32)).astype(BF16)], axis=1)


def lanes(x, count):
    return jnp.concatenate([x[k : k + 1] for k in range(count)], axis=1)


def to_blocks(row, ref):
    for k in range(EB):
        ref[k : k + 1] = row[:, k * BS : (k + 1) * BS]
    return ref[...]


def block_mask(blocks, rows):
    return lax.broadcasted_iota(jnp.int32, (rows, blocks.shape[1]), 0) == blocks


def lane_onehot(index):
    spot = lax.broadcasted_iota(jnp.int32, (BS, index.shape[1]), 0)
    return jnp.where(spot == index % BS, 1.0, 0.0).astype(BF16)


def take(field, onehot, mask):
    parts = [pieces(part) for part in field]
    stack = jnp.concatenate([parts[c][p] for p in range(3) for c in range(2)], axis=0)
    got = jnp.dot(stack.astype(BF16), onehot[...], preferred_element_type=F32)
    got = got[:32] + got[32:64] + got[64:]
    return [
        jnp.sum(jnp.where(mask, got[16 * c : 16 * c + 16], 0.0), axis=0, keepdims=True)
        for c in range(2)
    ]


def put(rows, onehot, mask):
    parts = [pieces(part) for part in rows]
    stack = jnp.concatenate(
        [jnp.where(mask, parts[c][p], 0.0) for p in range(3) for c in range(2)], axis=0
    )
    got = lax.dot_general(stack.astype(BF16), onehot[...], NT, preferred_element_type=F32)
    got = got[:32] + got[32:64] + got[64:]
    return got[:16], got[16:]


def put_heads(rows, onehot, block):
    spot = lax.broadcasted_iota(jnp.int32, (8, block.shape[1]), 0)
    right = [pieces(part) for part in rows]
    match = (spot % 2 == block) & (spot < 4)
    stack = jnp.concatenate(
        [
            jnp.where(match, jnp.where(spot < 2, right[0][p], right[1][p]), 0.0)
            for p in range(3)
        ],
        axis=0,
    )
    got = lax.dot_general(stack.astype(BF16), onehot[...], NT, preferred_element_type=F32)
    return got[:8] + got[8:16] + got[16:]


def take_heads(own, onehot, block):
    stack = jnp.concatenate(pieces(own), axis=0)
    got = jnp.dot(stack.astype(BF16), onehot[...], preferred_element_type=F32)
    got = got[:8] + got[8:16] + got[16:]
    low = block == 0
    return [jnp.where(low, got[2 * c : 2 * c + 1], got[2 * c + 1 : 2 * c + 2]) for c in range(2)]


def parities():
    return lax.axis_index("lat") % 2 == 0, lax.axis_index("lon") % 2 == 0


def hand_out(refs, towards, at=0):
    even_lat, even_lon = parities()
    refs[0][at : at + 4] = jnp.where(even_lon, towards[2], towards[3])
    refs[1][at : at + 4] = jnp.where(even_lon, towards[3], towards[2])
    refs[2][at : at + 4] = jnp.where(even_lat, towards[0], towards[1])
    refs[3][at : at + 4] = jnp.where(even_lat, towards[1], towards[0])


def collect(refs, at=0):
    even_lat, even_lon = parities()
    wide, near, far, core = [ref[at : at + 4] for ref in refs]
    return (
        jnp.where(even_lat, far, core),
        jnp.where(even_lat, core, far),
        jnp.where(even_lon, wide, near),
        jnp.where(even_lon, near, wide),
    )


def index_rows(pack_ref):
    return lanes(pack_ref[INDEX : INDEX + 8], 8).astype(jnp.int32)


def ends_rows(pack_ref):
    return [lanes(pack_ref[at : at + EB], EB).astype(jnp.int32) for at in (TAILS, HEADS)]


def coef_row(pack_ref):
    return lanes(pack_ref[COEF : COEF + 8], 8)


def interface_messages(field, onehot, index):
    got = take(field, onehot, block_mask(index // BS, EB))
    return [
        jnp.concatenate(
            [
                got[c][:, d * IFC + h * BS : d * IFC + (h + 1) * BS]
                for c in range(2)
                for h in range(2)
            ],
            axis=0,
        )
        for d in range(4)
    ]


def interface_sum(arrived, coefs, onehot, index):
    rows = [
        jnp.concatenate(
            [arrived[d][2 * c + h : 2 * c + h + 1] for d in range(4) for h in range(2)], axis=1
        )
        * coefs
        for c in range(2)
    ]
    return put(rows, onehot, block_mask(index // BS, EB))


def pair(ref, at=0):
    return ref[at : at + EB], ref[at + EB : at + 2 * EB]


def keep(ref, value):
    ref[0:EB] = value[0]
    ref[EB : 2 * EB] = value[1]


def nodal(rows, onehot_head, onehot_tail, pack_ref, sign):
    tails, heads = ends_rows(pack_ref)
    own = put_heads(rows, onehot_head, heads // BS)
    ext = put(rows, onehot_tail, block_mask(tails // BS, EB))
    parts = [
        sign * jnp.concatenate([ext[0][2 * d : 2 * d + 2], ext[1][2 * d : 2 * d + 2]], axis=0)
        for d in range(5)
    ]
    return own[0:4] + parts[0], parts[1:]


def pack_kernel(
    rhs_ref, cond_ref, coup_ref, cnt_ref, idx_ref, nodes_ref, pack_ref,
    rhs_got, cond_got, coup_got, cnt_got, idx_got, nodes_got, sems,
):
    pairs = (
        (rhs_ref, rhs_got), (cond_ref, cond_got), (coup_ref, coup_got),
        (cnt_ref, cnt_got), (idx_ref, idx_got), (nodes_ref, nodes_got),
    )
    copies = [pltpu.make_async_copy(here, there, sems.at[k]) for k, (here, there) in enumerate(pairs)]
    for copy in copies:
        copy.start()
    for copy in copies:
        copy.wait()

    def rows(at, row):
        for k in range(row.shape[1] // BS):
            pack_ref[at + k : at + k + 1] = row[:, k * BS : (k + 1) * BS]

    for c in range(2):
        rows(RIGHT + EB * c, rhs_got[c, 0])
        rows((TAILS, HEADS)[c], nodes_got[0, 0, c : c + 1].astype(F32))
    rows(COND, cond_got[0])
    slot = lax.broadcasted_iota(jnp.int32, (1, IFC), 1)
    for d in range(4):
        rows(COEF + 2 * d, jnp.where(slot < cnt_got[0, 0, d], coup_got[0, 0, d : d + 1], 0.0))
        rows(INDEX + 2 * d, idx_got[0, 0, d : d + 1].astype(F32))


def begin_kernel(
    pack_ref, diag_ref,
    m0, m1, m2, m3, value_ref, scale_ref, first_ref, own_ref,
    ohi_ref, oht_ref, ohh_ref, wd_ref,
):
    messages = (m0, m1, m2, m3)
    index = index_rows(pack_ref)
    tails, heads = ends_rows(pack_ref)
    ohi_ref[...] = lane_onehot(index)
    oht_ref[...] = lane_onehot(tails)
    ohh_ref[...] = lane_onehot(heads)
    eye = lax.broadcasted_iota(jnp.int32, (BS, BS), 0) == lax.broadcasted_iota(jnp.int32, (BS, BS), 1)
    for b in range(EB):
        block = diag_ref[0, 0, b]
        value_ref[b : b + 1] = jnp.sum(jnp.where(eye, block, 0.0), axis=0, keepdims=True)
        wd_ref[b] = split(jnp.where(eye, 0.0, block))
    value_ref[EB : 2 * EB] = pack_ref[COND : COND + EB]
    value = pair(value_ref)
    inverse = complex_inverse(value)
    scale = (OMEGA * inverse[0], OMEGA * inverse[1])
    keep(scale_ref, scale)
    first = complex_times(scale, pair(pack_ref, RIGHT))
    keep(first_ref, first)
    hand_out(messages, interface_messages(first, ohi_ref, index), 0)
    rows = [lanes(value[c], EB) for c in range(2)]
    own, towards = nodal(rows, ohh_ref, oht_ref, pack_ref, 1.0)
    own_ref[0:4] = own
    hand_out(messages, towards, 4)
    ends = [pack_ref[at : at + EB] for at in (HEADS, TAILS)]
    hand_out(messages, interface_messages(ends, ohi_ref, index), 8)


def weight_kernel(off_ref, wo_ref):
    zero = jnp.zeros((BS, 2 * BS), BF16)
    wo_ref[0, 0:BS] = zero
    wo_ref[EB - 1, BS:] = zero
    for b in range(EB - 1):
        off = off_ref[0, 0, b]
        wo_ref[b + 1, 0:BS] = split(off)
        wo_ref[b, BS:] = split(off.T)


def stiffness(field, value, wd_ref, wo_ref, wide, out):
    wide[0:8] = jnp.zeros((8, BS), F32)
    wide[8 * (EB + 1) :] = jnp.zeros((8, BS), F32)
    for c in range(2):
        for p, piece in enumerate(pieces(field[c])):
            wide[pl.ds(8 + 2 * p + c, EB, stride=8)] = piece
    for k in (6, 7):
        wide[pl.ds(8 + k, EB, stride=8)] = jnp.zeros((EB, BS), F32)
    for b in range(EB):
        low, here, high = [wide[8 * (b + k) : 8 * (b + k) + 8] for k in range(3)]
        beside = jnp.concatenate([low, high], axis=1)
        got = jnp.dot(here.astype(BF16), wd_ref[b], preferred_element_type=F32)
        got = got + jnp.dot(beside.astype(BF16), wo_ref[b], preferred_element_type=F32)
        out[8 * b : 8 * b + 8] = got[:, :BS] + got[:, BS:]
    sums = [
        out[pl.ds(c, EB, stride=8)] + out[pl.ds(2 + c, EB, stride=8)] + out[pl.ds(4 + c, EB, stride=8)]
        for c in range(2)
    ]
    turned = complex_times(value, field)
    return sums[0] + turned[0], sums[1] + turned[1]


def local_kernel(field_ref, value_ref, wd_ref, wo_ref, out_ref, wide, out):
    keep(out_ref, stiffness(pair(field_ref), pair(value_ref), wd_ref, wo_ref, wide, out))


def smooth(arrived, ohi_ref, pack_ref, first_ref, local_ref, scale_ref, right_ref, m, second_ref):
    index = index_rows(pack_ref)
    extra = interface_sum(arrived, coef_row(pack_ref), ohi_ref, index)
    first, local, right = pair(first_ref), pair(local_ref), pair(right_ref)
    change = complex_times(pair(scale_ref), [right[c] - local[c] - extra[c] for c in range(2)])
    second = (first[0] + change[0], first[1] + change[1])
    keep(second_ref, second)
    hand_out(m, interface_messages(second, ohi_ref, index))


def smooth_first_kernel(
    a0, a1, a2, a3, own_ref, ohi_ref, pack_ref, first_ref, local_ref, scale_ref,
    m0, m1, m2, m3, second_ref, ninv_ref,
):
    arrived = collect((a0, a1, a2, a3))
    smooth(arrived, ohi_ref, pack_ref, first_ref, local_ref, scale_ref, pack_ref, (m0, m1, m2, m3), second_ref)
    sums = own_ref[0:4]
    for part in collect((a0, a1, a2, a3), 4):
        sums = sums + part
    inverse = complex_inverse((sums[0:2], sums[2:4]))
    ninv_ref[0:2] = inverse[0]
    ninv_ref[2:4] = inverse[1]
    for ref in (m0, m1):
        ref[4:8] = ninv_ref[...]


def ends_kernel(a0, a1, a2, a3, second_ref, ends_ref, oha_ref):
    for d, part in enumerate(collect((a0, a1, a2, a3), 8)):
        for k in range(2):
            row = jnp.concatenate([part[2 * k : 2 * k + 1], part[2 * k + 1 : 2 * k + 2]], axis=1)
            row = row.astype(jnp.int32)
            at = (2 * d + k) * IFC
            ends_ref[:, at : at + IFC] = row
            oha_ref[:, at : at + IFC] = lane_onehot(row)


def smooth_kernel(
    a0, a1, a2, a3, ohi_ref, pack_ref, first_ref, local_ref, scale_ref, right_ref,
    m0, m1, m2, m3, second_ref,
):
    arrived = collect((a0, a1, a2, a3))
    smooth(arrived, ohi_ref, pack_ref, first_ref, local_ref, scale_ref, right_ref, (m0, m1, m2, m3), second_ref)


def times_inverse(inverse, value):
    result = complex_times((inverse[0:2], inverse[2:4]), (value[0:2], value[2:4]))
    return jnp.concatenate(result, axis=0)


def restrict_kernel(known, a0, a1, a2, a3, ohi_ref, oht_ref, ohh_ref, pack_ref, local_ref, right_ref, beside_ref, *refs):
    far_ref, core_ref, row_ref, extra_ref = refs[:4]
    even_lat, even_lon = parities()
    if known:
        west, east = beside_ref[0], beside_ref[1]
    else:
        wide, near = a0[4:8], a1[4:8]
        west, east = jnp.where(even_lon, wide, near), jnp.where(even_lon, near, wide)
        refs[4][0] = west
        refs[4][1] = east
    index = index_rows(pack_ref)
    extra = interface_sum(collect((a0, a1, a2, a3)), coef_row(pack_ref), ohi_ref, index)
    keep(extra_ref, extra)
    local, right = pair(local_ref), pair(right_ref)
    rows = [lanes(right[c] - local[c] - extra[c], EB) for c in range(2)]
    own, towards = nodal(rows, ohh_ref, oht_ref, pack_ref, -1.0)
    far_ref[...] = jnp.where(even_lat, towards[0], towards[1])
    core_ref[...] = jnp.where(even_lat, towards[1], towards[0])
    row_ref[0] = own
    row_ref[1] = times_inverse(west, towards[2])
    row_ref[2] = times_inverse(east, towards[3])


def row_kernel(far_ref, core_ref, row_ref, ninv_ref, out_ref):
    even_lat, _ = parities()
    core = jnp.where(even_lat, core_ref[1], core_ref[0])
    mine = times_inverse(ninv_ref[...], row_ref[0] + far_ref[...] + core)
    for k, part in enumerate((mine, row_ref[1], row_ref[2])):
        out_ref[:, k] = jnp.broadcast_to(part[None], (out_ref.shape[0], 4, BS))


def column_kernel(lon, row_ref, near_ref, out_ref):
    me = lax.axis_index("lon")

    def at(step):
        return lax.rem(me + (lon + step), lon)

    for k in range(5):
        near_ref[k] = row_ref[at(k - 2), 0] + row_ref[at(k - 1), 1] + row_ref[at(k - 3), 2]
    for k in range(3):
        out_ref[k] = near_ref[k + 1]


def extend(nodes, ref):
    for d in range(5):
        for c in range(2):
            ref[EB * c + 2 * d : EB * c + 2 * d + 2] = nodes[d][2 * c : 2 * c + 2]
    return pair(ref)


def gradient(nodes, ref, onehot_head, onehot_tail, heads, tails):
    low = take(extend(nodes, ref), onehot_tail, block_mask(tails // BS, EB))
    high = take_heads(jnp.concatenate([nodes[0], nodes[0]], axis=0), onehot_head, heads // BS)
    return [high[c] - low[c] for c in range(2)]


def prolong(
    lat, chip_ref, away_ref, near_ref, ohi_ref, oht_ref, ohh_ref, pack_ref, second_ref, extra_ref,
    ends_ref, oha_ref, value_ref, wd_ref, wo_ref, direction_ref, blocks, ext, wide, out, column,
):
    me = lax.axis_index("lat")

    for k in range(2):
        column[k] = away_ref[0, 3 * k : 3 * k + 3]
        column[2 + k] = chip_ref[k]
        column[4 + k] = away_ref[1, 3 * k : 3 * k + 3]
    here = 2 + me % 2

    def node(down, right):
        if down == 0:
            return near_ref[right + 2]
        return column[here + down, right + 1]

    def around(down, right):
        steps = ((0, 0), (-1, 0), (1, 0), (0, -1), (0, 1))
        return [node(down + i, right + j) for i, j in steps]

    ext[...] = jnp.zeros((2 * EB, BS), F32)
    tails, heads = ends_rows(pack_ref)
    rise = gradient(around(0, 0), ext, ohh_ref, oht_ref, heads, tails)
    second = pair(second_ref)
    direction = [second[c] + to_blocks(rise[c], blocks) for c in range(2)]
    keep(direction_ref, direction)
    rises = []
    for d, step in enumerate(((-1, 0), (1, 0), (0, -1), (0, 1))):
        spots = [pl.ds((2 * d + k) * IFC, IFC) for k in range(2)]
        rise = gradient(
            around(*step), ext, oha_ref.at[:, spots[0]], oha_ref.at[:, spots[1]],
            ends_ref[:, spots[0]], ends_ref[:, spots[1]],
        )
        if d < 2:
            there = me + step[0]
            real = (there >= 0) & (there < lat)
            rise = [jnp.where(real, part, 0.0) for part in rise]
        rises.append(rise)
    rows = [jnp.concatenate([rise[c] for rise in rises], axis=1) * coef_row(pack_ref) for c in range(2)]
    more = put(rows, ohi_ref, block_mask(index_rows(pack_ref) // BS, EB))
    extra = pair(extra_ref)
    local = stiffness(direction, pair(value_ref), wd_ref, wo_ref, wide, out)
    return [local[c] + extra[c] + more[c] for c in range(2)]


def prolong_first_kernel(
    lat, chip_ref, away_ref, near_ref, ohi_ref, oht_ref, ohh_ref, pack_ref, second_ref, extra_ref,
    ends_ref, oha_ref, value_ref, wd_ref, wo_ref, scale_ref,
    m0, m1, m2, m3, direction_ref, image_ref, first_ref,
    *scratch,
):
    image = prolong(
        lat, chip_ref, away_ref, near_ref, ohi_ref, oht_ref, ohh_ref, pack_ref, second_ref, extra_ref,
        ends_ref, oha_ref, value_ref, wd_ref, wo_ref, direction_ref, *scratch,
    )
    keep(image_ref, image)
    first = complex_times(pair(scale_ref), image)
    keep(first_ref, first)
    hand_out((m0, m1, m2, m3), interface_messages(first, ohi_ref, index_rows(pack_ref)))


def total(x):
    return jnp.sum(jnp.sum(x, axis=0, keepdims=True), axis=1, keepdims=True)


def inner(a, b):
    return total(a[0] * b[0] + a[1] * b[1]), total(a[0] * b[1] - a[1] * b[0])


def prolong_last_kernel(
    lat, chip_ref, away_ref, near_ref, ohi_ref, oht_ref, ohh_ref, pack_ref, second_ref, extra_ref,
    ends_ref, oha_ref, value_ref, wd_ref, wo_ref, image_ref,
    direction_ref, image2_ref, sums_ref,
    *scratch,
):
    image2 = prolong(
        lat, chip_ref, away_ref, near_ref, ohi_ref, oht_ref, ohh_ref, pack_ref, second_ref, extra_ref,
        ends_ref, oha_ref, value_ref, wd_ref, wo_ref, direction_ref, *scratch,
    )
    right, image = pair(pack_ref, RIGHT), pair(image_ref)
    keep(image2_ref, image2)
    rest = (right[0] - image[0], right[1] - image[1])
    turn = (image[0] - image2[0], image[1] - image2[1])
    found = [inner(right, right)[0], inner(image, image)[0], inner(rest, rest)[0], inner(turn, turn)[0]]
    found += [*inner(image, rest), *inner(turn, rest), *inner(turn, image)]
    lane = lax.broadcasted_iota(jnp.int32, (1, BS), 1)
    row = jnp.zeros((1, BS), F32)
    for k, value in enumerate(found):
        row = jnp.where(lane == k, value, row)
    sums_ref[...] = jnp.broadcast_to(row[None], sums_ref.shape)


def finish_kernel(
    sums_ref, pack_ref, image_ref, image2_ref, direction_ref, direction2_ref,
    solution_ref, residual_ref, history_ref,
):
    row = jnp.sum(sums_ref[...], axis=0)
    lane = lax.broadcasted_iota(jnp.int32, (1, BS), 1)
    found = [jnp.sum(jnp.where(lane == k, row, 0.0), axis=1, keepdims=True) for k in range(10)]
    start, ww, rr, tt = found[:4]
    wr, tr, tw = found[4:6], found[6:8], found[8:10]
    extra = (wr[0] / ww, wr[1] / ww)
    alpha = (1.0 + extra[0], extra[1])
    fresh = rr - (wr[0] * extra[0] + wr[1] * extra[1])
    moved = complex_times(extra, tw)
    c2 = complex_times((alpha[0], -alpha[1]), (tr[0] - moved[0], tr[1] - moved[1]))
    cross = complex_times(complex_times((extra[0], -extra[1]), alpha), (tw[0], -tw[1]))
    ww2 = (alpha[0] * alpha[0] + alpha[1] * alpha[1]) * tt
    ww2 = ww2 + (extra[0] * extra[0] + extra[1] * extra[1]) * ww - 2.0 * cross[0]
    alpha2 = (c2[0] / ww2, c2[1] / ww2)
    fresh2 = fresh - (c2[0] * alpha2[0] + c2[1] * alpha2[1])
    history_ref[0] = (fresh / start)[0, 0]
    history_ref[1] = (fresh2 / start)[0, 0]
    right, image, image2 = pair(pack_ref, RIGHT), pair(image_ref), pair(image2_ref)
    direction, direction2 = pair(direction_ref), pair(direction2_ref)
    step = complex_times(alpha, direction)
    other = complex_times(alpha, direction2)
    step2 = complex_times(alpha2, (direction[0] - other[0], direction[1] - other[1]))
    away = complex_times(extra, image)
    other = complex_times(alpha, image2)
    away2 = complex_times(alpha2, (image[0] - other[0], image[1] - other[1]))
    for c in range(2):
        solution_ref[c, 0] = lanes(step[c] + step2[c], EB)
        residual_ref[c, 0] = lanes(right[c] - image[c] - away[c] - away2[c], EB)


def shape(*dims, dtype=F32):
    return jax.ShapeDtypeStruct(dims, dtype)


FIELD = shape(2 * EB, BS)
MESSAGES = [shape(4, BS)] * 4


def call(body, outs, args, name, scratch=(), space=pltpu.VMEM, out_spaces=None, limit=LIMIT, flops=0):
    specs = [pl.BlockSpec(memory_space=space)] * len(args)
    moved = sum(a.size * a.dtype.itemsize for a in args)
    return pl.pallas_call(
        body,
        out_shape=outs,
        in_specs=specs,
        out_specs=[pl.BlockSpec(memory_space=place) for place in out_spaces or [pltpu.VMEM] * len(outs)],
        scratch_shapes=scratch,
        compiler_params=pltpu.CompilerParams(vmem_limit_bytes=limit),
        cost_estimate=pl.CostEstimate(flops=flops, bytes_accessed=moved, transcendentals=0),
        name=name,
    )(*args)


def swap(pairs):
    return [(a, b) for a, b in pairs] + [(b, a) for a, b in pairs]


def lat_pairs(first):
    return [(k, k + 1) for k in range(first, lax.axis_size("lat") - 1, 2)]


def swap_far(message):
    return lax.ppermute(message, "lat", swap(lat_pairs(1)))


def on_chip(message):
    return lax.all_gather(message, "lat", axis_index_groups=lat_pairs(0))


def exchange(messages):
    lon = lax.axis_size("lon")
    return [
        lax.ppermute(messages[0], "lon", swap([(k, (k + 1) % lon) for k in range(1, lon, 2)])),
        lax.ppermute(messages[1], "lon", swap([(k, k + 1) for k in range(0, lon, 2)])),
        swap_far(messages[2]),
        lax.ppermute(messages[3], "lat", swap(lat_pairs(0))),
    ]


def everywhere(row, axis):
    return lax.all_to_all(row, axis, 0, 0)


def on_device(rhs, cond, blk_diag, blk_off, idx, cnt, coup, nodes):
    blocks = pltpu.VMEM((EB, BS), F32)
    wide = pltpu.VMEM((8 * (EB + 2), BS), F32)
    out = pltpu.VMEM((8 * EB, BS), F32)
    small = (rhs, cond, coup, cnt, idx, nodes)
    (pack,) = call(
        pack_kernel,
        [shape(PACKED, BS)],
        small,
        "pack",
        scratch=[(pltpu.SMEM if part is cnt else pltpu.VMEM)(part.shape, part.dtype) for part in small]
        + [pltpu.SemaphoreType.DMA((6,))],
        space=pltpu.HBM,
        limit=PACK_LIMIT,
    )
    onehots = [(BS, 4 * IFC), (BS, E), (BS, E)]
    *sent, value, scale, first, own, ohi, oht, ohh, inside = call(
        begin_kernel,
        [shape(12, BS)] * 4 + [FIELD] * 3 + [shape(4, BS)] + [shape(*dims, dtype=BF16) for dims in onehots]
        + [shape(EB, BS, 2 * BS, dtype=BF16)],
        (pack, blk_diag),
        "begin",
    )
    arrived = exchange(sent)
    (beside,) = call(weight_kernel, [shape(EB, 2 * BS, 2 * BS, dtype=BF16)], (blk_off,), "weights", flops=10**7)

    def local(field):
        return call(
            local_kernel, [FIELD], (field, value, inside, beside), "local", scratch=[wide, out], flops=2 * 8 * EB * 3 * BS * 2 * BS
        )[0]

    lat, lon = lax.axis_size("lat"), lax.axis_size("lon")
    scratch = [blocks, pltpu.VMEM((2 * EB, BS), F32), wide, out, pltpu.VMEM((6, 3, 4, BS), F32)]
    directions = []
    for step in range(ITERS):
        stiff = local(first)
        if step == 0:
            *sent, second, ninv = call(
                smooth_first_kernel,
                [shape(8, BS)] * 2 + MESSAGES[2:] + [FIELD, shape(4, BS)],
                (*arrived, own, ohi, pack, first, stiff, scale),
                "smooth_first",
            )
            ends, oha = call(
                ends_kernel,
                [shape(1, 8 * IFC, dtype=jnp.int32), shape(BS, 8 * IFC, dtype=BF16)],
                (*arrived, second),
                "ends",
                flops=10**7,
            )
            source = pack
        else:
            *sent, second = call(
                smooth_kernel,
                MESSAGES + [FIELD],
                (*arrived, ohi, pack, first, stiff, scale, source),
                "smooth",
            )
        arrived = exchange(sent)
        stiff = local(second)
        known = step > 0
        far, core, row, extra, *found = call(
            functools.partial(restrict_kernel, known),
            MESSAGES[:2] + [shape(3, 4, BS), FIELD] + ([] if known else [shape(2, 4, BS)]),
            (*arrived, ohi, oht, ohh, pack, stiff, source, sides if known else ninv),
            "restrict",
        )
        if not known:
            (sides,) = found
        (row,) = call(
            row_kernel, [shape(lon, 3, 4, BS)], (swap_far(far), on_chip(core), row, ninv), "row"
        )
        near, column = call(
            functools.partial(column_kernel, lon),
            [shape(5, 4, BS), shape(3, 4, BS)],
            (everywhere(row, "lon"),),
            "column",
        )
        chip = on_chip(column)
        away = on_chip(swap_far(chip.reshape(6, 4, BS)))
        args = (chip, away, near, ohi, oht, ohh, pack, second, extra, ends, oha, value, inside, beside)
        if step == 0:
            *sent, direction, image, first = call(
                functools.partial(prolong_first_kernel, lat),
                MESSAGES + [FIELD] * 3,
                args + (scale,),
                "prolong_first",
                scratch=scratch,
            )
            source = image
            arrived = exchange(sent)
        else:
            direction, image2, sums = call(
                functools.partial(prolong_last_kernel, lat),
                [FIELD, FIELD, shape(lat, 1, BS)],
                args + (image,),
                "prolong_last",
                scratch=scratch,
            )
        directions.append(direction)
    sums = jnp.sum(everywhere(sums, "lat"), axis=0, keepdims=True)
    sums = everywhere(jnp.broadcast_to(sums, (lax.axis_size("lon"), 1, BS)), "lon")
    solution, residual, history = call(
        finish_kernel,
        [shape(2, 1, 1, E), shape(2, 1, 1, E), shape(ITERS)],
        (sums, pack, image, image2, directions[0], directions[1]),
        "finish",
        out_spaces=[pltpu.VMEM, pltpu.VMEM, pltpu.SMEM],
    )
    return solution, residual, history


def solution(mesh):
    placed = (
        P(None, "lat", "lon", None),
        P("lat", "lon", None),
        P("lat", "lon", None, None, None),
        P("lat", "lon", None, None, None),
        P("lat", "lon", None, None),
        P("lat", "lon", None),
        P("lat", "lon", None, None),
        P("lat", "lon", None, None),
    )
    return jax.shard_map(
        on_device,
        mesh=mesh,
        in_specs=placed,
        out_specs=(P(None, "lat", "lon", None), P(None, "lat", "lon", None), P()),
        check_vma=False,
    )
```

```python
import functools

import jax
import jax.numpy as jnp
from jax import lax
from jax.experimental import pallas as pl
from jax.experimental.pallas import tpu as pltpu
from jax.sharding import PartitionSpec as P

ITERS = 2
EB = 16
BS = 128
E = EB * BS
ND = 256
IFC = 256
OMEGA = 0.8
F32 = jnp.float32
BF16 = jnp.bfloat16
LIMIT = 20 * 1024 * 1024
PACK_LIMIT = 60 * 1024 * 1024
RIGHT, COND, COEF, INDEX, TAILS, HEADS, PACKED = 0, 32, 48, 56, 64, 80, 96
NT = (((1,), (1,)), ((), ()))


def complex_times(a, b):
    return a[0] * b[0] - a[1] * b[1], a[0] * b[1] + a[1] * b[0]


def complex_inverse(a):
    scale = a[0] * a[0] + a[1] * a[1]
    return a[0] / scale, -a[1] / scale


def pieces(x):
    first = x.astype(BF16).astype(F32)
    rest = x - first
    second = rest.astype(BF16).astype(F32)
    return first, second, rest - second


def split(block):
    high = block.astype(BF16)
    return jnp.concatenate([high, (block - high.astype(F32)).astype(BF16)], axis=1)


def lanes(x, count):
    return jnp.concatenate([x[k : k + 1] for k in range(count)], axis=1)


def to_blocks(row, ref):
    for k in range(EB):
        ref[k : k + 1] = row[:, k * BS : (k + 1) * BS]
    return ref[...]


def block_mask(blocks, rows):
    return lax.broadcasted_iota(jnp.int32, (rows, blocks.shape[1]), 0) == blocks


def lane_onehot(index):
    spot = lax.broadcasted_iota(jnp.int32, (BS, index.shape[1]), 0)
    return jnp.where(spot == index % BS, 1.0, 0.0).astype(BF16)


def take(field, onehot, mask):
    parts = [pieces(part) for part in field]
    stack = jnp.concatenate([parts[c][p] for p in range(3) for c in range(2)], axis=0)
    got = jnp.dot(stack.astype(BF16), onehot[...], preferred_element_type=F32)
    got = got[:32] + got[32:64] + got[64:]
    return [
        jnp.sum(jnp.where(mask, got[16 * c : 16 * c + 16], 0.0), axis=0, keepdims=True)
        for c in range(2)
    ]


def put(rows, onehot, mask):
    parts = [pieces(part) for part in rows]
    stack = jnp.concatenate(
        [jnp.where(mask, parts[c][p], 0.0) for p in range(3) for c in range(2)], axis=0
    )
    got = lax.dot_general(stack.astype(BF16), onehot[...], NT, preferred_element_type=F32)
    got = got[:32] + got[32:64] + got[64:]
    return got[:16], got[16:]


def put_heads(rows, onehot, block):
    spot = lax.broadcasted_iota(jnp.int32, (8, block.shape[1]), 0)
    right = [pieces(part) for part in rows]
    match = (spot % 2 == block) & (spot < 4)
    stack = jnp.concatenate(
        [
            jnp.where(match, jnp.where(spot < 2, right[0][p], right[1][p]), 0.0)
            for p in range(3)
        ],
        axis=0,
    )
    got = lax.dot_general(stack.astype(BF16), onehot[...], NT, preferred_element_type=F32)
    return got[:8] + got[8:16] + got[16:]


def take_heads(own, onehot, block):
    stack = jnp.concatenate(pieces(own), axis=0)
    got = jnp.dot(stack.astype(BF16), onehot[...], preferred_element_type=F32)
    got = got[:8] + got[8:16] + got[16:]
    low = block == 0
    return [jnp.where(low, got[2 * c : 2 * c + 1], got[2 * c + 1 : 2 * c + 2]) for c in range(2)]


def parities():
    return lax.axis_index("lat") % 2 == 0, lax.axis_index("lon") % 2 == 0


def hand_out(refs, towards, at=0):
    even_lat, even_lon = parities()
    refs[0][at : at + 4] = jnp.where(even_lon, towards[2], towards[3])
    refs[1][at : at + 4] = jnp.where(even_lon, towards[3], towards[2])
    refs[2][at : at + 4] = jnp.where(even_lat, towards[0], towards[1])
    refs[3][at : at + 4] = jnp.where(even_lat, towards[1], towards[0])


def collect(refs, at=0):
    even_lat, even_lon = parities()
    wide, near, far, core = [ref[at : at + 4] for ref in refs]
    return (
        jnp.where(even_lat, far, core),
        jnp.where(even_lat, core, far),
        jnp.where(even_lon, wide, near),
        jnp.where(even_lon, near, wide),
    )


def index_rows(pack_ref):
    return lanes(pack_ref[INDEX : INDEX + 8], 8).astype(jnp.int32)


def ends_rows(pack_ref):
    return [lanes(pack_ref[at : at + EB], EB).astype(jnp.int32) for at in (TAILS, HEADS)]


def coef_row(pack_ref):
    return lanes(pack_ref[COEF : COEF + 8], 8)


def interface_messages(field, onehot, index):
    got = take(field, onehot, block_mask(index // BS, EB))
    return [
        jnp.concatenate(
            [
                got[c][:, d * IFC + h * BS : d * IFC + (h + 1) * BS]
                for c in range(2)
                for h in range(2)
            ],
            axis=0,
        )
        for d in range(4)
    ]


def interface_sum(arrived, coefs, onehot, index):
    rows = [
        jnp.concatenate(
            [arrived[d][2 * c + h : 2 * c + h + 1] for d in range(4) for h in range(2)], axis=1
        )
        * coefs
        for c in range(2)
    ]
    return put(rows, onehot, block_mask(index // BS, EB))


def pair(ref, at=0):
    return ref[at : at + EB], ref[at + EB : at + 2 * EB]


def keep(ref, value):
    ref[0:EB] = value[0]
    ref[EB : 2 * EB] = value[1]


def nodal(rows, onehot_head, onehot_tail, pack_ref, sign):
    tails, heads = ends_rows(pack_ref)
    own = put_heads(rows, onehot_head, heads // BS)
    ext = put(rows, onehot_tail, block_mask(tails // BS, EB))
    parts = [
        sign * jnp.concatenate([ext[0][2 * d : 2 * d + 2], ext[1][2 * d : 2 * d + 2]], axis=0)
        for d in range(5)
    ]
    return own[0:4] + parts[0], parts[1:]


def pack_kernel(
    rhs_ref, cond_ref, coup_ref, cnt_ref, idx_ref, nodes_ref, pack_ref,
    rhs_got, cond_got, coup_got, cnt_got, idx_got, nodes_got, sems,
):
    pairs = (
        (rhs_ref, rhs_got), (cond_ref, cond_got), (coup_ref, coup_got),
        (cnt_ref, cnt_got), (idx_ref, idx_got), (nodes_ref, nodes_got),
    )
    copies = [pltpu.make_async_copy(here, there, sems.at[k]) for k, (here, there) in enumerate(pairs)]
    for copy in copies:
        copy.start()
    for copy in copies:
        copy.wait()

    def rows(at, row):
        for k in range(row.shape[1] // BS):
            pack_ref[at + k : at + k + 1] = row[:, k * BS : (k + 1) * BS]

    for c in range(2):
        rows(RIGHT + EB * c, rhs_got[c, 0])
        rows((TAILS, HEADS)[c], nodes_got[0, 0, c : c + 1].astype(F32))
    rows(COND, cond_got[0])
    slot = lax.broadcasted_iota(jnp.int32, (1, IFC), 1)
    for d in range(4):
        rows(COEF + 2 * d, jnp.where(slot < cnt_got[0, 0, d], coup_got[0, 0, d : d + 1], 0.0))
        rows(INDEX + 2 * d, idx_got[0, 0, d : d + 1].astype(F32))


def begin_kernel(
    pack_ref, diag_ref,
    m0, m1, m2, m3, value_ref, scale_ref, first_ref, own_ref,
    ohi_ref, oht_ref, ohh_ref, wd_ref,
):
    messages = (m0, m1, m2, m3)
    index = index_rows(pack_ref)
    tails, heads = ends_rows(pack_ref)
    ohi_ref[...] = lane_onehot(index)
    oht_ref[...] = lane_onehot(tails)
    ohh_ref[...] = lane_onehot(heads)
    eye = lax.broadcasted_iota(jnp.int32, (BS, BS), 0) == lax.broadcasted_iota(jnp.int32, (BS, BS), 1)
    for b in range(EB):
        block = diag_ref[0, 0, b]
        value_ref[b : b + 1] = jnp.sum(jnp.where(eye, block, 0.0), axis=0, keepdims=True)
        wd_ref[b] = split(jnp.where(eye, 0.0, block))
    value_ref[EB : 2 * EB] = pack_ref[COND : COND + EB]
    value = pair(value_ref)
    inverse = complex_inverse(value)
    scale = (OMEGA * inverse[0], OMEGA * inverse[1])
    keep(scale_ref, scale)
    first = complex_times(scale, pair(pack_ref, RIGHT))
    keep(first_ref, first)
    hand_out(messages, interface_messages(first, ohi_ref, index), 0)
    rows = [lanes(value[c], EB) for c in range(2)]
    own, towards = nodal(rows, ohh_ref, oht_ref, pack_ref, 1.0)
    own_ref[0:4] = own
    hand_out(messages, towards, 4)
    ends = [pack_ref[at : at + EB] for at in (HEADS, TAILS)]
    hand_out(messages, interface_messages(ends, ohi_ref, index), 8)


def weight_kernel(off_ref, wo_ref):
    zero = jnp.zeros((BS, 2 * BS), BF16)
    wo_ref[0, 0:BS] = zero
    wo_ref[EB - 1, BS:] = zero
    for b in range(EB - 1):
        off = off_ref[0, 0, b]
        wo_ref[b + 1, 0:BS] = split(off)
        wo_ref[b, BS:] = split(off.T)


def stiffness(field, value, wd_ref, wo_ref, wide, out):
    wide[0:8] = jnp.zeros((8, BS), F32)
    wide[8 * (EB + 1) :] = jnp.zeros((8, BS), F32)
    for c in range(2):
        for p, piece in enumerate(pieces(field[c])):
            wide[pl.ds(8 + 2 * p + c, EB, stride=8)] = piece
    for k in (6, 7):
        wide[pl.ds(8 + k, EB, stride=8)] = jnp.zeros((EB, BS), F32)
    for b in range(EB):
        low, here, high = [wide[8 * (b + k) : 8 * (b + k) + 8] for k in range(3)]
        beside = jnp.concatenate([low, high], axis=1)
        got = jnp.dot(here.astype(BF16), wd_ref[b], preferred_element_type=F32)
        got = got + jnp.dot(beside.astype(BF16), wo_ref[b], preferred_element_type=F32)
        out[8 * b : 8 * b + 8] = got[:, :BS] + got[:, BS:]
    sums = [
        out[pl.ds(c, EB, stride=8)] + out[pl.ds(2 + c, EB, stride=8)] + out[pl.ds(4 + c, EB, stride=8)]
        for c in range(2)
    ]
    turned = complex_times(value, field)
    return sums[0] + turned[0], sums[1] + turned[1]


def local_kernel(field_ref, value_ref, wd_ref, wo_ref, out_ref, wide, out):
    keep(out_ref, stiffness(pair(field_ref), pair(value_ref), wd_ref, wo_ref, wide, out))


def smooth(arrived, ohi_ref, pack_ref, first_ref, local_ref, scale_ref, right_ref, m, second_ref):
    index = index_rows(pack_ref)
    extra = interface_sum(arrived, coef_row(pack_ref), ohi_ref, index)
    first, local, right = pair(first_ref), pair(local_ref), pair(right_ref)
    change = complex_times(pair(scale_ref), [right[c] - local[c] - extra[c] for c in range(2)])
    second = (first[0] + change[0], first[1] + change[1])
    keep(second_ref, second)
    hand_out(m, interface_messages(second, ohi_ref, index))


def smooth_first_kernel(
    a0, a1, a2, a3, own_ref, ohi_ref, pack_ref, first_ref, local_ref, scale_ref,
    m0, m1, m2, m3, second_ref, ninv_ref,
):
    arrived = collect((a0, a1, a2, a3))
    smooth(arrived, ohi_ref, pack_ref, first_ref, local_ref, scale_ref, pack_ref, (m0, m1, m2, m3), second_ref)
    sums = own_ref[0:4]
    for part in collect((a0, a1, a2, a3), 4):
        sums = sums + part
    inverse = complex_inverse((sums[0:2], sums[2:4]))
    ninv_ref[0:2] = inverse[0]
    ninv_ref[2:4] = inverse[1]
    for ref in (m0, m1):
        ref[4:8] = ninv_ref[...]


def ends_kernel(a0, a1, a2, a3, second_ref, ends_ref, oha_ref):
    for d, part in enumerate(collect((a0, a1, a2, a3), 8)):
        for k in range(2):
            row = jnp.concatenate([part[2 * k : 2 * k + 1], part[2 * k + 1 : 2 * k + 2]], axis=1)
            row = row.astype(jnp.int32)
            at = (2 * d + k) * IFC
            ends_ref[:, at : at + IFC] = row
            oha_ref[:, at : at + IFC] = lane_onehot(row)


def smooth_kernel(
    a0, a1, a2, a3, ohi_ref, pack_ref, first_ref, local_ref, scale_ref, right_ref,
    m0, m1, m2, m3, second_ref,
):
    arrived = collect((a0, a1, a2, a3))
    smooth(arrived, ohi_ref, pack_ref, first_ref, local_ref, scale_ref, right_ref, (m0, m1, m2, m3), second_ref)


def times_inverse(inverse, value):
    result = complex_times((inverse[0:2], inverse[2:4]), (value[0:2], value[2:4]))
    return jnp.concatenate(result, axis=0)


def restrict_kernel(known, a0, a1, a2, a3, ohi_ref, oht_ref, ohh_ref, pack_ref, local_ref, right_ref, beside_ref, *refs):
    refs = refs if known else refs[1:]
    far_ref, core_ref, row_ref, extra_ref = refs[:4]
    even_lat, even_lon = parities()
    if known:
        west, east = beside_ref[0], beside_ref[1]
    else:
        wide, near = a0[4:8], a1[4:8]
        west, east = jnp.where(even_lon, wide, near), jnp.where(even_lon, near, wide)
        refs[4][0] = west
        refs[4][1] = east
    index = index_rows(pack_ref)
    extra = interface_sum(collect((a0, a1, a2, a3)), coef_row(pack_ref), ohi_ref, index)
    keep(extra_ref, extra)
    local, right = pair(local_ref), pair(right_ref)
    rows = [lanes(right[c] - local[c] - extra[c], EB) for c in range(2)]
    own, towards = nodal(rows, ohh_ref, oht_ref, pack_ref, -1.0)
    far_ref[...] = jnp.where(even_lat, towards[0], towards[1])
    core_ref[...] = jnp.where(even_lat, towards[1], towards[0])
    row_ref[0] = own
    row_ref[1] = times_inverse(west, towards[2])
    row_ref[2] = times_inverse(east, towards[3])


def row_kernel(far_ref, core_ref, row_ref, ninv_ref, out_ref):
    even_lat, _ = parities()
    core = jnp.where(even_lat, core_ref[1], core_ref[0])
    mine = times_inverse(ninv_ref[...], row_ref[0] + far_ref[...] + core)
    for k, part in enumerate((mine, row_ref[1], row_ref[2])):
        out_ref[:, k] = jnp.broadcast_to(part[None], (out_ref.shape[0], 4, BS))


def column_kernel(lon, row_ref, near_ref, out_ref):
    me = lax.axis_index("lon")

    def at(step):
        return lax.rem(me + (lon + step), lon)

    for k in range(5):
        near_ref[k] = row_ref[at(k - 2), 0] + row_ref[at(k - 1), 1] + row_ref[at(k - 3), 2]
    for k in range(3):
        out_ref[k] = near_ref[k + 1]


def extend(nodes, ref):
    for d in range(5):
        for c in range(2):
            ref[EB * c + 2 * d : EB * c + 2 * d + 2] = nodes[d][2 * c : 2 * c + 2]
    return pair(ref)


def gradient(nodes, ref, onehot_head, onehot_tail, heads, tails):
    low = take(extend(nodes, ref), onehot_tail, block_mask(tails // BS, EB))
    high = take_heads(jnp.concatenate([nodes[0], nodes[0]], axis=0), onehot_head, heads // BS)
    return [high[c] - low[c] for c in range(2)]


def prolong(
    lat, chip_ref, away_ref, near_ref, ohi_ref, oht_ref, ohh_ref, pack_ref, second_ref, extra_ref,
    ends_ref, oha_ref, value_ref, wd_ref, wo_ref, direction_ref, blocks, ext, wide, out, column,
):
    me = lax.axis_index("lat")

    for k in range(2):
        column[k] = away_ref[0, 3 * k : 3 * k + 3]
        column[2 + k] = chip_ref[k]
        column[4 + k] = away_ref[1, 3 * k : 3 * k + 3]
    here = 2 + me % 2

    def node(down, right):
        if down == 0:
            return near_ref[right + 2]
        return column[here + down, right + 1]

    def around(down, right):
        steps = ((0, 0), (-1, 0), (1, 0), (0, -1), (0, 1))
        return [node(down + i, right + j) for i, j in steps]

    ext[...] = jnp.zeros((2 * EB, BS), F32)
    tails, heads = ends_rows(pack_ref)
    rise = gradient(around(0, 0), ext, ohh_ref, oht_ref, heads, tails)
    second = pair(second_ref)
    direction = [second[c] + to_blocks(rise[c], blocks) for c in range(2)]
    keep(direction_ref, direction)
    rises = []
    for d, step in enumerate(((-1, 0), (1, 0), (0, -1), (0, 1))):
        spots = [pl.ds((2 * d + k) * IFC, IFC) for k in range(2)]
        rise = gradient(
            around(*step), ext, oha_ref.at[:, spots[0]], oha_ref.at[:, spots[1]],
            ends_ref[:, spots[0]], ends_ref[:, spots[1]],
        )
        if d < 2:
            there = me + step[0]
            real = (there >= 0) & (there < lat)
            rise = [jnp.where(real, part, 0.0) for part in rise]
        rises.append(rise)
    rows = [jnp.concatenate([rise[c] for rise in rises], axis=1) * coef_row(pack_ref) for c in range(2)]
    more = put(rows, ohi_ref, block_mask(index_rows(pack_ref) // BS, EB))
    extra = pair(extra_ref)
    local = stiffness(direction, pair(value_ref), wd_ref, wo_ref, wide, out)
    return [local[c] + extra[c] + more[c] for c in range(2)]


def prolong_first_kernel(
    lat, chip_ref, away_ref, near_ref, ohi_ref, oht_ref, ohh_ref, pack_ref, second_ref, extra_ref,
    ends_ref, oha_ref, value_ref, wd_ref, wo_ref, scale_ref,
    m0, m1, m2, m3, direction_ref, image_ref, first_ref,
    *scratch,
):
    image = prolong(
        lat, chip_ref, away_ref, near_ref, ohi_ref, oht_ref, ohh_ref, pack_ref, second_ref, extra_ref,
        ends_ref, oha_ref, value_ref, wd_ref, wo_ref, direction_ref, *scratch,
    )
    keep(image_ref, image)
    first = complex_times(pair(scale_ref), image)
    keep(first_ref, first)
    hand_out((m0, m1, m2, m3), interface_messages(first, ohi_ref, index_rows(pack_ref)))


def total(x):
    return jnp.sum(jnp.sum(x, axis=0, keepdims=True), axis=1, keepdims=True)


def inner(a, b):
    return total(a[0] * b[0] + a[1] * b[1]), total(a[0] * b[1] - a[1] * b[0])


def prolong_last_kernel(
    lat, chip_ref, away_ref, near_ref, ohi_ref, oht_ref, ohh_ref, pack_ref, second_ref, extra_ref,
    ends_ref, oha_ref, value_ref, wd_ref, wo_ref, image_ref,
    direction_ref, image2_ref, sums_ref,
    *scratch,
):
    image2 = prolong(
        lat, chip_ref, away_ref, near_ref, ohi_ref, oht_ref, ohh_ref, pack_ref, second_ref, extra_ref,
        ends_ref, oha_ref, value_ref, wd_ref, wo_ref, direction_ref, *scratch,
    )
    right, image = pair(pack_ref, RIGHT), pair(image_ref)
    keep(image2_ref, image2)
    rest = (right[0] - image[0], right[1] - image[1])
    turn = (image[0] - image2[0], image[1] - image2[1])
    found = [inner(right, right)[0], inner(image, image)[0], inner(rest, rest)[0], inner(turn, turn)[0]]
    found += [*inner(image, rest), *inner(turn, rest), *inner(turn, image)]
    lane = lax.broadcasted_iota(jnp.int32, (1, BS), 1)
    row = jnp.zeros((1, BS), F32)
    for k, value in enumerate(found):
        row = jnp.where(lane == k, value, row)
    sums_ref[...] = jnp.broadcast_to(row[None], sums_ref.shape)


def finish_kernel(
    sums_ref, pack_ref, image_ref, image2_ref, direction_ref, direction2_ref,
    solution_ref, residual_ref, history_ref,
):
    row = jnp.sum(sums_ref[...], axis=0)
    lane = lax.broadcasted_iota(jnp.int32, (1, BS), 1)
    found = [jnp.sum(jnp.where(lane == k, row, 0.0), axis=1, keepdims=True) for k in range(10)]
    start, ww, rr, tt = found[:4]
    wr, tr, tw = found[4:6], found[6:8], found[8:10]
    extra = (wr[0] / ww, wr[1] / ww)
    alpha = (1.0 + extra[0], extra[1])
    fresh = rr - (wr[0] * extra[0] + wr[1] * extra[1])
    moved = complex_times(extra, tw)
    c2 = complex_times((alpha[0], -alpha[1]), (tr[0] - moved[0], tr[1] - moved[1]))
    cross = complex_times(complex_times((extra[0], -extra[1]), alpha), (tw[0], -tw[1]))
    ww2 = (alpha[0] * alpha[0] + alpha[1] * alpha[1]) * tt
    ww2 = ww2 + (extra[0] * extra[0] + extra[1] * extra[1]) * ww - 2.0 * cross[0]
    alpha2 = (c2[0] / ww2, c2[1] / ww2)
    fresh2 = fresh - (c2[0] * alpha2[0] + c2[1] * alpha2[1])
    history_ref[0] = (fresh / start)[0, 0]
    history_ref[1] = (fresh2 / start)[0, 0]
    right, image, image2 = pair(pack_ref, RIGHT), pair(image_ref), pair(image2_ref)
    direction, direction2 = pair(direction_ref), pair(direction2_ref)
    step = complex_times(alpha, direction)
    other = complex_times(alpha, direction2)
    step2 = complex_times(alpha2, (direction[0] - other[0], direction[1] - other[1]))
    away = complex_times(extra, image)
    other = complex_times(alpha, image2)
    away2 = complex_times(alpha2, (image[0] - other[0], image[1] - other[1]))
    for c in range(2):
        solution_ref[c, 0] = lanes(step[c] + step2[c], EB)
        residual_ref[c, 0] = lanes(right[c] - image[c] - away[c] - away2[c], EB)


def shape(*dims, dtype=F32):
    return jax.ShapeDtypeStruct(dims, dtype)


FIELD = shape(2 * EB, BS)
MESSAGES = [shape(4, BS)] * 4


def call(body, outs, args, name, scratch=(), space=pltpu.VMEM, out_spaces=None, limit=LIMIT, flops=0):
    specs = [pl.BlockSpec(memory_space=space)] * len(args)
    moved = sum(a.size * a.dtype.itemsize for a in args)
    return pl.pallas_call(
        body,
        out_shape=outs,
        in_specs=specs,
        out_specs=[pl.BlockSpec(memory_space=place) for place in out_spaces or [pltpu.VMEM] * len(outs)],
        scratch_shapes=scratch,
        compiler_params=pltpu.CompilerParams(vmem_limit_bytes=limit),
        cost_estimate=pl.CostEstimate(flops=flops, bytes_accessed=moved, transcendentals=0),
        name=name,
    )(*args)


def swap(pairs):
    return [(a, b) for a, b in pairs] + [(b, a) for a, b in pairs]


def lat_pairs(first):
    return [(k, k + 1) for k in range(first, lax.axis_size("lat") - 1, 2)]


def swap_far(message):
    return lax.ppermute(message, "lat", swap(lat_pairs(1)))


def on_chip(message):
    return lax.all_gather(message, "lat", axis_index_groups=lat_pairs(0))


def exchange(messages):
    lon = lax.axis_size("lon")
    return [
        lax.ppermute(messages[0], "lon", swap([(k, (k + 1) % lon) for k in range(1, lon, 2)])),
        lax.ppermute(messages[1], "lon", swap([(k, k + 1) for k in range(0, lon, 2)])),
        swap_far(messages[2]),
        lax.ppermute(messages[3], "lat", swap(lat_pairs(0))),
    ]


def everywhere(row, axis):
    return lax.all_to_all(row, axis, 0, 0)


def on_device(rhs, cond, blk_diag, blk_off, idx, cnt, coup, nodes):
    blocks = pltpu.VMEM((EB, BS), F32)
    wide = pltpu.VMEM((8 * (EB + 2), BS), F32)
    out = pltpu.VMEM((8 * EB, BS), F32)
    small = (rhs, cond, coup, cnt, idx, nodes)
    (pack,) = call(
        pack_kernel,
        [shape(PACKED, BS)],
        small,
        "pack",
        scratch=[(pltpu.SMEM if part is cnt else pltpu.VMEM)(part.shape, part.dtype) for part in small]
        + [pltpu.SemaphoreType.DMA((6,))],
        space=pltpu.HBM,
        limit=PACK_LIMIT,
    )
    onehots = [(BS, 4 * IFC), (BS, E), (BS, E)]
    *sent, value, scale, first, own, ohi, oht, ohh, inside = call(
        begin_kernel,
        [shape(12, BS)] * 4 + [FIELD] * 3 + [shape(4, BS)] + [shape(*dims, dtype=BF16) for dims in onehots]
        + [shape(EB, BS, 2 * BS, dtype=BF16)],
        (pack, blk_diag),
        "begin",
    )
    arrived = exchange(sent)
    (beside,) = call(weight_kernel, [shape(EB, 2 * BS, 2 * BS, dtype=BF16)], (blk_off,), "weights", flops=10**7)

    def local(field):
        return call(
            local_kernel, [FIELD], (field, value, inside, beside), "local", scratch=[wide, out], flops=2 * 8 * EB * 3 * BS * 2 * BS
        )[0]

    lat, lon = lax.axis_size("lat"), lax.axis_size("lon")
    scratch = [blocks, pltpu.VMEM((2 * EB, BS), F32), wide, out, pltpu.VMEM((6, 3, 4, BS), F32)]
    directions = []
    for step in range(ITERS):
        stiff = local(first)
        if step == 0:
            *sent, second, ninv = call(
                smooth_first_kernel,
                [shape(8, BS)] * 2 + MESSAGES[2:] + [FIELD, shape(4, BS)],
                (*arrived, own, ohi, pack, first, stiff, scale),
                "smooth_first",
            )
            ends, oha = call(
                ends_kernel,
                [shape(1, 8 * IFC, dtype=jnp.int32), shape(BS, 8 * IFC, dtype=BF16)],
                (*arrived, second),
                "ends",
                flops=10**7,
            )
            source = pack
        else:
            *sent, second = call(
                smooth_kernel,
                MESSAGES + [FIELD],
                (*arrived, ohi, pack, first, stiff, scale, source),
                "smooth",
            )
        arrived = exchange(sent)
        stiff = local(second)
        known = step > 0
        far, core, row, extra, *found = call(
            functools.partial(restrict_kernel, known),
            MESSAGES[:2] + [shape(3, 4, BS), FIELD] + ([] if known else [shape(2, 4, BS)]),
            (*arrived, ohi, oht, ohh, pack, stiff, source) + ((sides,) if known else (ninv, ends)),
            "restrict",
        )
        if not known:
            (sides,) = found
        (row,) = call(
            row_kernel, [shape(lon, 3, 4, BS)], (swap_far(far), on_chip(core), row, ninv), "row"
        )
        near, column = call(
            functools.partial(column_kernel, lon),
            [shape(5, 4, BS), shape(3, 4, BS)],
            (everywhere(row, "lon"),),
            "column",
        )
        chip = on_chip(column)
        away = on_chip(swap_far(chip.reshape(6, 4, BS)))
        args = (chip, away, near, ohi, oht, ohh, pack, second, extra, ends, oha, value, inside, beside)
        if step == 0:
            *sent, direction, image, first = call(
                functools.partial(prolong_first_kernel, lat),
                MESSAGES + [FIELD] * 3,
                args + (scale,),
                "prolong_first",
                scratch=scratch,
            )
            source = image
            arrived = exchange(sent)
        else:
            direction, image2, sums = call(
                functools.partial(prolong_last_kernel, lat),
                [FIELD, FIELD, shape(lat, 1, BS)],
                args + (image,),
                "prolong_last",
                scratch=scratch,
            )
        directions.append(direction)
    sums = jnp.sum(everywhere(sums, "lat"), axis=0, keepdims=True)
    sums = everywhere(jnp.broadcast_to(sums, (lax.axis_size("lon"), 1, BS)), "lon")
    solution, residual, history = call(
        finish_kernel,
        [shape(2, 1, 1, E), shape(2, 1, 1, E), shape(ITERS)],
        (sums, pack, image, image2, directions[0], directions[1]),
        "finish",
        out_spaces=[pltpu.VMEM, pltpu.VMEM, pltpu.SMEM],
    )
    return solution, residual, history


def solution(mesh):
    placed = (
        P(None, "lat", "lon", None),
        P("lat", "lon", None),
        P("lat", "lon", None, None, None),
        P("lat", "lon", None, None, None),
        P("lat", "lon", None, None),
        P("lat", "lon", None),
        P("lat", "lon", None, None),
        P("lat", "lon", None, None),
    )
    return jax.shard_map(
        on_device,
        mesh=mesh,
        in_specs=placed,
        out_specs=(P(None, "lat", "lon", None), P(None, "lat", "lon", None), P()),
        check_vma=False,
    )
```
